128 devices in a mesh: brow: 8 (over x_lo, y), bcol: 16 (over z, x_hi, core).
Axes of the slice: x: 4 (x_hi: 2, x_lo: 2; x = x_hi * 2 + x_lo), y: 4, z: 4, core: 2. Of those that a mesh axis runs over, the one named last changes fastest.
Arguments:
- uvel: float32 [8, 2048, 8192], P(None, 'brow', 'bcol'), may hold values from -6 to 6
- vvel: float32 [8, 2048, 8192], P(None, 'brow', 'bcol'), may hold values from -6 to 6
- wind_stress: float32 [2, 2048, 8192], P(None, 'brow', 'bcol'), may hold values from -6 to 6
- ocean_mask: int32 [2048, 8192], P('brow', 'bcol'), may hold values from 0 to 1
- depth_level: int32 [2048, 8192], P('brow', 'bcol'), may hold values from 1 to 8
- baro_owner: int32 [32, 64], replicated, may hold values from -1 to 1535, as said below
- eta_guess: float32 [1536, 64, 128], P(('brow', 'bcol')), may hold values from -6 to 6
Outputs:
- uvel_next: float32 [8, 2048, 8192], P(None, 'brow', 'bcol')
- vvel_next: float32 [8, 2048, 8192], P(None, 'brow', 'bcol')
- surface_height: float32 [1536, 64, 128], P(('brow', 'bcol'))
The draws below stay inside these ranges and needn't reach their ends.
Inputs may be any that keep to these rules, and one draw needn't show every extreme that they name: `baro_owner`: entry p, q is the slot of block p, q in the barotropic distribution, or -1; every block with an ocean cell has a slot, and a slot holds at most one block. Slots are numbered device by device in the order brow then bcol, 12 a device; a device uses its lowest slots first and some device uses all 12. A block's slot lies on a device with the brow index of the block's tile (block row p // 4); of the blocks of one tile at most 1 lie on one device, and some tile has exactly 1 on one device.
All inputs are finite; a program needn't handle non-finite values.
Results may differ from the reference program's by a relative error of at most 0.0002.
Values sent between devices are 32-bit elements; how exact they have to be, the bound alone decides.
A program may use at most 128 MiB of HBM per device.

```python
import jax
import jax.numpy as jnp
from jax import lax

LEVELS = 8
BLOCK_X = 64
BLOCK_Y = 128
TILE_BX = 4
TILE_BY = 4
SLOTS_DEV = 12
ITERS = 4
NX = 2048
NY = 8192
GRID_BX = 32
GRID_BY = 64
SLOTS = 1536
N_BROW = 8
N_BCOL = 16
DEVICES = 128


def block_layout(key):
    key = jax.random.fold_in(key, 11)
    tile_blocks = TILE_BX * TILE_BY
    subkeys = jax.random.split(key, 4)
    offsets = jax.random.permutation(subkeys[0], tile_blocks) % N_BCOL
    counts = jax.random.randint(subkeys[1], (N_BROW, N_BCOL), SLOTS_DEV - 4, SLOTS_DEV + 1)
    chosen = jax.random.randint(subkeys[2], (), 0, DEVICES)
    device_ids = jnp.arange(DEVICES).reshape(N_BROW, N_BCOL)
    counts = jnp.where(device_ids == chosen, SLOTS_DEV, counts)
    scores = jax.random.randint(subkeys[3], (N_BROW, N_BCOL, tile_blocks), 0, 1 << 20) * tile_blocks + jnp.arange(tile_blocks)
    ranking = jnp.argsort(jnp.argsort(scores, axis=-1), axis=-1)
    wet_block = ranking < counts[:, :, None]
    slot_index = jnp.cumsum(wet_block.astype(jnp.int32), axis=-1) - 1
    global_slot = jnp.where(wet_block, device_ids[:, :, None] * SLOTS_DEV + slot_index, -1)
    source_cols = (jnp.arange(N_BCOL)[:, None] - offsets[None, :]) % N_BCOL
    shape_all = (N_BROW, N_BCOL, tile_blocks)
    block_rows = jnp.broadcast_to(jnp.arange(N_BROW)[:, None, None] * TILE_BX + (jnp.arange(tile_blocks) // TILE_BY)[None, None, :], shape_all)
    block_cols = jnp.broadcast_to(source_cols[None, :, :] * TILE_BY + (jnp.arange(tile_blocks) % TILE_BY)[None, None, :], shape_all)
    owner_map = jnp.full((GRID_BX, GRID_BY), -1, jnp.int32)
    return owner_map.at[block_rows, block_cols].set(global_slot.astype(jnp.int32))


def draw_ocean_mask(key, part):
    owner_map = block_layout(key)
    key = jax.random.fold_in(key, 3)
    coast = jax.random.randint(key, (NX, NY), 0, 20) < 17
    block_wet = jnp.repeat(jnp.repeat(owner_map >= 0, BLOCK_X, axis=0), BLOCK_Y, axis=1)
    return (block_wet & coast).astype(jnp.int32)


def draw_baro_owner(key, part):
    owner_map = block_layout(key)
    return owner_map


def plant(result, rng, low, top_value):
    longest = result.shape.index(max(result.shape))
    spots = []
    for shift in (0, 1):
        where = [jax.random.randint(jax.random.fold_in(rng, axis), (), 0, length) for axis, length in enumerate(result.shape)]
        where[longest] = (where[longest] + shift) % result.shape[longest]
        spots.append(tuple(where))
    return result.at[spots[0]].set(low).at[spots[1]].set(top_value)


def block_levels(own_key, dims, shards, smallest, top_value):
    gain, own = 1.0, jax.random.fold_in(own_key, 6)
    for dim, blocks in shards:
        steps = jnp.exp(jax.random.uniform(jax.random.fold_in(own, dim), (blocks,), jnp.float32, smallest / len(shards), top_value / len(shards)))
        gain = gain * jnp.repeat(steps, dims[dim] // blocks).reshape([-1 if axis == dim else 1 for axis in range(len(dims))])
    return gain


def bell_draw(own_key, dims, width, limit, shards=(), dtype=jnp.bfloat16):
    result = width * jax.random.normal(own_key, dims, jnp.float32)
    if shards:
        result = result * block_levels(own_key, dims, shards, -0.22, 0.18)
    return jnp.clip(result, -limit, limit).astype(dtype)


def setup_inputs(seed: int = 0) -> dict:
    arg_keys = jax.random.split(jax.random.key(seed), 8)
    return {
        "uvel": bell_draw(arg_keys[0], (LEVELS, NX, NY), 1.0, 6.0, ((1, 8), (2, 16)), jnp.float32),
        "vvel": bell_draw(arg_keys[1], (LEVELS, NX, NY), 1.0, 6.0, ((1, 8), (2, 16)), jnp.float32),
        "wind_stress": bell_draw(arg_keys[2], (2, NX, NY), 1.0, 6.0, ((1, 8), (2, 16)), jnp.float32),
        "ocean_mask": draw_ocean_mask(jax.random.fold_in(arg_keys[7], 71), 0),
        "depth_level": plant(jax.random.randint(arg_keys[4], (NX, NY), 1, LEVELS + 1), jax.random.fold_in(arg_keys[4], 1), 1, LEVELS).astype(jnp.int32),
        "baro_owner": draw_baro_owner(jax.random.fold_in(arg_keys[7], 71), 0),
        "eta_guess": bell_draw(arg_keys[6], (SLOTS, BLOCK_X, BLOCK_Y), 1.0, 6.0, ((0, 128),), jnp.float32),
    }


VISCOSITY = 0.2
CORIOLIS = 0.5
SURFACE_TERM = 0.25
LOWER_BOUND = 0.05
UPPER_BOUND = 2.0


def neighbours(padded):
    return [padded[..., :-2, 1:-1], padded[..., 2:, 1:-1], padded[..., 1:-1, :-2], padded[..., 1:-1, 2:],
            padded[..., :-2, :-2], padded[..., :-2, 2:], padded[..., 2:, :-2], padded[..., 2:, 2:]]


def operator_weights(padded_depth):
    centre = padded_depth[..., 1:-1, 1:-1]
    beside_all = neighbours(padded_depth)
    weights = [jnp.minimum(centre, other) for other in beside_all[:4]]
    weights = weights + [0.5 * jnp.minimum(centre, other) for other in beside_all[4:]]
    diagonal = SURFACE_TERM + weights[0]
    for weight_term in weights[1:]:
        diagonal = diagonal + weight_term
    return weights, diagonal


def apply_operator(padded, weights, diagonal):
    applied = diagonal * padded[..., 1:-1, 1:-1]
    for weight_term, neighbour in zip(weights, neighbours(padded)):
        applied = applied - weight_term * neighbour
    return applied


def chebyshev(initial, forcing, weights, diagonal, pad_field):
    alpha_term = 2.0 / (UPPER_BOUND - LOWER_BOUND)
    gamma_term = (UPPER_BOUND + LOWER_BOUND) / 2.0
    omega_term = 2.0 / gamma_term
    surface = initial
    increment = None
    for sweep_index in range(ITERS):
        residual = forcing - apply_operator(pad_field(surface), weights, diagonal)
        if sweep_index == 0:
            increment = residual / (gamma_term * diagonal)
        else:
            omega_term = 1.0 / (gamma_term - omega_term / (4.0 * alpha_term * alpha_term))
            increment = omega_term * residual / diagonal + (gamma_term * omega_term - 1.0) * increment
        surface = surface + increment
    return surface


def momentum(padded, wet_mask, coriolis, top_level, wind_stress):
    centre = padded[:, :, 1:-1, 1:-1]
    spread = padded[:, :, :-2, 1:-1] + padded[:, :, 2:, 1:-1] + padded[:, :, 1:-1, :-2] + padded[:, :, 1:-1, 2:] - 4.0 * centre
    ustar = wet_mask * (centre[0] + VISCOSITY * spread[0] + coriolis * centre[1] + top_level * wind_stress[0])
    vstar = wet_mask * (centre[1] + VISCOSITY * spread[1] - coriolis * centre[0] + top_level * wind_stress[1])
    return ustar, vstar


def divergence(transport_pad):
    return 0.5 * (transport_pad[0, 2:, 1:-1] - transport_pad[0, :-2, 1:-1] + transport_pad[1, 1:-1, 2:] - transport_pad[1, 1:-1, :-2])


def gradient_of(padded):
    return jnp.stack([0.5 * (padded[..., 2:, 1:-1] - padded[..., :-2, 1:-1]),
                      0.5 * (padded[..., 1:-1, 2:] - padded[..., 1:-1, :-2])], axis=-3)


def pad_zero(surface):
    return jnp.pad(surface, 1)


def reference(uvel, vvel, wind_stress, ocean_mask, depth_level, baro_owner, eta_guess):
    levels = lax.broadcasted_iota(jnp.int32, (LEVELS, 1, 1), 0)
    ocean_cells = ocean_mask.astype(jnp.float32)
    below = (levels < depth_level[None]).astype(jnp.float32)
    wet_mask = ocean_cells[None] * below
    thickness = (1.0 + levels.astype(jnp.float32)) / LEVELS
    top_level = (levels == 0).astype(jnp.float32)
    row_ids = lax.broadcasted_iota(jnp.int32, (NX, 1), 0).astype(jnp.float32)
    coriolis = CORIOLIS * ((2.0 * row_ids + 1.0) / NX - 1.0)
    velocities = jnp.stack([wet_mask * uvel, wet_mask * vvel])
    padded = jnp.pad(velocities, ((0, 0), (0, 0), (1, 1), (1, 1)))
    ustar, vstar = momentum(padded, wet_mask, coriolis, top_level, wind_stress)
    transport = jnp.stack([jnp.sum(thickness * ustar, axis=0), jnp.sum(thickness * vstar, axis=0)])
    column_depth = ocean_cells * jnp.sum(thickness * below, axis=0)
    transport_pad = jnp.pad(transport, ((0, 0), (1, 1), (1, 1)))
    forcing = -ocean_cells * divergence(transport_pad)
    present = baro_owner >= 0
    guess_blocks = jnp.where(present[:, :, None, None], eta_guess[jnp.maximum(baro_owner, 0)], 0.0)
    guess_grid = guess_blocks.transpose(0, 2, 1, 3).reshape(NX, NY)
    weights, diagonal = operator_weights(jnp.pad(column_depth, 1))
    height_grid = chebyshev(ocean_cells * guess_grid, forcing, weights, diagonal, pad_zero)
    gradient = gradient_of(jnp.pad(height_grid, 1))
    uvel_next = wet_mask * (ustar - gradient[0])
    vvel_next = wet_mask * (vstar - gradient[1])
    height_blocks = height_grid.reshape(GRID_BX, BLOCK_X, GRID_BY, BLOCK_Y).transpose(0, 2, 1, 3).reshape(-1, BLOCK_X, BLOCK_Y)
    target = jnp.where(present, baro_owner, SLOTS).reshape(-1)
    slot_table = jnp.zeros((SLOTS + 1, BLOCK_X, BLOCK_Y), jnp.float32).at[target].set(height_blocks)
    return uvel_next, vvel_next, slot_table[:SLOTS]
```

```python
import functools

import jax
import jax.numpy as jnp
from jax import lax
from jax.experimental import pallas as pl
from jax.experimental.pallas import tpu as pltpu
from jax.sharding import PartitionSpec as P

ITERS = 4
VISCOSITY = 0.2
CORIOLIS = 0.5
SURFACE_TERM = 0.25
LOWER_BOUND = 0.05
UPPER_BOUND = 2.0

LANES = 128
CHUNK = 8
PAD = 16
EAST_ROW = 64
MESH = pl.DeviceIdType.MESH
DIRECTIONS = ((-1, 0), (1, 0), (0, -1), (0, 1), (-1, -1), (-1, 1), (1, -1), (1, 1))


def chebyshev_factors():
    alpha = 2.0 / (UPPER_BOUND - LOWER_BOUND)
    gamma = (UPPER_BOUND + LOWER_BOUND) / 2.0
    omega = 2.0 / gamma
    factors = [(1.0 / gamma, 0.0)]
    for _ in range(ITERS - 1):
        omega = 1.0 / (gamma - omega / (4.0 * alpha * alpha))
        factors.append((omega, gamma * omega - 1.0))
    return factors


def lane_ids():
    return lax.broadcasted_iota(jnp.int32, (CHUNK, LANES), 1)


def from_west(tiles, lanes):
    rolled = [pltpu.roll(tile, 1, 1) for tile in tiles]
    return [jnp.where(lanes == 0, rolled[t - 1], rolled[t]) for t in range(len(tiles))]


def from_east(tiles, lanes):
    rolled = [pltpu.roll(tile, LANES - 1, 1) for tile in tiles]
    count = len(tiles)
    return [jnp.where(lanes == LANES - 1, rolled[(t + 1) % count], rolled[t]) for t in range(count)]


def rows_at(start):
    return pl.ds(pl.multiple_of(start, CHUNK), CHUNK)


def kernel(
    sizes,
    owner_ref, u_hbm, v_hbm, wind_hbm, mask_hbm, level_hbm, eta_hbm,
    u_out, v_out, height_out,
    vel, star, wind, mask_v, level_v, eta_v, wet_levels,
    depth_e, trans_e, xa, xb, forcing_e, step_e, inv_c, weights,
    eta_send, eta_recv, height_send, height_recv, height_v,
    row_send, row_recv, col_send, col_recv, col_back,
    d_pack, d_halo, d_corner, t_pack, t_halo, t_corner, x_pack, x_halo, x_corner,
    height_b,
    load_sem, vel_sem, out_sem,
    r1_sem, d_sem, t_sem, x_sem, eta_sem, height_sem,
):
    n_brow, n_bcol, level_count, rows, tiles, block_x, slots = sizes
    blocks_x = rows // block_x
    blocks = blocks_x * tiles
    chunks = rows // CHUNK
    ext = tiles + 1
    first, last = PAD, PAD + rows
    r = lax.axis_index("brow")
    c = lax.axis_index("bcol")
    lanes = lane_ids()

    def device(dr, dc):
        return (lax.rem(r + dr + n_brow, n_brow), lax.rem(c + dc + n_bcol, n_bcol))

    loads = []

    def load(src, dst):
        copy = pltpu.make_async_copy(src, dst, load_sem.at[len(loads)])
        copy.start()
        loads.append(copy)
        return copy

    def columns(t):
        return slice(t * LANES, (t + 1) * LANES)

    load_eta = load(eta_hbm, eta_v)
    load_masks = []
    for t in range(tiles):
        load_masks.append(load(mask_hbm.at[:, columns(t)], mask_v.at[t]))
        load_masks.append(load(level_hbm.at[:, columns(t)], level_v.at[t]))
    groups = 2
    per_group = level_count // groups
    vel_loads = []
    for g in range(groups):
        these = []
        for t in range(tiles):
            for f, source in enumerate((u_hbm, v_hbm)):
                copy = pltpu.make_async_copy(
                    source.at[g * per_group : (g + 1) * per_group, :, columns(t)],
                    vel.at[g * per_group : (g + 1) * per_group, f, t, CHUNK : CHUNK + rows, :],
                    vel_sem.at[g, t, f],
                )
                copy.start()
                these.append(copy)
        vel_loads.append(these)
    load_wind = [load(wind_hbm.at[:, :, columns(t)], wind.at[:, t]) for t in range(tiles)]

    barrier = pltpu.get_barrier_semaphore()
    partners = [(0, s) for s in range(1, n_bcol)]
    partners += [(dr, dc) for dr, dc in DIRECTIONS if dr != 0]
    for dr, dc in partners:
        pl.semaphore_signal(barrier, inc=1, device_id=device(dr, dc), device_id_type=MESH)

    zero = jnp.zeros((CHUNK, LANES), jnp.float32)
    for t in range(ext):
        for ref in (depth_e.at[0], trans_e.at[0], trans_e.at[1], xa.at[0], xb):
            ref[t, 0:CHUNK, :] = zero
            ref[t, last + CHUNK : last + 2 * CHUNK, :] = zero

    device_first = (r * n_bcol + c) * slots
    none = jnp.int32(-1)
    slot_of = []
    for s in range(n_bcol):
        q = lax.rem(c + s, n_bcol)
        found = none
        for b in range(blocks):
            local = owner_ref[r * blocks_x + b // tiles, q * tiles + b % tiles] - device_first
            found = jnp.where((local >= 0) & (local < slots), local, found)
        slot_of.append(found)
    owners = [owner_ref[r * blocks_x + b // tiles, c * tiles + b % tiles] for b in range(blocks)]
    block_for, shift_of = [], [jnp.int32(0)] * blocks
    for s in range(n_bcol):
        holder_first = (r * n_bcol + lax.rem(c + s, n_bcol)) * slots
        found = jnp.int32(0)
        for b in range(blocks):
            here = (owners[b] >= holder_first) & (owners[b] < holder_first + slots)
            found = jnp.where(here, b, found)
            shift_of[b] = jnp.where(here, (n_bcol - s) % n_bcol, shift_of[b])
        block_for.append(found)
    source_of = []
    for slot in range(slots):
        found = none
        for s in range(n_bcol):
            found = jnp.where(slot_of[s] == slot, (n_bcol - s) % n_bcol, found)
        source_of.append(found)

    for copy in load_masks:
        copy.wait()

    def depth_body(i, carry):
        at = rows_at(i * CHUNK)
        to = rows_at(i * CHUNK + PAD)
        for t in range(tiles):
            n = mask_v[t, at, :] * level_v[t, at, :]
            wet_levels[t, at, :] = n
            nf = n.astype(jnp.float32)
            depth_e[0, t, to, :] = nf * (nf + 1.0) * (1.0 / (2 * level_count))
        return carry

    lax.fori_loop(0, chunks, depth_body, 0)

    def pack(field_ref, count, packed_ref, back_ref):
        def pack_body(i, carry):
            at = rows_at(i * CHUNK + PAD)
            value = jnp.zeros((CHUNK, LANES), jnp.float32)
            for f in range(count):
                low = EAST_ROW + CHUNK * f
                west = field_ref[f, 0, at, :]
                east = pltpu.roll(field_ref[f, tiles - 1, at, :], (low + CHUNK) % LANES, 1)
                if f > 0:
                    west = pltpu.roll(west, CHUNK * f, 1)
                value = jnp.where((lanes >= CHUNK * f) & (lanes < CHUNK * (f + 1)), west, value)
                value = jnp.where((lanes >= low) & (lanes < low + CHUNK), east, value)
            back_ref[rows_at(i * CHUNK), :] = value
            return carry

        lax.fori_loop(0, chunks, pack_body, 0)
        packed_ref[...] = jnp.transpose(back_ref[...])

    def exchange(field_ref, count, packed_ref, halo_ref, corner_ref, sems):
        height = CHUNK * count
        top, bottom = pl.ds(first, CHUNK), pl.ds(last - CHUNK, CHUNK)
        pairs = (
            (field_ref.at[:, 0:tiles, top, :], field_ref.at[:, 0:tiles, pl.ds(last, CHUNK), :]),
            (field_ref.at[:, 0:tiles, bottom, :], field_ref.at[:, 0:tiles, pl.ds(first - CHUNK, CHUNK), :]),
            (packed_ref.at[0:height, :], halo_ref.at[0:height, :]),
            (packed_ref.at[EAST_ROW : EAST_ROW + height, :], halo_ref.at[EAST_ROW : EAST_ROW + height, :]),
            (field_ref.at[:, 0, top, :], corner_ref.at[0]),
            (field_ref.at[:, tiles - 1, top, :], corner_ref.at[1]),
            (field_ref.at[:, 0, bottom, :], corner_ref.at[2]),
            (field_ref.at[:, tiles - 1, bottom, :], corner_ref.at[3]),
        )
        copies = []
        for d in (2, 3, 0, 1, 4, 5, 6, 7):
            src, dst = pairs[d]
            copy = pltpu.make_async_remote_copy(
                src_ref=src, dst_ref=dst, send_sem=sems.at[0, d], recv_sem=sems.at[1, d],
                device_id=device(*DIRECTIONS[d]), device_id_type=MESH,
            )
            copy.start()
            copies.append(copy)
        return copies

    def arrived(copies, field_ref, count, halo_ref, corner_ref, back_ref):
        for copy in copies:
            copy.wait_recv()
        has_n, has_s, has_w, has_e = r > 0, r < n_brow - 1, c > 0, c < n_bcol - 1
        height = CHUNK * count
        spare = jnp.zeros((EAST_ROW - height, rows), jnp.float32)
        halo = jnp.concatenate(
            [halo_ref[0:height, :], spare, halo_ref[EAST_ROW : EAST_ROW + height, :], spare], axis=0
        )
        back_ref[...] = jnp.transpose(halo)
        right = (lanes < CHUNK) & has_e
        left = (lanes >= LANES - CHUNK) & has_w

        def sides(east, west):
            return jnp.where(right, east, jnp.where(left, west, 0.0))

        def side_body(i, carry):
            value = back_ref[rows_at(i * CHUNK), :]
            for f in range(count):
                east = value if f == 0 else pltpu.roll(value, LANES - CHUNK * f, 1)
                west = pltpu.roll(value, (2 * LANES - CHUNK - EAST_ROW - CHUNK * f) % LANES, 1)
                field_ref[f, tiles, rows_at(i * CHUNK + PAD), :] = sides(east, west)
            return carry

        lax.fori_loop(0, chunks, side_body, 0)
        north, south = pl.ds(first - CHUNK, CHUNK), pl.ds(last, CHUNK)
        for f in range(count):
            for t in range(tiles):
                field_ref[f, t, north, :] = jnp.where(has_n, field_ref[f, t, north, :], 0.0)
                field_ref[f, t, south, :] = jnp.where(has_s, field_ref[f, t, south, :], 0.0)
            field_ref[f, tiles, south, :] = jnp.where(has_s, sides(corner_ref[0, f], corner_ref[1, f]), 0.0)
            field_ref[f, tiles, north, :] = jnp.where(has_n, sides(corner_ref[2, f], corner_ref[3, f]), 0.0)

    pack(depth_e, 1, d_pack, col_back)

    load_eta.wait()
    for s in range(n_bcol):
        slot = jnp.maximum(slot_of[s], 0)
        into = eta_recv if s == 0 else eta_send
        into[s] = eta_v[slot]

    pl.semaphore_wait(barrier, len(partners))
    d_copies = exchange(depth_e, 1, d_pack, d_halo, d_corner, d_sem)

    for g in range(groups):
        for copy in vel_loads[g]:
            copy.wait()

        def wet_body(i, carry, g=g):
            at = rows_at(i * CHUNK + CHUNK)
            for t in range(tiles):
                n = wet_levels[t, rows_at(i * CHUNK), :]
                for k in range(g * per_group, (g + 1) * per_group):
                    wet = n > k
                    for f in range(2):
                        vel[k, f, t, at, :] = jnp.where(wet, vel[k, f, t, at, :], 0.0)
            return carry

        lax.fori_loop(0, chunks, wet_body, 0)

    def edge_body(i, carry):
        at = rows_at(i * CHUNK + CHUNK)
        value = jnp.zeros((CHUNK, LANES), jnp.float32)
        for k in range(level_count):
            for f in range(2):
                j = 2 * k + f
                west = vel[k, f, 0, at, :]
                if j > 0:
                    west = pltpu.roll(west, j, 1)
                east = pltpu.roll(vel[k, f, tiles - 1, at, :], EAST_ROW + j + 1, 1)
                value = jnp.where(lanes == j, west, value)
                value = jnp.where(lanes == EAST_ROW + j, east, value)
        col_back[rows_at(i * CHUNK), :] = value
        return carry

    lax.fori_loop(0, chunks, edge_body, 0)
    col_send[...] = jnp.transpose(col_back[...])
    for k in range(level_count):
        for f in range(2):
            j = 2 * k + f
            for t in range(tiles):
                row_send[0, t, j : j + 1, :] = vel[k, f, t, CHUNK : CHUNK + 1, :]
                row_send[1, t, j : j + 1, :] = vel[k, f, t, CHUNK + rows - 1 : CHUNK + rows, :]
    count = 2 * level_count
    east_rows = slice(EAST_ROW, EAST_ROW + count)
    r1_pairs = (
        (row_send.at[0], row_recv.at[1]),
        (row_send.at[1], row_recv.at[0]),
        (col_send.at[0:count, :], col_recv.at[0:count, :]),
        (col_send.at[east_rows, :], col_recv.at[east_rows, :]),
    )
    r1_copies = []
    for d in (2, 3, 0, 1):
        src, dst = r1_pairs[d]
        copy = pltpu.make_async_remote_copy(
            src_ref=src, dst_ref=dst, send_sem=r1_sem.at[0, d], recv_sem=r1_sem.at[1, d],
            device_id=device(*DIRECTIONS[d]), device_id_type=MESH,
        )
        copy.start()
        r1_copies.append(copy)

    def all_pairs(send, recv, sems):
        copies = []
        for s in range(1, n_bcol):
            copy = pltpu.make_async_remote_copy(
                src_ref=send.at[s], dst_ref=recv.at[s], send_sem=sems.at[0, s], recv_sem=sems.at[1, s],
                device_id=device(0, s), device_id_type=MESH,
            )
            copy.start()
            copies.append(copy)
        return copies

    eta_copies = all_pairs(eta_send, eta_recv, eta_sem)

    arrived(d_copies, depth_e, 1, d_halo, d_corner, col_back)

    def weight_body(i, carry):
        start = i * CHUNK + CHUNK
        at = rows_at(start)
        dc = [depth_e[0, t, at, :] for t in range(ext)]
        dn = [depth_e[0, t, pl.ds(start - 1, CHUNK), :] for t in range(ext)]
        ds = [depth_e[0, t, pl.ds(start + 1, CHUNK), :] for t in range(ext)]
        de, dw = from_east(dc, lanes), from_west(dc, lanes)
        span = range(ext)
        north = [jnp.minimum(dc[t], dn[t]) for t in span]
        south = [jnp.minimum(dc[t], ds[t]) for t in span]
        east = [
            [jnp.minimum(dc[t], de[t]) for t in span],
            [0.5 * jnp.minimum(dn[t], de[t]) for t in span],
            [0.5 * jnp.minimum(ds[t], de[t]) for t in span],
        ]
        west = [
            [jnp.minimum(dc[t], dw[t]) for t in span],
            [0.5 * jnp.minimum(dn[t], dw[t]) for t in span],
            [0.5 * jnp.minimum(ds[t], dw[t]) for t in span],
        ]
        sum_w = from_west([east[0][t] + east[1][t] + east[2][t] for t in span], lanes)
        sum_e = from_east([west[0][t] + west[1][t] + west[2][t] for t in span], lanes)
        inv = [1.0 / (SURFACE_TERM + north[t] + south[t] + sum_w[t] + sum_e[t]) for t in span]
        inv_e, inv_w = from_east(inv, lanes), from_west(inv, lanes)
        for t in span:
            inv_c[t, at, :] = inv[t]
            weights[0, t, at, :] = north[t] * inv[t]
            weights[1, t, at, :] = south[t] * inv[t]
            for m in range(3):
                weights[2 + m, t, at, :] = east[m][t] * inv_e[t]
                weights[5 + m, t, at, :] = west[m][t] * inv_w[t]
        return carry

    lax.fori_loop(0, chunks + 2, weight_body, 0)

    for copy in load_wind:
        copy.wait()
    for copy in r1_copies:
        copy.wait_recv()
    has_n, has_s = r > 0, r < n_brow - 1
    has_w, has_e = c > 0, c < n_bcol - 1
    for k in range(level_count):
        for f in range(2):
            j = 2 * k + f
            for t in range(tiles):
                vel[k, f, t, CHUNK - 1 : CHUNK, :] = jnp.where(has_n, row_recv[0, t, j : j + 1, :], 0.0)
                vel[k, f, t, CHUNK + rows : CHUNK + rows + 1, :] = jnp.where(
                    has_s, row_recv[1, t, j : j + 1, :], 0.0
                )
    spare = jnp.zeros((EAST_ROW - count, rows), jnp.float32)
    halo = jnp.concatenate(
        [
            jnp.where(has_e, col_recv[0:count, :], 0.0),
            spare,
            jnp.where(has_w, col_recv[east_rows, :], 0.0),
            spare,
        ],
        axis=0,
    )
    col_back[...] = jnp.transpose(halo)

    total_rows = rows * n_brow

    def momentum_body(i, carry):
        here = rows_at(i * CHUNK)
        start = i * CHUNK + CHUNK
        at = rows_at(start)
        above, below = pl.ds(start - 1, CHUNK), pl.ds(start + 1, CHUNK)
        row_ids = (r * rows + i * CHUNK + lax.broadcasted_iota(jnp.int32, (CHUNK, LANES), 0)).astype(jnp.float32)
        coriolis = CORIOLIS * ((2.0 * row_ids + 1.0) * (1.0 / total_rows) - 1.0)
        sides = col_back[here, :]
        n = [wet_levels[t, here, :] for t in range(tiles)]
        sums = [[None] * tiles, [None] * tiles]
        for k in range(level_count):
            centre = [[vel[k, f, t, at, :] for t in range(tiles)] for f in range(2)]
            for f in range(2):
                j = 2 * k + f
                wide = pltpu.roll(sides, (EAST_ROW - j) % LANES, 1)
                far = pltpu.roll(sides, LANES - 1 - j, 1)
                west_rolled = [pltpu.roll(tile, 1, 1) for tile in centre[f]]
                east_rolled = [pltpu.roll(tile, LANES - 1, 1) for tile in centre[f]]
                for t in range(tiles):
                    west = jnp.where(lanes == 0, west_rolled[t - 1] if t > 0 else wide, west_rolled[t])
                    east = jnp.where(
                        lanes == LANES - 1, east_rolled[t + 1] if t < tiles - 1 else far, east_rolled[t]
                    )
                    spread = (west + east) + (vel[k, f, t, above, :] + vel[k, f, t, below, :]) + centre[f][t]
                    turn = coriolis * centre[1 - f][t]
                    value = VISCOSITY * spread + (turn if f == 0 else -turn)
                    if k == 0:
                        value = value + wind[f, t, here, :]
                    value = jnp.where(n[t] > k, value, 0.0)
                    star[f, k, here, columns(t)] = value
                    part = value * ((1.0 + k) / level_count)
                    sums[f][t] = part if k == 0 else sums[f][t] + part
        to = rows_at(i * CHUNK + PAD)
        for f in range(2):
            for t in range(tiles):
                trans_e[f, t, to, :] = sums[f][t]
        return carry

    lax.fori_loop(0, chunks, momentum_body, 0)
    pack(trans_e, 2, t_pack, col_back)
    t_copies = exchange(trans_e, 2, t_pack, t_halo, t_corner, t_sem)

    for copy in eta_copies:
        copy.wait_recv()
    for b in range(blocks):
        a, t = b // tiles, b % tiles
        guess = eta_recv[shift_of[b]]
        at = pl.ds(first + a * block_x, block_x)
        xa[0, t, at, :] = jnp.where(depth_e[0, t, at, :] > 0.0, guess, 0.0)
    pack(xa, 1, x_pack, col_back)
    x_copies = exchange(xa, 1, x_pack, x_halo, x_corner, x_sem)

    arrived(t_copies, trans_e, 2, t_halo, t_corner, col_back)

    def forcing_body(i, carry):
        start = i * CHUNK + CHUNK
        at = rows_at(start)
        above, below = pl.ds(start - 1, CHUNK), pl.ds(start + 1, CHUNK)
        second = [trans_e[1, t, at, :] for t in range(ext)]
        east, west = from_east(second, lanes), from_west(second, lanes)
        for t in range(ext):
            spread = trans_e[0, t, below, :] - trans_e[0, t, above, :] + east[t] - west[t]
            value = jnp.where(depth_e[0, t, at, :] > 0.0, -0.5 * spread, 0.0)
            forcing_e[t, at, :] = value * inv_c[t, at, :]
        return carry

    lax.fori_loop(0, chunks + 2, forcing_body, 0)

    arrived(x_copies, xa, 1, x_halo, x_corner, col_back)
    fields = (xa.at[0], xb)
    for sweep, (omega, beta) in enumerate(chebyshev_factors()):
        old, new = fields[sweep % 2], fields[(sweep + 1) % 2]
        if sweep == 1:
            for copy in x_copies:
                copy.wait_send()

        def sweep_body(i, carry, old=old, new=new, sweep=sweep, omega=omega, beta=beta):
            start = i * CHUNK + CHUNK
            at = rows_at(start)
            span = range(ext)
            xc = [old[t, at, :] for t in span]
            xn = [old[t, pl.ds(start - 1, CHUNK), :] for t in span]
            xs = [old[t, pl.ds(start + 1, CHUNK), :] for t in span]

            def side(base):
                return [
                    weights[base, t, at, :] * xc[t]
                    + weights[base + 1, t, at, :] * xn[t]
                    + weights[base + 2, t, at, :] * xs[t]
                    for t in span
                ]

            west, east = from_west(side(2), lanes), from_east(side(5), lanes)
            for t in span:
                near = weights[0, t, at, :] * xn[t] + weights[1, t, at, :] * xs[t]
                residual = (forcing_e[t, at, :] - xc[t]) + (near + (west[t] + east[t]))
                step = omega * residual
                if sweep > 0:
                    step = step + beta * step_e[t, at, :]
                if sweep < ITERS - 1:
                    step_e[t, at, :] = step
                new[t, at, :] = xc[t] + step
            return carry

        lax.fori_loop(0, chunks + 2, sweep_body, 0)
    result = fields[ITERS % 2]

    for b in range(blocks):
        height_b[b] = result[b % tiles, pl.ds(first + (b // tiles) * block_x, block_x), :]
    for s in range(n_bcol):
        into = height_recv if s == 0 else height_send
        into[s] = height_b[block_for[s]]
    height_copies = all_pairs(height_send, height_recv, height_sem)

    def final_body(i, carry):
        here = rows_at(i * CHUNK)
        start = i * CHUNK + PAD
        at = rows_at(start)
        span = range(ext)
        xc = [result[t, at, :] for t in span]
        east, west = from_east(xc, lanes), from_west(xc, lanes)
        for t in range(tiles):
            n = wet_levels[t, here, :]
            north, south = result[t, pl.ds(start - 1, CHUNK), :], result[t, pl.ds(start + 1, CHUNK), :]
            slopes = (0.5 * (south - north), 0.5 * (east[t] - west[t]))
            for k in range(level_count):
                wet = n > k
                for f in range(2):
                    star[f, k, here, columns(t)] = star[f, k, here, columns(t)] - jnp.where(wet, slopes[f], 0.0)
        return carry

    strips = 4
    strip_rows = rows // strips
    stores = []
    for strip in range(strips):
        lax.fori_loop(strip * chunks // strips, (strip + 1) * chunks // strips, final_body, 0)
        at = pl.ds(strip * strip_rows, strip_rows)
        for f, target in enumerate((u_out, v_out)):
            copy = pltpu.make_async_copy(star.at[f, :, at, :], target.at[:, at, :], out_sem.at[strip, f])
            copy.start()
            stores.append(copy)

    for copy in height_copies:
        copy.wait_recv()
    for slot in range(slots):
        source = source_of[slot]
        held = jnp.broadcast_to(source, (block_x, LANES)) >= 0
        height_v[slot] = jnp.where(held, height_recv[jnp.maximum(source, 0)], 0.0)
    copy = pltpu.make_async_copy(height_v, height_out, out_sem.at[strips, 0])
    copy.start()
    stores.append(copy)
    for copies in (d_copies, r1_copies, eta_copies, t_copies, height_copies):
        for copy in copies:
            copy.wait_send()
    for copy in stores:
        copy.wait()


def solution(mesh):
    n_brow, n_bcol = mesh.shape["brow"], mesh.shape["bcol"]

    def local(uvel, vvel, wind_stress, ocean_mask, depth_level, baro_owner, eta_guess):
        level_count, rows, width = uvel.shape
        slots, block_x, block_y = eta_guess.shape
        tiles = width // LANES
        ext = tiles + 1
        span = rows + 2 * PAD
        sizes = (n_brow, n_bcol, level_count, rows, tiles, block_x, slots)
        f32 = jnp.float32
        vmem = pltpu.VMEM
        any_spec = pl.BlockSpec(memory_space=pl.ANY)

        def halo_buffers(count):
            return [
                vmem((LANES, rows), f32),
                vmem((LANES, rows), f32),
                vmem((4, count, CHUNK, LANES), f32),
            ]

        scratch = [
            vmem((level_count, 2, tiles, rows + 2 * CHUNK, LANES), f32),
            vmem((2, level_count, rows, width), f32),
            vmem((2, tiles, rows, LANES), f32),
            vmem((tiles, rows, LANES), jnp.int32),
            vmem((tiles, rows, LANES), jnp.int32),
            vmem((slots, block_x, LANES), f32),
            vmem((tiles, rows, LANES), jnp.int32),
            vmem((1, ext, span, LANES), f32),
            vmem((2, ext, span, LANES), f32),
            vmem((1, ext, span, LANES), f32),
            vmem((ext, span, LANES), f32),
            vmem((ext, span, LANES), f32),
            vmem((ext, span, LANES), f32),
            vmem((ext, span, LANES), f32),
            vmem((8, ext, span, LANES), f32),
            vmem((n_bcol, block_x, LANES), f32),
            vmem((n_bcol, block_x, LANES), f32),
            vmem((n_bcol, block_x, LANES), f32),
            vmem((n_bcol, block_x, LANES), f32),
            vmem((slots, block_x, LANES), f32),
            vmem((2, tiles, 2 * level_count, LANES), f32),
            vmem((2, tiles, 2 * level_count, LANES), f32),
            vmem((LANES, rows), f32),
            vmem((LANES, rows), f32),
            vmem((rows, LANES), f32),
            *halo_buffers(1),
            *halo_buffers(2),
            *halo_buffers(1),
            vmem(((rows // block_x) * tiles, block_x, LANES), f32),
            pltpu.SemaphoreType.DMA((1 + 3 * tiles,)),
            pltpu.SemaphoreType.DMA((2, tiles, 2)),
            pltpu.SemaphoreType.DMA((5, 2)),
            pltpu.SemaphoreType.DMA((2, 4)),
            pltpu.SemaphoreType.DMA((2, 8)),
            pltpu.SemaphoreType.DMA((2, 8)),
            pltpu.SemaphoreType.DMA((2, 8)),
            pltpu.SemaphoreType.DMA((2, n_bcol)),
            pltpu.SemaphoreType.DMA((2, n_bcol)),
        ]
        return pl.pallas_call(
            functools.partial(kernel, sizes),
            out_shape=(
                jax.ShapeDtypeStruct(uvel.shape, f32),
                jax.ShapeDtypeStruct(vvel.shape, f32),
                jax.ShapeDtypeStruct(eta_guess.shape, f32),
            ),
            in_specs=[pl.BlockSpec(memory_space=pltpu.SMEM)] + [any_spec] * 6,
            out_specs=(any_spec, any_spec, any_spec),
            scratch_shapes=scratch,
            compiler_params=pltpu.CompilerParams(
                collective_id=0, has_side_effects=True, vmem_limit_bytes=56 * 1024 * 1024
            ),
            cost_estimate=pl.CostEstimate(flops=60_000_000, bytes_accessed=20_000_000, transcendentals=0),
        )(baro_owner, uvel, vvel, wind_stress, ocean_mask, depth_level, eta_guess)

    in_specs = (
        P(None, "brow", "bcol"),
        P(None, "brow", "bcol"),
        P(None, "brow", "bcol"),
        P("brow", "bcol"),
        P("brow", "bcol"),
        P(),
        P(("brow", "bcol"), None, None),
    )
    out_specs = (P(None, "brow", "bcol"), P(None, "brow", "bcol"), P(("brow", "bcol"), None, None))
    return jax.shard_map(local, mesh=mesh, in_specs=in_specs, out_specs=out_specs, check_vma=False)
```

```python
import functools

import jax
import jax.numpy as jnp
from jax import lax
from jax.experimental import pallas as pl
from jax.experimental.pallas import tpu as pltpu
from jax.sharding import PartitionSpec as P

ITERS = 4
VISCOSITY = 0.2
CORIOLIS = 0.5
SURFACE_TERM = 0.25
LOWER_BOUND = 0.05
UPPER_BOUND = 2.0

LANES = 128
CHUNK = 8
PAD = 16
EAST_ROW = 64
MESH = pl.DeviceIdType.MESH
DIRECTIONS = ((-1, 0), (1, 0), (0, -1), (0, 1), (-1, -1), (-1, 1), (1, -1), (1, 1))


def chebyshev_factors():
    alpha = 2.0 / (UPPER_BOUND - LOWER_BOUND)
    gamma = (UPPER_BOUND + LOWER_BOUND) / 2.0
    omega = 2.0 / gamma
    factors = [(1.0 / gamma, 0.0)]
    for _ in range(ITERS - 1):
        omega = 1.0 / (gamma - omega / (4.0 * alpha * alpha))
        factors.append((omega, gamma * omega - 1.0))
    return factors


def lane_ids():
    return lax.broadcasted_iota(jnp.int32, (CHUNK, LANES), 1)


def from_west(tiles, lanes):
    rolled = [pltpu.roll(tile, 1, 1) for tile in tiles]
    return [jnp.where(lanes == 0, rolled[t - 1], rolled[t]) for t in range(len(tiles))]


def from_east(tiles, lanes):
    rolled = [pltpu.roll(tile, LANES - 1, 1) for tile in tiles]
    count = len(tiles)
    return [jnp.where(lanes == LANES - 1, rolled[(t + 1) % count], rolled[t]) for t in range(count)]


def grouped(first, count, group, body):
    def step(i, carry):
        for m in range(group):
            body(first + i * group + m)
        return carry

    lax.fori_loop(0, count // group, step, 0)


def with_rim(chunks, group, body):
    grouped(1, chunks, group, body)
    for edge in (0, chunks + 1):
        body(jnp.int32(edge))


def rows_at(start):
    return pl.ds(pl.multiple_of(start, CHUNK), CHUNK)


def kernel(
    sizes,
    owner_ref, u_hbm, v_hbm, wind_hbm, mask_hbm, level_hbm, eta_hbm,
    u_out, v_out, height_out,
    vel, star, wind, mask_v, level_v, eta_v, wet_levels,
    depth_e, trans_e, xa, xb, forcing_e, step_e, inv_c, weights,
    eta_send, eta_recv, height_send, height_recv, height_v,
    row_send, row_recv, col_send, col_recv, col_back,
    d_pack, d_halo, d_corner, t_pack, t_halo, t_corner, x_pack, x_halo, x_corner,
    height_b,
    load_sem, vel_sem, out_sem,
    r1_sem, d_sem, t_sem, x_sem, eta_sem, height_sem,
):
    n_brow, n_bcol, level_count, rows, tiles, block_x, slots = sizes
    blocks_x = rows // block_x
    blocks = blocks_x * tiles
    chunks = rows // CHUNK
    ext = tiles + 1
    first, last = PAD, PAD + rows
    r = lax.axis_index("brow")
    c = lax.axis_index("bcol")
    lanes = lane_ids()

    def device(dr, dc):
        return (lax.rem(r + dr + n_brow, n_brow), lax.rem(c + dc + n_bcol, n_bcol))

    loads = []

    def load(src, dst):
        copy = pltpu.make_async_copy(src, dst, load_sem.at[len(loads)])
        copy.start()
        loads.append(copy)
        return copy

    def columns(t):
        return slice(t * LANES, (t + 1) * LANES)

    load_eta = load(eta_hbm, eta_v)
    load_masks = []
    for t in range(tiles):
        load_masks.append(load(mask_hbm.at[:, columns(t)], mask_v.at[t]))
        load_masks.append(load(level_hbm.at[:, columns(t)], level_v.at[t]))
    groups = 2
    per_group = level_count // groups
    vel_loads = []
    for g in range(groups):
        these = []
        for t in range(tiles):
            for f, source in enumerate((u_hbm, v_hbm)):
                copy = pltpu.make_async_copy(
                    source.at[g * per_group : (g + 1) * per_group, :, columns(t)],
                    vel.at[g * per_group : (g + 1) * per_group, f, t, CHUNK : CHUNK + rows, :],
                    vel_sem.at[g, t, f],
                )
                copy.start()
                these.append(copy)
        vel_loads.append(these)
    load_wind = [load(wind_hbm.at[:, :, columns(t)], wind.at[:, t]) for t in range(tiles)]

    barrier = pltpu.get_barrier_semaphore()
    partners = [(0, s) for s in range(1, n_bcol)]
    partners += [(dr, dc) for dr, dc in DIRECTIONS if dr != 0]
    for dr, dc in partners:
        pl.semaphore_signal(barrier, inc=1, device_id=device(dr, dc), device_id_type=MESH)

    zero = jnp.zeros((CHUNK, LANES), jnp.float32)
    for t in range(ext):
        for ref in (depth_e.at[0], trans_e.at[0], trans_e.at[1], xa.at[0], xb):
            ref[t, 0:CHUNK, :] = zero
            ref[t, last + CHUNK : last + 2 * CHUNK, :] = zero

    device_first = (r * n_bcol + c) * slots
    none = jnp.int32(-1)
    slot_of = []
    for s in range(n_bcol):
        q = lax.rem(c + s, n_bcol)
        found = none
        for b in range(blocks):
            local = owner_ref[r * blocks_x + b // tiles, q * tiles + b % tiles] - device_first
            found = jnp.where((local >= 0) & (local < slots), local, found)
        slot_of.append(found)
    owners = [owner_ref[r * blocks_x + b // tiles, c * tiles + b % tiles] for b in range(blocks)]
    block_for, shift_of = [], [jnp.int32(0)] * blocks
    for s in range(n_bcol):
        holder_first = (r * n_bcol + lax.rem(c + s, n_bcol)) * slots
        found = jnp.int32(0)
        for b in range(blocks):
            here = (owners[b] >= holder_first) & (owners[b] < holder_first + slots)
            found = jnp.where(here, b, found)
            shift_of[b] = jnp.where(here, (n_bcol - s) % n_bcol, shift_of[b])
        block_for.append(found)
    source_of = []
    for slot in range(slots):
        found = none
        for s in range(n_bcol):
            found = jnp.where(slot_of[s] == slot, (n_bcol - s) % n_bcol, found)
        source_of.append(found)

    for copy in load_masks:
        copy.wait()

    def depth_body(i):
        at = rows_at(i * CHUNK)
        to = rows_at(i * CHUNK + PAD)
        for t in range(tiles):
            n = mask_v[t, at, :] * level_v[t, at, :]
            wet_levels[t, at, :] = n
            nf = n.astype(jnp.float32)
            depth_e[0, t, to, :] = nf * (nf + 1.0) * (1.0 / (2 * level_count))

    grouped(0, chunks, 4, depth_body)

    def pack(field_ref, count, packed_ref, back_ref):
        def pack_body(i):
            at = rows_at(i * CHUNK + PAD)
            value = jnp.zeros((CHUNK, LANES), jnp.float32)
            for f in range(count):
                low = EAST_ROW + CHUNK * f
                west = field_ref[f, 0, at, :]
                east = pltpu.roll(field_ref[f, tiles - 1, at, :], (low + CHUNK) % LANES, 1)
                if f > 0:
                    west = pltpu.roll(west, CHUNK * f, 1)
                value = jnp.where((lanes >= CHUNK * f) & (lanes < CHUNK * (f + 1)), west, value)
                value = jnp.where((lanes >= low) & (lanes < low + CHUNK), east, value)
            back_ref[rows_at(i * CHUNK), :] = value

        grouped(0, chunks, 16, pack_body)
        packed_ref[...] = jnp.transpose(back_ref[...])

    def exchange(field_ref, count, packed_ref, halo_ref, corner_ref, sems):
        height = CHUNK * count
        top, bottom = pl.ds(first, CHUNK), pl.ds(last - CHUNK, CHUNK)
        pairs = (
            (field_ref.at[:, 0:tiles, top, :], field_ref.at[:, 0:tiles, pl.ds(last, CHUNK), :]),
            (field_ref.at[:, 0:tiles, bottom, :], field_ref.at[:, 0:tiles, pl.ds(first - CHUNK, CHUNK), :]),
            (packed_ref.at[0:height, :], halo_ref.at[0:height, :]),
            (packed_ref.at[EAST_ROW : EAST_ROW + height, :], halo_ref.at[EAST_ROW : EAST_ROW + height, :]),
            (field_ref.at[:, 0, top, :], corner_ref.at[0]),
            (field_ref.at[:, tiles - 1, top, :], corner_ref.at[1]),
            (field_ref.at[:, 0, bottom, :], corner_ref.at[2]),
            (field_ref.at[:, tiles - 1, bottom, :], corner_ref.at[3]),
        )
        copies = []
        for d in (2, 3, 0, 1, 4, 5, 6, 7):
            src, dst = pairs[d]
            copy = pltpu.make_async_remote_copy(
                src_ref=src, dst_ref=dst, send_sem=sems.at[0, d], recv_sem=sems.at[1, d],
                device_id=device(*DIRECTIONS[d]), device_id_type=MESH,
            )
            copy.start()
            copies.append(copy)
        return copies

    def arrived(copies, field_ref, count, halo_ref, corner_ref, back_ref):
        for copy in copies:
            copy.wait_recv()
        has_n, has_s, has_w, has_e = r > 0, r < n_brow - 1, c > 0, c < n_bcol - 1
        height = CHUNK * count
        spare = jnp.zeros((EAST_ROW - height, rows), jnp.float32)
        halo = jnp.concatenate(
            [halo_ref[0:height, :], spare, halo_ref[EAST_ROW : EAST_ROW + height, :], spare], axis=0
        )
        back_ref[...] = jnp.transpose(halo)
        right = (lanes < CHUNK) & has_e
        left = (lanes >= LANES - CHUNK) & has_w

        def sides(east, west):
            return jnp.where(right, east, jnp.where(left, west, 0.0))

        def side_body(i):
            value = back_ref[rows_at(i * CHUNK), :]
            for f in range(count):
                east = value if f == 0 else pltpu.roll(value, LANES - CHUNK * f, 1)
                west = pltpu.roll(value, (2 * LANES - CHUNK - EAST_ROW - CHUNK * f) % LANES, 1)
                field_ref[f, tiles, rows_at(i * CHUNK + PAD), :] = sides(east, west)

        grouped(0, chunks, 16, side_body)
        north, south = pl.ds(first - CHUNK, CHUNK), pl.ds(last, CHUNK)
        for f in range(count):
            for t in range(tiles):
                field_ref[f, t, north, :] = jnp.where(has_n, field_ref[f, t, north, :], 0.0)
                field_ref[f, t, south, :] = jnp.where(has_s, field_ref[f, t, south, :], 0.0)
            field_ref[f, tiles, south, :] = jnp.where(has_s, sides(corner_ref[0, f], corner_ref[1, f]), 0.0)
            field_ref[f, tiles, north, :] = jnp.where(has_n, sides(corner_ref[2, f], corner_ref[3, f]), 0.0)

    pack(depth_e, 1, d_pack, col_back)

    load_eta.wait()
    for s in range(n_bcol):
        slot = jnp.maximum(slot_of[s], 0)
        into = eta_recv if s == 0 else eta_send
        into[s] = eta_v[slot]

    pl.semaphore_wait(barrier, len(partners))
    d_copies = exchange(depth_e, 1, d_pack, d_halo, d_corner, d_sem)

    for g in range(groups):
        for copy in vel_loads[g]:
            copy.wait()

        def wet_body(i, g=g):
            at = rows_at(i * CHUNK + CHUNK)
            for t in range(tiles):
                n = wet_levels[t, rows_at(i * CHUNK), :]
                for k in range(g * per_group, (g + 1) * per_group):
                    wet = n > k
                    for f in range(2):
                        vel[k, f, t, at, :] = jnp.where(wet, vel[k, f, t, at, :], 0.0)

        grouped(0, chunks, 2, wet_body)

    def edge_body(i):
        at = rows_at(i * CHUNK + CHUNK)
        low = jnp.zeros((CHUNK, LANES), jnp.float32)
        high = low
        for k in range(level_count):
            for f in range(2):
                j = 2 * k + f
                west = vel[k, f, 0, at, :]
                if j > 0:
                    west = pltpu.roll(west, j, 1)
                east = pltpu.roll(vel[k, f, tiles - 1, at, :], EAST_ROW + j + 1, 1)
                low = jnp.where(lanes == j, west, low)
                high = jnp.where(lanes == EAST_ROW + j, east, high)
        col_back[rows_at(i * CHUNK), :] = jnp.where(lanes < EAST_ROW, low, high)

    grouped(0, chunks, 8, edge_body)
    col_send[...] = jnp.transpose(col_back[...])
    for k in range(level_count):
        for f in range(2):
            j = 2 * k + f
            for t in range(tiles):
                row_send[0, t, j : j + 1, :] = vel[k, f, t, CHUNK : CHUNK + 1, :]
                row_send[1, t, j : j + 1, :] = vel[k, f, t, CHUNK + rows - 1 : CHUNK + rows, :]
    count = 2 * level_count
    east_rows = slice(EAST_ROW, EAST_ROW + count)
    r1_pairs = (
        (row_send.at[0], row_recv.at[1]),
        (row_send.at[1], row_recv.at[0]),
        (col_send.at[0:count, :], col_recv.at[0:count, :]),
        (col_send.at[east_rows, :], col_recv.at[east_rows, :]),
    )
    r1_copies = []
    for d in (2, 3, 0, 1):
        src, dst = r1_pairs[d]
        copy = pltpu.make_async_remote_copy(
            src_ref=src, dst_ref=dst, send_sem=r1_sem.at[0, d], recv_sem=r1_sem.at[1, d],
            device_id=device(*DIRECTIONS[d]), device_id_type=MESH,
        )
        copy.start()
        r1_copies.append(copy)

    def all_pairs(send, recv, sems):
        copies = []
        for s in range(1, n_bcol):
            copy = pltpu.make_async_remote_copy(
                src_ref=send.at[s], dst_ref=recv.at[s], send_sem=sems.at[0, s], recv_sem=sems.at[1, s],
                device_id=device(0, s), device_id_type=MESH,
            )
            copy.start()
            copies.append(copy)
        return copies

    eta_copies = all_pairs(eta_send, eta_recv, eta_sem)

    arrived(d_copies, depth_e, 1, d_halo, d_corner, col_back)

    def weight_body(i):
        start = i * CHUNK + CHUNK
        at = rows_at(start)
        dc = [depth_e[0, t, at, :] for t in range(ext)]
        dn = [depth_e[0, t, pl.ds(start - 1, CHUNK), :] for t in range(ext)]
        ds = [depth_e[0, t, pl.ds(start + 1, CHUNK), :] for t in range(ext)]
        de, dw = from_east(dc, lanes), from_west(dc, lanes)
        span = range(ext)
        north = [jnp.minimum(dc[t], dn[t]) for t in span]
        south = [jnp.minimum(dc[t], ds[t]) for t in span]
        east = [
            [jnp.minimum(dc[t], de[t]) for t in span],
            [0.5 * jnp.minimum(dn[t], de[t]) for t in span],
            [0.5 * jnp.minimum(ds[t], de[t]) for t in span],
        ]
        west = [
            [jnp.minimum(dc[t], dw[t]) for t in span],
            [0.5 * jnp.minimum(dn[t], dw[t]) for t in span],
            [0.5 * jnp.minimum(ds[t], dw[t]) for t in span],
        ]
        sum_w = from_west([east[0][t] + east[1][t] + east[2][t] for t in span], lanes)
        sum_e = from_east([west[0][t] + west[1][t] + west[2][t] for t in span], lanes)
        inv = [1.0 / (SURFACE_TERM + north[t] + south[t] + sum_w[t] + sum_e[t]) for t in span]
        inv_e, inv_w = from_east(inv, lanes), from_west(inv, lanes)
        for t in span:
            inv_c[t, at, :] = inv[t]
            weights[0, t, at, :] = north[t] * inv[t]
            weights[1, t, at, :] = south[t] * inv[t]
            for m in range(3):
                weights[2 + m, t, at, :] = east[m][t] * inv_e[t]
                weights[5 + m, t, at, :] = west[m][t] * inv_w[t]

    with_rim(chunks, 8, weight_body)

    for copy in load_wind:
        copy.wait()
    for copy in r1_copies:
        copy.wait_recv()
    has_n, has_s = r > 0, r < n_brow - 1
    has_w, has_e = c > 0, c < n_bcol - 1
    for k in range(level_count):
        for f in range(2):
            j = 2 * k + f
            for t in range(tiles):
                vel[k, f, t, CHUNK - 1 : CHUNK, :] = jnp.where(has_n, row_recv[0, t, j : j + 1, :], 0.0)
                vel[k, f, t, CHUNK + rows : CHUNK + rows + 1, :] = jnp.where(
                    has_s, row_recv[1, t, j : j + 1, :], 0.0
                )
    spare = jnp.zeros((EAST_ROW - count, rows), jnp.float32)
    halo = jnp.concatenate(
        [
            jnp.where(has_e, col_recv[0:count, :], 0.0),
            spare,
            jnp.where(has_w, col_recv[east_rows, :], 0.0),
            spare,
        ],
        axis=0,
    )
    col_back[...] = jnp.transpose(halo)

    total_rows = rows * n_brow

    def momentum_body(i):
        here = rows_at(i * CHUNK)
        start = i * CHUNK + CHUNK
        at = rows_at(start)
        above, below = pl.ds(start - 1, CHUNK), pl.ds(start + 1, CHUNK)
        row_ids = (r * rows + i * CHUNK + lax.broadcasted_iota(jnp.int32, (CHUNK, LANES), 0)).astype(jnp.float32)
        coriolis = CORIOLIS * ((2.0 * row_ids + 1.0) * (1.0 / total_rows) - 1.0)
        sides = col_back[here, :]
        n = [wet_levels[t, here, :] for t in range(tiles)]
        sums = [[None] * tiles, [None] * tiles]
        for k in range(level_count):
            centre = [[vel[k, f, t, at, :] for t in range(tiles)] for f in range(2)]
            for f in range(2):
                j = 2 * k + f
                wide = pltpu.roll(sides, (EAST_ROW - j) % LANES, 1)
                far = pltpu.roll(sides, LANES - 1 - j, 1)
                west_rolled = [pltpu.roll(tile, 1, 1) for tile in centre[f]]
                east_rolled = [pltpu.roll(tile, LANES - 1, 1) for tile in centre[f]]
                for t in range(tiles):
                    west = jnp.where(lanes == 0, west_rolled[t - 1] if t > 0 else wide, west_rolled[t])
                    east = jnp.where(
                        lanes == LANES - 1, east_rolled[t + 1] if t < tiles - 1 else far, east_rolled[t]
                    )
                    spread = (west + east) + (vel[k, f, t, above, :] + vel[k, f, t, below, :]) + centre[f][t]
                    turn = coriolis * centre[1 - f][t]
                    value = VISCOSITY * spread + (turn if f == 0 else -turn)
                    if k == 0:
                        value = value + wind[f, t, here, :]
                    value = jnp.where(n[t] > k, value, 0.0)
                    star[f, k, here, columns(t)] = value
                    part = value * ((1.0 + k) / level_count)
                    sums[f][t] = part if k == 0 else sums[f][t] + part
        to = rows_at(i * CHUNK + PAD)
        for f in range(2):
            for t in range(tiles):
                trans_e[f, t, to, :] = sums[f][t]

    grouped(0, chunks, 2, momentum_body)
    pack(trans_e, 2, t_pack, col_back)
    t_copies = exchange(trans_e, 2, t_pack, t_halo, t_corner, t_sem)

    for copy in eta_copies:
        copy.wait_recv()
    for b in range(blocks):
        a, t = b // tiles, b % tiles
        guess = eta_recv[shift_of[b]]
        at = pl.ds(first + a * block_x, block_x)
        xa[0, t, at, :] = jnp.where(depth_e[0, t, at, :] > 0.0, guess, 0.0)
    pack(xa, 1, x_pack, col_back)
    x_copies = exchange(xa, 1, x_pack, x_halo, x_corner, x_sem)

    arrived(t_copies, trans_e, 2, t_halo, t_corner, col_back)

    def forcing_body(i):
        start = i * CHUNK + CHUNK
        at = rows_at(start)
        above, below = pl.ds(start - 1, CHUNK), pl.ds(start + 1, CHUNK)
        second = [trans_e[1, t, at, :] for t in range(ext)]
        east, west = from_east(second, lanes), from_west(second, lanes)
        for t in range(ext):
            spread = trans_e[0, t, below, :] - trans_e[0, t, above, :] + east[t] - west[t]
            value = jnp.where(depth_e[0, t, at, :] > 0.0, -0.5 * spread, 0.0)
            forcing_e[t, at, :] = value * inv_c[t, at, :]

    with_rim(chunks, 16, forcing_body)

    arrived(x_copies, xa, 1, x_halo, x_corner, col_back)
    fields = (xa.at[0], xb)
    for sweep, (omega, beta) in enumerate(chebyshev_factors()):
        old, new = fields[sweep % 2], fields[(sweep + 1) % 2]
        if sweep == 1:
            for copy in x_copies:
                copy.wait_send()

        def sweep_body(i, old=old, new=new, sweep=sweep, omega=omega, beta=beta):
            start = i * CHUNK + CHUNK
            at = rows_at(start)
            span = range(ext)
            xc = [old[t, at, :] for t in span]
            xn = [old[t, pl.ds(start - 1, CHUNK), :] for t in span]
            xs = [old[t, pl.ds(start + 1, CHUNK), :] for t in span]

            def side(base):
                return [
                    weights[base, t, at, :] * xc[t]
                    + weights[base + 1, t, at, :] * xn[t]
                    + weights[base + 2, t, at, :] * xs[t]
                    for t in span
                ]

            west, east = from_west(side(2), lanes), from_east(side(5), lanes)
            for t in span:
                near = weights[0, t, at, :] * xn[t] + weights[1, t, at, :] * xs[t]
                residual = (forcing_e[t, at, :] - xc[t]) + (near + (west[t] + east[t]))
                step = omega * residual
                if sweep > 0:
                    step = step + beta * step_e[(sweep + 1) % 2, t, at, :]
                if sweep < ITERS - 1:
                    step_e[sweep % 2, t, at, :] = step
                new[t, at, :] = xc[t] + step

        with_rim(chunks, 16, sweep_body)
    result = fields[ITERS % 2]

    for b in range(blocks):
        height_b[b] = result[b % tiles, pl.ds(first + (b // tiles) * block_x, block_x), :]
    for s in range(n_bcol):
        into = height_recv if s == 0 else height_send
        into[s] = height_b[block_for[s]]
    height_copies = all_pairs(height_send, height_recv, height_sem)

    def final_body(i):
        here = rows_at(i * CHUNK)
        start = i * CHUNK + PAD
        at = rows_at(start)
        span = range(ext)
        xc = [result[t, at, :] for t in span]
        east, west = from_east(xc, lanes), from_west(xc, lanes)
        for t in range(tiles):
            n = wet_levels[t, here, :]
            north, south = result[t, pl.ds(start - 1, CHUNK), :], result[t, pl.ds(start + 1, CHUNK), :]
            slopes = (0.5 * (south - north), 0.5 * (east[t] - west[t]))
            for k in range(level_count):
                wet = n > k
                for f in range(2):
                    star[f, k, here, columns(t)] = star[f, k, here, columns(t)] - jnp.where(wet, slopes[f], 0.0)

    strips = 4
    strip_rows = rows // strips
    stores = []
    for strip in range(strips):
        grouped(strip * chunks // strips, chunks // strips, 2, final_body)
        at = pl.ds(strip * strip_rows, strip_rows)
        for f, target in enumerate((u_out, v_out)):
            copy = pltpu.make_async_copy(star.at[f, :, at, :], target.at[:, at, :], out_sem.at[strip, f])
            copy.start()
            stores.append(copy)

    for copy in height_copies:
        copy.wait_recv()
    for slot in range(slots):
        source = source_of[slot]
        held = jnp.broadcast_to(source, (block_x, LANES)) >= 0
        height_v[slot] = jnp.where(held, height_recv[jnp.maximum(source, 0)], 0.0)
    copy = pltpu.make_async_copy(height_v, height_out, out_sem.at[strips, 0])
    copy.start()
    stores.append(copy)
    for copies in (d_copies, r1_copies, eta_copies, t_copies, height_copies):
        for copy in copies:
            copy.wait_send()
    for copy in stores:
        copy.wait()


def solution(mesh):
    n_brow, n_bcol = mesh.shape["brow"], mesh.shape["bcol"]

    def local(uvel, vvel, wind_stress, ocean_mask, depth_level, baro_owner, eta_guess):
        level_count, rows, width = uvel.shape
        slots, block_x, block_y = eta_guess.shape
        tiles = width // LANES
        ext = tiles + 1
        span = rows + 2 * PAD
        sizes = (n_brow, n_bcol, level_count, rows, tiles, block_x, slots)
        f32 = jnp.float32
        vmem = pltpu.VMEM
        any_spec = pl.BlockSpec(memory_space=pl.ANY)

        def halo_buffers(count):
            return [
                vmem((LANES, rows), f32),
                vmem((LANES, rows), f32),
                vmem((4, count, CHUNK, LANES), f32),
            ]

        scratch = [
            vmem((level_count, 2, tiles, rows + 2 * CHUNK, LANES), f32),
            vmem((2, level_count, rows, width), f32),
            vmem((2, tiles, rows, LANES), f32),
            vmem((tiles, rows, LANES), jnp.int32),
            vmem((tiles, rows, LANES), jnp.int32),
            vmem((slots, block_x, LANES), f32),
            vmem((tiles, rows, LANES), jnp.int32),
            vmem((1, ext, span, LANES), f32),
            vmem((2, ext, span, LANES), f32),
            vmem((1, ext, span, LANES), f32),
            vmem((ext, span, LANES), f32),
            vmem((ext, span, LANES), f32),
            vmem((2, ext, span, LANES), f32),
            vmem((ext, span, LANES), f32),
            vmem((8, ext, span, LANES), f32),
            vmem((n_bcol, block_x, LANES), f32),
            vmem((n_bcol, block_x, LANES), f32),
            vmem((n_bcol, block_x, LANES), f32),
            vmem((n_bcol, block_x, LANES), f32),
            vmem((slots, block_x, LANES), f32),
            vmem((2, tiles, 2 * level_count, LANES), f32),
            vmem((2, tiles, 2 * level_count, LANES), f32),
            vmem((LANES, rows), f32),
            vmem((LANES, rows), f32),
            vmem((rows, LANES), f32),
            *halo_buffers(1),
            *halo_buffers(2),
            *halo_buffers(1),
            vmem(((rows // block_x) * tiles, block_x, LANES), f32),
            pltpu.SemaphoreType.DMA((1 + 3 * tiles,)),
            pltpu.SemaphoreType.DMA((2, tiles, 2)),
            pltpu.SemaphoreType.DMA((5, 2)),
            pltpu.SemaphoreType.DMA((2, 4)),
            pltpu.SemaphoreType.DMA((2, 8)),
            pltpu.SemaphoreType.DMA((2, 8)),
            pltpu.SemaphoreType.DMA((2, 8)),
            pltpu.SemaphoreType.DMA((2, n_bcol)),
            pltpu.SemaphoreType.DMA((2, n_bcol)),
        ]
        return pl.pallas_call(
            functools.partial(kernel, sizes),
            out_shape=(
                jax.ShapeDtypeStruct(uvel.shape, f32),
                jax.ShapeDtypeStruct(vvel.shape, f32),
                jax.ShapeDtypeStruct(eta_guess.shape, f32),
            ),
            in_specs=[pl.BlockSpec(memory_space=pltpu.SMEM)] + [any_spec] * 6,
            out_specs=(any_spec, any_spec, any_spec),
            scratch_shapes=scratch,
            compiler_params=pltpu.CompilerParams(
                collective_id=0, has_side_effects=True, vmem_limit_bytes=56 * 1024 * 1024
            ),
            cost_estimate=pl.CostEstimate(flops=60_000_000, bytes_accessed=20_000_000, transcendentals=0),
        )(baro_owner, uvel, vvel, wind_stress, ocean_mask, depth_level, eta_guess)

    in_specs = (
        P(None, "brow", "bcol"),
        P(None, "brow", "bcol"),
        P(None, "brow", "bcol"),
        P("brow", "bcol"),
        P("brow", "bcol"),
        P(),
        P(("brow", "bcol"), None, None),
    )
    out_specs = (P(None, "brow", "bcol"), P(None, "brow", "bcol"), P(("brow", "bcol"), None, None))
    return jax.shard_map(local, mesh=mesh, in_specs=in_specs, out_specs=out_specs, check_vma=False)
```

```python
import functools

import jax
import jax.numpy as jnp
from jax import lax
from jax.experimental import pallas as pl
from jax.experimental.pallas import tpu as pltpu
from jax.sharding import PartitionSpec as P

ITERS = 4
VISCOSITY = 0.2
CORIOLIS = 0.5
SURFACE_TERM = 0.25
LOWER_BOUND = 0.05
UPPER_BOUND = 2.0

LANES = 128
CHUNK = 8
PAD = 16
EAST_ROW = 64
MESH = pl.DeviceIdType.MESH
DIRECTIONS = ((-1, 0), (1, 0), (0, -1), (0, 1), (-1, -1), (-1, 1), (1, -1), (1, 1))


def chebyshev_factors():
    alpha = 2.0 / (UPPER_BOUND - LOWER_BOUND)
    gamma = (UPPER_BOUND + LOWER_BOUND) / 2.0
    omega = 2.0 / gamma
    factors = [(1.0 / gamma, 0.0)]
    for _ in range(ITERS - 1):
        omega = 1.0 / (gamma - omega / (4.0 * alpha * alpha))
        factors.append((omega, gamma * omega - 1.0))
    return factors


def lane_ids():
    return lax.broadcasted_iota(jnp.int32, (CHUNK, LANES), 1)


def from_west(tiles, lanes):
    rolled = [pltpu.roll(tile, 1, 1) for tile in tiles]
    return [jnp.where(lanes == 0, rolled[t - 1], rolled[t]) for t in range(len(tiles))]


def from_east(tiles, lanes):
    rolled = [pltpu.roll(tile, LANES - 1, 1) for tile in tiles]
    count = len(tiles)
    return [jnp.where(lanes == LANES - 1, rolled[(t + 1) % count], rolled[t]) for t in range(count)]


def grouped(first, count, group, body):
    def step(i, carry):
        for m in range(group):
            body(first + i * group + m)
        return carry

    lax.fori_loop(0, count // group, step, 0)


def with_rim(chunks, group, body):
    grouped(1, chunks, group, body)
    for edge in (0, chunks + 1):
        body(jnp.int32(edge))


def rows_at(start):
    return pl.ds(pl.multiple_of(start, CHUNK), CHUNK)


def kernel(
    sizes,
    owner_ref, u_hbm, v_hbm, wind_hbm, mask_hbm, level_hbm, eta_hbm,
    u_out, v_out, height_out,
    vel, wind, mask_v, level_v, eta_v, wet_levels,
    depth_e, trans_e, xa, xb, forcing_e, step_e, inv_c, weights,
    eta_send, eta_recv, height_send, height_recv,
    row_send, row_recv, col_send, col_recv, col_back, x_back,
    d_pack, d_halo, d_corner, t_pack, t_halo, t_corner, x_pack, x_halo, x_corner,
    height_b,
    load_sem, vel_sem,
    r1_sem, d_sem, t_sem, x_sem, eta_sem, height_sem,
):
    n_brow, n_bcol, level_count, rows, tiles, block_x, slots = sizes
    blocks_x = rows // block_x
    blocks = blocks_x * tiles
    chunks = rows // CHUNK
    ext = tiles + 1
    first, last = PAD, PAD + rows
    star = (u_out, v_out)
    r = lax.axis_index("brow")
    c = lax.axis_index("bcol")
    lanes = lane_ids()

    def device(dr, dc):
        return (lax.rem(r + dr + n_brow, n_brow), lax.rem(c + dc + n_bcol, n_bcol))

    loads = []

    def load(src, dst):
        copy = pltpu.make_async_copy(src, dst, load_sem.at[len(loads)])
        copy.start()
        loads.append(copy)
        return copy

    def columns(t):
        return slice(t * LANES, (t + 1) * LANES)

    load_eta = load(eta_hbm, eta_v)
    load_masks = []
    for t in range(tiles):
        load_masks.append(load(mask_hbm.at[:, columns(t)], mask_v.at[t]))
        load_masks.append(load(level_hbm.at[:, columns(t)], level_v.at[t]))
    groups = 2
    per_group = level_count // groups
    vel_loads = []
    for g in range(groups):
        these = []
        for t in range(tiles):
            for f, source in enumerate((u_hbm, v_hbm)):
                copy = pltpu.make_async_copy(
                    source.at[g * per_group : (g + 1) * per_group, :, columns(t)],
                    vel.at[g * per_group : (g + 1) * per_group, f, t, CHUNK : CHUNK + rows, :],
                    vel_sem.at[g, t, f],
                )
                copy.start()
                these.append(copy)
        vel_loads.append(these)
    load_wind = [load(wind_hbm.at[:, :, columns(t)], wind.at[:, t]) for t in range(tiles)]

    barrier = pltpu.get_barrier_semaphore()
    partners = [(0, s) for s in range(1, n_bcol)]
    partners += [(dr, dc) for dr, dc in DIRECTIONS if dr != 0]
    for dr, dc in partners:
        pl.semaphore_signal(barrier, inc=1, device_id=device(dr, dc), device_id_type=MESH)

    zero = jnp.zeros((CHUNK, LANES), jnp.float32)
    for t in range(ext):
        for ref in (depth_e.at[0], trans_e.at[0], trans_e.at[1], xa.at[0], xb):
            ref[t, 0:CHUNK, :] = zero
            ref[t, last + CHUNK : last + 2 * CHUNK, :] = zero

    device_first = (r * n_bcol + c) * slots
    none = jnp.int32(-1)
    slot_of = []
    for s in range(n_bcol):
        q = lax.rem(c + s, n_bcol)
        found = none
        for b in range(blocks):
            local = owner_ref[r * blocks_x + b // tiles, q * tiles + b % tiles] - device_first
            found = jnp.where((local >= 0) & (local < slots), local, found)
        slot_of.append(found)
    owners = [owner_ref[r * blocks_x + b // tiles, c * tiles + b % tiles] for b in range(blocks)]
    block_for, shift_of = [], [jnp.int32(0)] * blocks
    for s in range(n_bcol):
        holder_first = (r * n_bcol + lax.rem(c + s, n_bcol)) * slots
        found = jnp.int32(0)
        for b in range(blocks):
            here = (owners[b] >= holder_first) & (owners[b] < holder_first + slots)
            found = jnp.where(here, b, found)
            shift_of[b] = jnp.where(here, (n_bcol - s) % n_bcol, shift_of[b])
        block_for.append(found)
    source_of = []
    for slot in range(slots):
        found = none
        for s in range(n_bcol):
            found = jnp.where(slot_of[s] == slot, (n_bcol - s) % n_bcol, found)
        source_of.append(found)

    def all_pairs(send, recv, sems):
        copies = []
        for s in range(1, n_bcol):
            copy = pltpu.make_async_remote_copy(
                src_ref=send.at[s], dst_ref=recv.at[s], send_sem=sems.at[0, s], recv_sem=sems.at[1, s],
                device_id=device(0, s), device_id_type=MESH,
            )
            copy.start()
            copies.append(copy)
        return copies

    load_eta.wait()
    for s in range(n_bcol):
        slot = jnp.maximum(slot_of[s], 0)
        into = eta_recv if s == 0 else eta_send
        into[s] = eta_v[slot]

    pl.semaphore_wait(barrier, len(partners))
    eta_copies = all_pairs(eta_send, eta_recv, eta_sem)

    for copy in load_masks:
        copy.wait()

    def depth_body(i):
        at = rows_at(i * CHUNK)
        to = rows_at(i * CHUNK + PAD)
        for t in range(tiles):
            n = mask_v[t, at, :] * level_v[t, at, :]
            wet_levels[t, at, :] = n
            nf = n.astype(jnp.float32)
            depth_e[0, t, to, :] = nf * (nf + 1.0) * (1.0 / (2 * level_count))

    grouped(0, chunks, 4, depth_body)

    def pack(field_ref, count, packed_ref, back_ref):
        def pack_body(i):
            at = rows_at(i * CHUNK + PAD)
            value = jnp.zeros((CHUNK, LANES), jnp.float32)
            for f in range(count):
                low = EAST_ROW + CHUNK * f
                west = field_ref[f, 0, at, :]
                east = pltpu.roll(field_ref[f, tiles - 1, at, :], (low + CHUNK) % LANES, 1)
                if f > 0:
                    west = pltpu.roll(west, CHUNK * f, 1)
                value = jnp.where((lanes >= CHUNK * f) & (lanes < CHUNK * (f + 1)), west, value)
                value = jnp.where((lanes >= low) & (lanes < low + CHUNK), east, value)
            back_ref[rows_at(i * CHUNK), :] = value

        grouped(0, chunks, 16, pack_body)
        packed_ref[...] = jnp.transpose(back_ref[...])

    def exchange(field_ref, count, packed_ref, halo_ref, corner_ref, sems):
        height = CHUNK * count
        top, bottom = pl.ds(first, CHUNK), pl.ds(last - CHUNK, CHUNK)
        pairs = (
            (field_ref.at[:, 0:tiles, top, :], field_ref.at[:, 0:tiles, pl.ds(last, CHUNK), :]),
            (field_ref.at[:, 0:tiles, bottom, :], field_ref.at[:, 0:tiles, pl.ds(first - CHUNK, CHUNK), :]),
            (packed_ref.at[0:height, :], halo_ref.at[0:height, :]),
            (packed_ref.at[EAST_ROW : EAST_ROW + height, :], halo_ref.at[EAST_ROW : EAST_ROW + height, :]),
            (field_ref.at[:, 0, top, :], corner_ref.at[0]),
            (field_ref.at[:, tiles - 1, top, :], corner_ref.at[1]),
            (field_ref.at[:, 0, bottom, :], corner_ref.at[2]),
            (field_ref.at[:, tiles - 1, bottom, :], corner_ref.at[3]),
        )
        copies = []
        for d in (2, 3, 0, 1, 4, 5, 6, 7):
            src, dst = pairs[d]
            copy = pltpu.make_async_remote_copy(
                src_ref=src, dst_ref=dst, send_sem=sems.at[0, d], recv_sem=sems.at[1, d],
                device_id=device(*DIRECTIONS[d]), device_id_type=MESH,
            )
            copy.start()
            copies.append(copy)
        return copies

    def arrived(copies, field_ref, count, halo_ref, corner_ref, back_ref):
        for copy in copies:
            copy.wait_recv()
        has_n, has_s, has_w, has_e = r > 0, r < n_brow - 1, c > 0, c < n_bcol - 1
        height = CHUNK * count
        spare = jnp.zeros((EAST_ROW - height, rows), jnp.float32)
        halo = jnp.concatenate(
            [halo_ref[0:height, :], spare, halo_ref[EAST_ROW : EAST_ROW + height, :], spare], axis=0
        )
        back_ref[...] = jnp.transpose(halo)
        right = (lanes < CHUNK) & has_e
        left = (lanes >= LANES - CHUNK) & has_w

        def sides(east, west):
            return jnp.where(right, east, jnp.where(left, west, 0.0))

        def side_body(i):
            value = back_ref[rows_at(i * CHUNK), :]
            for f in range(count):
                east = value if f == 0 else pltpu.roll(value, LANES - CHUNK * f, 1)
                west = pltpu.roll(value, (2 * LANES - CHUNK - EAST_ROW - CHUNK * f) % LANES, 1)
                field_ref[f, tiles, rows_at(i * CHUNK + PAD), :] = sides(east, west)

        grouped(0, chunks, 16, side_body)
        north, south = pl.ds(first - CHUNK, CHUNK), pl.ds(last, CHUNK)
        for f in range(count):
            for t in range(tiles):
                field_ref[f, t, north, :] = jnp.where(has_n, field_ref[f, t, north, :], 0.0)
                field_ref[f, t, south, :] = jnp.where(has_s, field_ref[f, t, south, :], 0.0)
            field_ref[f, tiles, south, :] = jnp.where(has_s, sides(corner_ref[0, f], corner_ref[1, f]), 0.0)
            field_ref[f, tiles, north, :] = jnp.where(has_n, sides(corner_ref[2, f], corner_ref[3, f]), 0.0)

    pack(depth_e, 1, d_pack, col_back)
    d_copies = exchange(depth_e, 1, d_pack, d_halo, d_corner, d_sem)

    for g in range(groups):
        for copy in vel_loads[g]:
            copy.wait()

        def wet_body(i, g=g):
            at = rows_at(i * CHUNK + CHUNK)
            for t in range(tiles):
                n = wet_levels[t, rows_at(i * CHUNK), :]
                for k in range(g * per_group, (g + 1) * per_group):
                    wet = n > k
                    for f in range(2):
                        vel[k, f, t, at, :] = jnp.where(wet, vel[k, f, t, at, :], 0.0)

        grouped(0, chunks, 2, wet_body)

    def edge_body(i):
        at = rows_at(i * CHUNK + CHUNK)
        low = jnp.zeros((CHUNK, LANES), jnp.float32)
        high = low
        for k in range(level_count):
            for f in range(2):
                j = 2 * k + f
                west = vel[k, f, 0, at, :]
                if j > 0:
                    west = pltpu.roll(west, j, 1)
                east = pltpu.roll(vel[k, f, tiles - 1, at, :], EAST_ROW + j + 1, 1)
                low = jnp.where(lanes == j, west, low)
                high = jnp.where(lanes == EAST_ROW + j, east, high)
        col_back[rows_at(i * CHUNK), :] = jnp.where(lanes < EAST_ROW, low, high)

    grouped(0, chunks, 8, edge_body)
    col_send[...] = jnp.transpose(col_back[...])
    for k in range(level_count):
        for f in range(2):
            j = 2 * k + f
            for t in range(tiles):
                row_send[0, t, j : j + 1, :] = vel[k, f, t, CHUNK : CHUNK + 1, :]
                row_send[1, t, j : j + 1, :] = vel[k, f, t, CHUNK + rows - 1 : CHUNK + rows, :]
    count = 2 * level_count
    east_rows = slice(EAST_ROW, EAST_ROW + count)
    r1_pairs = (
        (row_send.at[0], row_recv.at[1]),
        (row_send.at[1], row_recv.at[0]),
        (col_send.at[0:count, :], col_recv.at[0:count, :]),
        (col_send.at[east_rows, :], col_recv.at[east_rows, :]),
    )
    r1_copies = []
    for d in (2, 3, 0, 1):
        src, dst = r1_pairs[d]
        copy = pltpu.make_async_remote_copy(
            src_ref=src, dst_ref=dst, send_sem=r1_sem.at[0, d], recv_sem=r1_sem.at[1, d],
            device_id=device(*DIRECTIONS[d]), device_id_type=MESH,
        )
        copy.start()
        r1_copies.append(copy)

    arrived(d_copies, depth_e, 1, d_halo, d_corner, col_back)

    def weight_body(i):
        start = i * CHUNK + CHUNK
        at = rows_at(start)
        dc = [depth_e[0, t, at, :] for t in range(ext)]
        dn = [depth_e[0, t, pl.ds(start - 1, CHUNK), :] for t in range(ext)]
        ds = [depth_e[0, t, pl.ds(start + 1, CHUNK), :] for t in range(ext)]
        de, dw = from_east(dc, lanes), from_west(dc, lanes)
        span = range(ext)
        north = [jnp.minimum(dc[t], dn[t]) for t in span]
        south = [jnp.minimum(dc[t], ds[t]) for t in span]
        east = [
            [jnp.minimum(dc[t], de[t]) for t in span],
            [0.5 * jnp.minimum(dn[t], de[t]) for t in span],
            [0.5 * jnp.minimum(ds[t], de[t]) for t in span],
        ]
        west = [
            [jnp.minimum(dc[t], dw[t]) for t in span],
            [0.5 * jnp.minimum(dn[t], dw[t]) for t in span],
            [0.5 * jnp.minimum(ds[t], dw[t]) for t in span],
        ]
        sum_w = from_west([east[0][t] + east[1][t] + east[2][t] for t in span], lanes)
        sum_e = from_east([west[0][t] + west[1][t] + west[2][t] for t in span], lanes)
        inv = [1.0 / (SURFACE_TERM + north[t] + south[t] + sum_w[t] + sum_e[t]) for t in span]
        inv_e, inv_w = from_east(inv, lanes), from_west(inv, lanes)
        for t in span:
            inv_c[t, at, :] = inv[t]
            weights[0, t, at, :] = north[t] * inv[t]
            weights[1, t, at, :] = south[t] * inv[t]
            for m in range(3):
                weights[2 + m, t, at, :] = east[m][t] * inv_e[t]
                weights[5 + m, t, at, :] = west[m][t] * inv_w[t]

    with_rim(chunks, 8, weight_body)

    for copy in load_wind:
        copy.wait()
    for copy in r1_copies:
        copy.wait_recv()
    has_n, has_s = r > 0, r < n_brow - 1
    has_w, has_e = c > 0, c < n_bcol - 1
    for k in range(level_count):
        for f in range(2):
            j = 2 * k + f
            for t in range(tiles):
                vel[k, f, t, CHUNK - 1 : CHUNK, :] = jnp.where(has_n, row_recv[0, t, j : j + 1, :], 0.0)
                vel[k, f, t, CHUNK + rows : CHUNK + rows + 1, :] = jnp.where(
                    has_s, row_recv[1, t, j : j + 1, :], 0.0
                )
    spare = jnp.zeros((EAST_ROW - count, rows), jnp.float32)
    halo = jnp.concatenate(
        [
            jnp.where(has_e, col_recv[0:count, :], 0.0),
            spare,
            jnp.where(has_w, col_recv[east_rows, :], 0.0),
            spare,
        ],
        axis=0,
    )
    col_back[...] = jnp.transpose(halo)

    total_rows = rows * n_brow

    def momentum_body(i):
        here = rows_at(i * CHUNK)
        start = i * CHUNK + CHUNK
        at = rows_at(start)
        above, below = pl.ds(start - 1, CHUNK), pl.ds(start + 1, CHUNK)
        row_ids = (r * rows + i * CHUNK + lax.broadcasted_iota(jnp.int32, (CHUNK, LANES), 0)).astype(jnp.float32)
        coriolis = CORIOLIS * ((2.0 * row_ids + 1.0) * (1.0 / total_rows) - 1.0)
        sides = col_back[here, :]
        n = [wet_levels[t, here, :] for t in range(tiles)]
        sums = [[None] * tiles, [None] * tiles]
        for k in range(level_count):
            centre = [[vel[k, f, t, at, :] for t in range(tiles)] for f in range(2)]
            for f in range(2):
                j = 2 * k + f
                wide = pltpu.roll(sides, (EAST_ROW - j) % LANES, 1)
                far = pltpu.roll(sides, LANES - 1 - j, 1)
                west_rolled = [pltpu.roll(tile, 1, 1) for tile in centre[f]]
                east_rolled = [pltpu.roll(tile, LANES - 1, 1) for tile in centre[f]]
                for t in range(tiles):
                    west = jnp.where(lanes == 0, west_rolled[t - 1] if t > 0 else wide, west_rolled[t])
                    east = jnp.where(
                        lanes == LANES - 1, east_rolled[t + 1] if t < tiles - 1 else far, east_rolled[t]
                    )
                    spread = (west + east) + (vel[k, f, t, above, :] + vel[k, f, t, below, :]) + centre[f][t]
                    turn = coriolis * centre[1 - f][t]
                    value = VISCOSITY * spread + (turn if f == 0 else -turn)
                    if k == 0:
                        value = value + wind[f, t, here, :]
                    value = jnp.where(n[t] > k, value, 0.0)
                    star[f][k, here, columns(t)] = value
                    part = value * ((1.0 + k) / level_count)
                    sums[f][t] = part if k == 0 else sums[f][t] + part
        to = rows_at(i * CHUNK + PAD)
        for f in range(2):
            for t in range(tiles):
                trans_e[f, t, to, :] = sums[f][t]

    grouped(0, chunks // 2, 2, momentum_body)

    for copy in eta_copies:
        copy.wait_recv()
    for b in range(blocks):
        a, t = b // tiles, b % tiles
        guess = eta_recv[shift_of[b]]
        at = pl.ds(first + a * block_x, block_x)
        xa[0, t, at, :] = jnp.where(depth_e[0, t, at, :] > 0.0, guess, 0.0)
    pack(xa, 1, x_pack, x_back)
    x_copies = exchange(xa, 1, x_pack, x_halo, x_corner, x_sem)

    grouped(chunks // 2, chunks // 2, 2, momentum_body)
    pack(trans_e, 2, t_pack, col_back)
    t_copies = exchange(trans_e, 2, t_pack, t_halo, t_corner, t_sem)

    def stencil(old, start):
        at = rows_at(start)
        span = range(ext)
        xc = [old[t, at, :] for t in span]
        xn = [old[t, pl.ds(start - 1, CHUNK), :] for t in span]
        xs = [old[t, pl.ds(start + 1, CHUNK), :] for t in span]

        def side(base):
            return [
                weights[base, t, at, :] * xc[t]
                + weights[base + 1, t, at, :] * xn[t]
                + weights[base + 2, t, at, :] * xs[t]
                for t in span
            ]

        west, east = from_west(side(2), lanes), from_east(side(5), lanes)
        near = [weights[0, t, at, :] * xn[t] + weights[1, t, at, :] * xs[t] for t in span]
        return xc, [(near[t] - xc[t]) + (west[t] + east[t]) for t in span]

    fields = (xa.at[0], xb)
    factors = chebyshev_factors()
    arrived(x_copies, xa, 1, x_halo, x_corner, x_back)

    def first_body(i):
        start = i * CHUNK + CHUNK
        _, applied = stencil(fields[0], start)
        for t in range(ext):
            step_e[1, t, rows_at(start), :] = applied[t]

    with_rim(chunks, 16, first_body)
    arrived(t_copies, trans_e, 2, t_halo, t_corner, col_back)

    def forcing_body(i):
        start = i * CHUNK + CHUNK
        at = rows_at(start)
        above, below = pl.ds(start - 1, CHUNK), pl.ds(start + 1, CHUNK)
        second = [trans_e[1, t, at, :] for t in range(ext)]
        east, west = from_east(second, lanes), from_west(second, lanes)
        for t in range(ext):
            spread = trans_e[0, t, below, :] - trans_e[0, t, above, :] + east[t] - west[t]
            value = jnp.where(depth_e[0, t, at, :] > 0.0, -0.5 * spread, 0.0) * inv_c[t, at, :]
            forcing_e[t, at, :] = value
            step = factors[0][0] * (value + step_e[1, t, at, :])
            step_e[0, t, at, :] = step
            xb[t, at, :] = xa[0, t, at, :] + step

    with_rim(chunks, 16, forcing_body)
    for sweep in range(1, ITERS):
        omega, beta = factors[sweep]
        old, new = fields[sweep % 2], fields[(sweep + 1) % 2]
        if sweep == 1:
            for copy in x_copies:
                copy.wait_send()

        def sweep_body(i, old=old, new=new, sweep=sweep, omega=omega, beta=beta):
            start = i * CHUNK + CHUNK
            at = rows_at(start)
            xc, applied = stencil(old, start)
            for t in range(ext):
                step = omega * (forcing_e[t, at, :] + applied[t]) + beta * step_e[(sweep + 1) % 2, t, at, :]
                if sweep < ITERS - 1:
                    step_e[sweep % 2, t, at, :] = step
                new[t, at, :] = xc[t] + step

        with_rim(chunks, 16, sweep_body)
    result = fields[ITERS % 2]

    for b in range(blocks):
        height_b[b] = result[b % tiles, pl.ds(first + (b // tiles) * block_x, block_x), :]
    for s in range(n_bcol):
        into = height_recv if s == 0 else height_send
        into[s] = height_b[block_for[s]]
    height_copies = all_pairs(height_send, height_recv, height_sem)

    def final_body(i):
        here = rows_at(i * CHUNK)
        start = i * CHUNK + PAD
        at = rows_at(start)
        span = range(ext)
        xc = [result[t, at, :] for t in span]
        east, west = from_east(xc, lanes), from_west(xc, lanes)
        for t in range(tiles):
            n = wet_levels[t, here, :]
            north, south = result[t, pl.ds(start - 1, CHUNK), :], result[t, pl.ds(start + 1, CHUNK), :]
            slopes = (0.5 * (south - north), 0.5 * (east[t] - west[t]))
            for k in range(level_count):
                wet = n > k
                for f in range(2):
                    star[f][k, here, columns(t)] = star[f][k, here, columns(t)] - jnp.where(wet, slopes[f], 0.0)

    grouped(0, chunks, 2, final_body)
    for copy in height_copies:
        copy.wait_recv()
    for slot in range(slots):
        source = source_of[slot]
        held = jnp.broadcast_to(source, (block_x, LANES)) >= 0
        height_out[slot] = jnp.where(held, height_recv[jnp.maximum(source, 0)], 0.0)
    for copies in (d_copies, r1_copies, eta_copies, t_copies, height_copies):
        for copy in copies:
            copy.wait_send()


def drain(u_in, v_in, height_in, u_out, v_out, height_out, sems):
    copies = [pltpu.make_async_copy(height_in, height_out, sems.at[0])]
    for source, target in ((u_in, u_out), (v_in, v_out)):
        for k in range(source.shape[0]):
            copies.append(pltpu.make_async_copy(source.at[k], target.at[k], sems.at[len(copies)]))
    for copy in copies:
        copy.start()
    for copy in copies:
        copy.wait()


def solution(mesh):
    n_brow, n_bcol = mesh.shape["brow"], mesh.shape["bcol"]

    def local(uvel, vvel, wind_stress, ocean_mask, depth_level, baro_owner, eta_guess):
        level_count, rows, width = uvel.shape
        slots, block_x, block_y = eta_guess.shape
        tiles = width // LANES
        ext = tiles + 1
        span = rows + 2 * PAD
        sizes = (n_brow, n_bcol, level_count, rows, tiles, block_x, slots)
        f32 = jnp.float32
        vmem = pltpu.VMEM
        any_spec = pl.BlockSpec(memory_space=pltpu.HBM)
        vmem_spec = pl.BlockSpec(memory_space=vmem)

        def halo_buffers(count):
            return [
                vmem((LANES, rows), f32),
                vmem((LANES, rows), f32),
                vmem((4, count, CHUNK, LANES), f32),
            ]

        scratch = [
            vmem((level_count, 2, tiles, rows + 2 * CHUNK, LANES), f32),
            vmem((2, tiles, rows, LANES), f32),
            vmem((tiles, rows, LANES), jnp.int32),
            vmem((tiles, rows, LANES), jnp.int32),
            vmem((slots, block_x, LANES), f32),
            vmem((tiles, rows, LANES), jnp.int32),
            vmem((1, ext, span, LANES), f32),
            vmem((2, ext, span, LANES), f32),
            vmem((1, ext, span, LANES), f32),
            vmem((ext, span, LANES), f32),
            vmem((ext, span, LANES), f32),
            vmem((2, ext, span, LANES), f32),
            vmem((ext, span, LANES), f32),
            vmem((8, ext, span, LANES), f32),
            vmem((n_bcol, block_x, LANES), f32),
            vmem((n_bcol, block_x, LANES), f32),
            vmem((n_bcol, block_x, LANES), f32),
            vmem((n_bcol, block_x, LANES), f32),
            vmem((2, tiles, 2 * level_count, LANES), f32),
            vmem((2, tiles, 2 * level_count, LANES), f32),
            vmem((LANES, rows), f32),
            vmem((LANES, rows), f32),
            vmem((rows, LANES), f32),
            vmem((rows, LANES), f32),
            *halo_buffers(1),
            *halo_buffers(2),
            *halo_buffers(1),
            vmem(((rows // block_x) * tiles, block_x, LANES), f32),
            pltpu.SemaphoreType.DMA((1 + 3 * tiles,)),
            pltpu.SemaphoreType.DMA((2, tiles, 2)),
            pltpu.SemaphoreType.DMA((2, 4)),
            pltpu.SemaphoreType.DMA((2, 8)),
            pltpu.SemaphoreType.DMA((2, 8)),
            pltpu.SemaphoreType.DMA((2, 8)),
            pltpu.SemaphoreType.DMA((2, n_bcol)),
            pltpu.SemaphoreType.DMA((2, n_bcol)),
        ]
        fields = (uvel, vvel, wind_stress, ocean_mask, depth_level, eta_guess)
        results = pl.pallas_call(
            functools.partial(kernel, sizes),
            out_shape=(
                vmem(uvel.shape, f32),
                vmem(vvel.shape, f32),
                vmem(eta_guess.shape, f32),
            ),
            in_specs=[pl.BlockSpec(memory_space=pltpu.SMEM)] + [any_spec] * 6,
            out_specs=(vmem_spec,) * 3,
            scratch_shapes=scratch,
            compiler_params=pltpu.CompilerParams(
                collective_id=0, has_side_effects=True, vmem_limit_bytes=50 * 1024 * 1024
            ),
            cost_estimate=pl.CostEstimate(flops=60_000_000, bytes_accessed=20_000_000, transcendentals=0),
        )(baro_owner, *[pltpu.with_memory_space_constraint(x, pltpu.HBM) for x in fields])
        return pl.pallas_call(
            drain,
            out_shape=[jax.ShapeDtypeStruct(x.shape, f32) for x in results],
            in_specs=[vmem_spec] * 3,
            out_specs=[any_spec] * 3,
            scratch_shapes=[pltpu.SemaphoreType.DMA((2 * level_count + 1,))],
            compiler_params=pltpu.CompilerParams(vmem_limit_bytes=1024 * 1024),
            cost_estimate=pl.CostEstimate(flops=0, bytes_accessed=8_800_000, transcendentals=0),
        )(*[pltpu.with_memory_space_constraint(x, vmem) for x in results])

    in_specs = (
        P(None, "brow", "bcol"),
        P(None, "brow", "bcol"),
        P(None, "brow", "bcol"),
        P("brow", "bcol"),
        P("brow", "bcol"),
        P(),
        P(("brow", "bcol"), None, None),
    )
    out_specs = (P(None, "brow", "bcol"), P(None, "brow", "bcol"), P(("brow", "bcol"), None, None))
    return jax.shard_map(local, mesh=mesh, in_specs=in_specs, out_specs=out_specs, check_vma=False)
```

```python
import functools

import jax
import jax.numpy as jnp
from jax import lax
from jax.experimental import pallas as pl
from jax.experimental.pallas import tpu as pltpu
from jax.sharding import PartitionSpec as P

ITERS = 4
VISCOSITY = 0.2
CORIOLIS = 0.5
SURFACE_TERM = 0.25
LOWER_BOUND = 0.05
UPPER_BOUND = 2.0

LANES = 128
CHUNK = 8
PAD = 16
EAST_ROW = 64
MESH = pl.DeviceIdType.MESH
DIRECTIONS = ((-1, 0), (1, 0), (0, -1), (0, 1), (-1, -1), (-1, 1), (1, -1), (1, 1))


def chebyshev_factors():
    alpha = 2.0 / (UPPER_BOUND - LOWER_BOUND)
    gamma = (UPPER_BOUND + LOWER_BOUND) / 2.0
    omega = 2.0 / gamma
    factors = [(1.0 / gamma, 0.0)]
    for _ in range(ITERS - 1):
        omega = 1.0 / (gamma - omega / (4.0 * alpha * alpha))
        factors.append((omega, gamma * omega - 1.0))
    return factors


def lane_ids():
    return lax.broadcasted_iota(jnp.int32, (CHUNK, LANES), 1)


def from_west(tiles, lanes):
    rolled = [pltpu.roll(tile, 1, 1) for tile in tiles]
    return [jnp.where(lanes == 0, rolled[t - 1], rolled[t]) for t in range(len(tiles))]


def from_east(tiles, lanes):
    rolled = [pltpu.roll(tile, LANES - 1, 1) for tile in tiles]
    count = len(tiles)
    return [jnp.where(lanes == LANES - 1, rolled[(t + 1) % count], rolled[t]) for t in range(count)]


def grouped(first, count, group, body):
    def step(i, carry):
        for m in range(group):
            body(first + i * group + m)
        return carry

    lax.fori_loop(0, count // group, step, 0)


def with_rim(chunks, group, body):
    grouped(1, chunks, group, body)
    for edge in (0, chunks + 1):
        body(jnp.int32(edge))


def rows_at(start):
    return pl.ds(pl.multiple_of(start, CHUNK), CHUNK)


def kernel(
    sizes,
    owner_ref, u_hbm, v_hbm, wind_hbm, mask_hbm, level_hbm, eta_hbm,
    u_out, v_out, height_out,
    vel, wind, mask_v, level_v, eta_v, wet_levels,
    depth_e, trans_e, xb, forcing_e, step_e, inv_c, weights,
    eta_send, eta_recv, height_send, height_recv,
    row_send, row_recv, col_send, col_recv, col_back,
    d_pack, d_halo, d_corner, t_pack, t_halo, t_corner,
    height_b,
    load_sem, vel_sem,
    r1_sem, d_sem, t_sem, eta_sem, height_sem,
):
    n_brow, n_bcol, level_count, rows, tiles, block_x, slots = sizes
    blocks_x = rows // block_x
    blocks = blocks_x * tiles
    chunks = rows // CHUNK
    ext = tiles + 1
    first, last = PAD, PAD + rows
    star = (u_out, v_out)
    xa = trans_e.at[2]
    r = lax.axis_index("brow")
    c = lax.axis_index("bcol")
    lanes = lane_ids()

    def device(dr, dc):
        return (lax.rem(r + dr + n_brow, n_brow), lax.rem(c + dc + n_bcol, n_bcol))

    loads = []

    def load(src, dst):
        copy = pltpu.make_async_copy(src, dst, load_sem.at[len(loads)])
        copy.start()
        loads.append(copy)
        return copy

    def columns(t):
        return slice(t * LANES, (t + 1) * LANES)

    load_eta = load(eta_hbm, eta_v)
    load_masks = [load(mask_hbm, mask_v), load(level_hbm, level_v)]
    groups = 2
    per_group = level_count // groups
    vel_loads = []
    for g in range(groups):
        these = []
        for t in range(tiles):
            for f, source in enumerate((u_hbm, v_hbm)):
                copy = pltpu.make_async_copy(
                    source.at[g * per_group : (g + 1) * per_group, :, columns(t)],
                    vel.at[g * per_group : (g + 1) * per_group, f, t, CHUNK : CHUNK + rows, :],
                    vel_sem.at[g, t, f],
                )
                copy.start()
                these.append(copy)
        vel_loads.append(these)
    load_wind = load(wind_hbm, wind)

    barrier = pltpu.get_barrier_semaphore()
    partners = [(0, s) for s in range(1, n_bcol)]
    partners += [(dr, dc) for dr, dc in DIRECTIONS if dr != 0]
    for dr, dc in partners:
        pl.semaphore_signal(barrier, inc=1, device_id=device(dr, dc), device_id_type=MESH)

    zero = jnp.zeros((CHUNK, LANES), jnp.float32)
    for t in range(ext):
        for ref in (depth_e.at[0], trans_e.at[0], trans_e.at[1], xa, xb):
            ref[t, 0:CHUNK, :] = zero
            ref[t, last + CHUNK : last + 2 * CHUNK, :] = zero

    for t in range(tiles):
        for k in range(level_count):
            for f in range(2):
                vel[k, f, t, 0:CHUNK, :] = zero
                vel[k, f, t, CHUNK + rows : 2 * CHUNK + rows, :] = zero

    device_first = (r * n_bcol + c) * slots
    none = jnp.int32(-1)
    slot_of = []
    for s in range(n_bcol):
        q = lax.rem(c + s, n_bcol)
        found = none
        for b in range(blocks):
            local = owner_ref[r * blocks_x + b // tiles, q * tiles + b % tiles] - device_first
            found = jnp.where((local >= 0) & (local < slots), local, found)
        slot_of.append(found)
    owners = [owner_ref[r * blocks_x + b // tiles, c * tiles + b % tiles] for b in range(blocks)]
    block_for, shift_of = [], [jnp.int32(0)] * blocks
    for s in range(n_bcol):
        holder_first = (r * n_bcol + lax.rem(c + s, n_bcol)) * slots
        found = jnp.int32(0)
        for b in range(blocks):
            here = (owners[b] >= holder_first) & (owners[b] < holder_first + slots)
            found = jnp.where(here, b, found)
            shift_of[b] = jnp.where(here, (n_bcol - s) % n_bcol, shift_of[b])
        block_for.append(found)
    source_of = []
    for slot in range(slots):
        found = none
        for s in range(n_bcol):
            found = jnp.where(slot_of[s] == slot, (n_bcol - s) % n_bcol, found)
        source_of.append(found)

    def all_pairs(send, recv, sems):
        copies = []
        for s in range(1, n_bcol):
            copy = pltpu.make_async_remote_copy(
                src_ref=send.at[s], dst_ref=recv.at[s], send_sem=sems.at[0, s], recv_sem=sems.at[1, s],
                device_id=device(0, s), device_id_type=MESH,
            )
            copy.start()
            copies.append(copy)
        return copies

    load_eta.wait()
    for s in range(n_bcol):
        slot = jnp.maximum(slot_of[s], 0)
        into = eta_recv if s == 0 else eta_send
        into[s] = eta_v[slot]

    pl.semaphore_wait(barrier, len(partners))
    eta_copies = all_pairs(eta_send, eta_recv, eta_sem)

    for copy in load_masks:
        copy.wait()

    def depth_body(i):
        at = rows_at(i * CHUNK)
        to = rows_at(i * CHUNK + PAD)
        for t in range(tiles):
            n = mask_v[at, columns(t)] * level_v[at, columns(t)]
            wet_levels[t, at, :] = n
            nf = n.astype(jnp.float32)
            depth_e[0, t, to, :] = nf * (nf + 1.0) * (1.0 / (2 * level_count))

    grouped(0, chunks, 4, depth_body)

    def pack(field_ref, count, packed_ref, back_ref):
        def pack_body(i):
            at = rows_at(i * CHUNK + PAD)
            value = jnp.zeros((CHUNK, LANES), jnp.float32)
            for f in range(count):
                low = EAST_ROW + CHUNK * f
                west = field_ref[f, 0, at, :]
                east = pltpu.roll(field_ref[f, tiles - 1, at, :], (low + CHUNK) % LANES, 1)
                if f > 0:
                    west = pltpu.roll(west, CHUNK * f, 1)
                value = jnp.where((lanes >= CHUNK * f) & (lanes < CHUNK * (f + 1)), west, value)
                value = jnp.where((lanes >= low) & (lanes < low + CHUNK), east, value)
            back_ref[rows_at(i * CHUNK), :] = value

        grouped(0, chunks, 16, pack_body)
        packed_ref[...] = jnp.transpose(back_ref[...])

    def exchange(field_ref, count, packed_ref, halo_ref, corner_ref, sems):
        height = CHUNK * count
        top, bottom = pl.ds(first, CHUNK), pl.ds(last - CHUNK, CHUNK)
        pairs = (
            (field_ref.at[:, 0:tiles, top, :], field_ref.at[:, 0:tiles, pl.ds(last, CHUNK), :]),
            (field_ref.at[:, 0:tiles, bottom, :], field_ref.at[:, 0:tiles, pl.ds(first - CHUNK, CHUNK), :]),
            (packed_ref.at[0:height, :], halo_ref.at[0:height, :]),
            (packed_ref.at[EAST_ROW : EAST_ROW + height, :], halo_ref.at[EAST_ROW : EAST_ROW + height, :]),
            (field_ref.at[:, 0, top, :], corner_ref.at[0]),
            (field_ref.at[:, tiles - 1, top, :], corner_ref.at[1]),
            (field_ref.at[:, 0, bottom, :], corner_ref.at[2]),
            (field_ref.at[:, tiles - 1, bottom, :], corner_ref.at[3]),
        )
        copies = []
        for d in (2, 3, 0, 1, 4, 5, 6, 7):
            src, dst = pairs[d]
            copy = pltpu.make_async_remote_copy(
                src_ref=src, dst_ref=dst, send_sem=sems.at[0, d], recv_sem=sems.at[1, d],
                device_id=device(*DIRECTIONS[d]), device_id_type=MESH,
            )
            copy.start()
            copies.append(copy)
        return copies

    def arrived(copies, field_ref, count, halo_ref, corner_ref, back_ref):
        for copy in copies:
            copy.wait_recv()
        has_n, has_s, has_w, has_e = r > 0, r < n_brow - 1, c > 0, c < n_bcol - 1
        height = CHUNK * count
        spare = jnp.zeros((EAST_ROW - height, rows), jnp.float32)
        halo = jnp.concatenate(
            [halo_ref[0:height, :], spare, halo_ref[EAST_ROW : EAST_ROW + height, :], spare], axis=0
        )
        back_ref[...] = jnp.transpose(halo)
        right = (lanes < CHUNK) & has_e
        left = (lanes >= LANES - CHUNK) & has_w

        def sides(east, west):
            return jnp.where(right, east, jnp.where(left, west, 0.0))

        def side_body(i):
            value = back_ref[rows_at(i * CHUNK), :]
            for f in range(count):
                east = value if f == 0 else pltpu.roll(value, LANES - CHUNK * f, 1)
                west = pltpu.roll(value, (2 * LANES - CHUNK - EAST_ROW - CHUNK * f) % LANES, 1)
                field_ref[f, tiles, rows_at(i * CHUNK + PAD), :] = sides(east, west)

        grouped(0, chunks, 16, side_body)
        north, south = pl.ds(first - CHUNK, CHUNK), pl.ds(last, CHUNK)
        for f in range(count):
            for t in range(tiles):
                field_ref[f, t, north, :] = jnp.where(has_n, field_ref[f, t, north, :], 0.0)
                field_ref[f, t, south, :] = jnp.where(has_s, field_ref[f, t, south, :], 0.0)
            field_ref[f, tiles, south, :] = jnp.where(has_s, sides(corner_ref[0, f], corner_ref[1, f]), 0.0)
            field_ref[f, tiles, north, :] = jnp.where(has_n, sides(corner_ref[2, f], corner_ref[3, f]), 0.0)

    pack(depth_e, 1, d_pack, col_back)
    d_copies = exchange(depth_e, 1, d_pack, d_halo, d_corner, d_sem)

    for g in range(groups):
        for copy in vel_loads[g]:
            copy.wait()

        def wet_body(i, g=g):
            at = rows_at(i * CHUNK + CHUNK)
            for t in range(tiles):
                n = wet_levels[t, rows_at(i * CHUNK), :]
                for k in range(g * per_group, (g + 1) * per_group):
                    wet = n > k
                    for f in range(2):
                        vel[k, f, t, at, :] = jnp.where(wet, VISCOSITY * vel[k, f, t, at, :], 0.0)

        grouped(0, chunks, 2, wet_body)

    def edge_body(i):
        at = rows_at(i * CHUNK + CHUNK)
        low = jnp.zeros((CHUNK, LANES), jnp.float32)
        high = low
        for k in range(level_count):
            for f in range(2):
                j = 2 * k + f
                west = vel[k, f, 0, at, :]
                if j > 0:
                    west = pltpu.roll(west, j, 1)
                east = pltpu.roll(vel[k, f, tiles - 1, at, :], EAST_ROW + j + 1, 1)
                low = jnp.where(lanes == j, west, low)
                high = jnp.where(lanes == EAST_ROW + j, east, high)
        col_back[rows_at(i * CHUNK), :] = jnp.where(lanes < EAST_ROW, low, high)

    grouped(0, chunks, 8, edge_body)
    col_send[...] = jnp.transpose(col_back[...])
    for k in range(level_count):
        for f in range(2):
            j = 2 * k + f
            for t in range(tiles):
                row_send[0, t, j : j + 1, :] = vel[k, f, t, CHUNK : CHUNK + 1, :]
                row_send[1, t, j : j + 1, :] = vel[k, f, t, CHUNK + rows - 1 : CHUNK + rows, :]
    count = 2 * level_count
    east_rows = slice(EAST_ROW, EAST_ROW + count)
    r1_pairs = (
        (row_send.at[0], row_recv.at[1]),
        (row_send.at[1], row_recv.at[0]),
        (col_send.at[0:count, :], col_recv.at[0:count, :]),
        (col_send.at[east_rows, :], col_recv.at[east_rows, :]),
    )
    r1_copies = []
    for d in (2, 3, 0, 1):
        src, dst = r1_pairs[d]
        copy = pltpu.make_async_remote_copy(
            src_ref=src, dst_ref=dst, send_sem=r1_sem.at[0, d], recv_sem=r1_sem.at[1, d],
            device_id=device(*DIRECTIONS[d]), device_id_type=MESH,
        )
        copy.start()
        r1_copies.append(copy)

    load_wind.wait()
    total_rows = rows * n_brow

    def momentum_body(i):
        here = rows_at(i * CHUNK)
        start = i * CHUNK + CHUNK
        at = rows_at(start)
        above, below = pl.ds(start - 1, CHUNK), pl.ds(start + 1, CHUNK)
        row_ids = (r * rows + i * CHUNK + lax.broadcasted_iota(jnp.int32, (CHUNK, LANES), 0)).astype(jnp.float32)
        coriolis = (CORIOLIS / VISCOSITY) * ((2.0 * row_ids + 1.0) * (1.0 / total_rows) - 1.0)
        n = [wet_levels[t, here, :] for t in range(tiles)]
        sums = [[None] * tiles, [None] * tiles]
        for k in range(level_count):
            centre = [[vel[k, f, t, at, :] for t in range(tiles)] for f in range(2)]
            for f in range(2):
                west_rolled = [pltpu.roll(tile, 1, 1) for tile in centre[f]]
                east_rolled = [pltpu.roll(tile, LANES - 1, 1) for tile in centre[f]]
                for t in range(tiles):
                    west = jnp.where(lanes == 0, west_rolled[t - 1] if t > 0 else 0.0, west_rolled[t])
                    east = jnp.where(
                        lanes == LANES - 1, east_rolled[t + 1] if t < tiles - 1 else 0.0, east_rolled[t]
                    )
                    spread = (west + east) + (vel[k, f, t, above, :] + vel[k, f, t, below, :]) + centre[f][t]
                    turn = coriolis * centre[1 - f][t]
                    value = spread + turn if f == 0 else spread - turn
                    if k == 0:
                        value = value + wind[f, here, columns(t)]
                    value = jnp.where(n[t] > k, value, 0.0)
                    star[f][k, here, columns(t)] = value
                    part = value * ((1.0 + k) / level_count)
                    sums[f][t] = part if k == 0 else sums[f][t] + part
        to = rows_at(i * CHUNK + PAD)
        for f in range(2):
            for t in range(tiles):
                trans_e[f, t, to, :] = sums[f][t]

    grouped(0, chunks, 2, momentum_body)

    for copy in r1_copies:
        copy.wait_recv()
    spare = jnp.zeros((EAST_ROW - count, rows), jnp.float32)
    col_back[...] = jnp.transpose(
        jnp.concatenate([col_recv[0:count, :], spare, col_recv[east_rows, :], spare], axis=0)
    )
    has_n, has_s, has_w, has_e = r > 0, r < n_brow - 1, c > 0, c < n_bcol - 1
    first_lane, last_lane = (lanes == 0) & has_w, (lanes == LANES - 1) & has_e

    def column_body(i):
        here = rows_at(i * CHUNK)
        to = rows_at(i * CHUNK + PAD)
        value = col_back[here, :]
        for t, edge in ((0, first_lane), (tiles - 1, last_lane)):
            n = jnp.where(edge, wet_levels[t, here, :], 0)
            sums = [trans_e[f, t, to, :] for f in range(2)]
            for k in range(level_count):
                for f in range(2):
                    j = 2 * k + f
                    turn = (EAST_ROW - j) % LANES if t == 0 else LANES - 1 - j
                    term = jnp.where(n > k, pltpu.roll(value, turn, 1), 0.0)
                    star[f][k, here, columns(t)] = star[f][k, here, columns(t)] + term
                    sums[f] = sums[f] + term * ((1.0 + k) / level_count)
            for f in range(2):
                trans_e[f, t, to, :] = sums[f]

    grouped(0, chunks, 4, column_body)
    sublanes = lax.broadcasted_iota(jnp.int32, (CHUNK, LANES), 0)
    for side, low, edge in ((0, 0, (sublanes == 0) & has_n), (1, rows - CHUNK, (sublanes == CHUNK - 1) & has_s)):
        here, to = slice(low, low + CHUNK), slice(low + PAD, low + PAD + CHUNK)
        for t in range(tiles):
            n = jnp.where(edge, wet_levels[t, here, :], 0)
            sums = [trans_e[f, t, to, :] for f in range(2)]
            for k in range(level_count):
                for f in range(2):
                    j = 2 * k + f
                    row = jnp.broadcast_to(row_recv[side, t, j : j + 1, :], (CHUNK, LANES))
                    term = jnp.where(n > k, row, 0.0)
                    star[f][k, here, columns(t)] = star[f][k, here, columns(t)] + term
                    sums[f] = sums[f] + term * ((1.0 + k) / level_count)
            for f in range(2):
                trans_e[f, t, to, :] = sums[f]

    for copy in eta_copies:
        copy.wait_recv()
    for b in range(blocks):
        a, t = b // tiles, b % tiles
        guess = eta_recv[shift_of[b]]
        at = pl.ds(first + a * block_x, block_x)
        xa[t, at, :] = jnp.where(depth_e[0, t, at, :] > 0.0, guess, 0.0)
    pack(trans_e, 3, t_pack, col_back)
    t_copies = exchange(trans_e, 3, t_pack, t_halo, t_corner, t_sem)

    arrived(d_copies, depth_e, 1, d_halo, d_corner, col_back)

    def weight_body(i):
        start = i * CHUNK + CHUNK
        at = rows_at(start)
        dc = [depth_e[0, t, at, :] for t in range(ext)]
        dn = [depth_e[0, t, pl.ds(start - 1, CHUNK), :] for t in range(ext)]
        ds = [depth_e[0, t, pl.ds(start + 1, CHUNK), :] for t in range(ext)]
        de, dw = from_east(dc, lanes), from_west(dc, lanes)
        span = range(ext)
        north = [jnp.minimum(dc[t], dn[t]) for t in span]
        south = [jnp.minimum(dc[t], ds[t]) for t in span]
        east = [
            [jnp.minimum(dc[t], de[t]) for t in span],
            [0.5 * jnp.minimum(dn[t], de[t]) for t in span],
            [0.5 * jnp.minimum(ds[t], de[t]) for t in span],
        ]
        west = [
            [jnp.minimum(dc[t], dw[t]) for t in span],
            [0.5 * jnp.minimum(dn[t], dw[t]) for t in span],
            [0.5 * jnp.minimum(ds[t], dw[t]) for t in span],
        ]
        sum_w = from_west([east[0][t] + east[1][t] + east[2][t] for t in span], lanes)
        sum_e = from_east([west[0][t] + west[1][t] + west[2][t] for t in span], lanes)
        inv = [1.0 / (SURFACE_TERM + north[t] + south[t] + sum_w[t] + sum_e[t]) for t in span]
        inv_e, inv_w = from_east(inv, lanes), from_west(inv, lanes)
        for t in span:
            inv_c[t, at, :] = inv[t]
            weights[0, t, at, :] = north[t] * inv[t]
            weights[1, t, at, :] = south[t] * inv[t]
            for m in range(3):
                weights[2 + m, t, at, :] = east[m][t] * inv_e[t]
                weights[5 + m, t, at, :] = west[m][t] * inv_w[t]

    with_rim(chunks, 8, weight_body)

    def stencil(old, start):
        at = rows_at(start)
        span = range(ext)
        xc = [old[t, at, :] for t in span]
        xn = [old[t, pl.ds(start - 1, CHUNK), :] for t in span]
        xs = [old[t, pl.ds(start + 1, CHUNK), :] for t in span]

        def side(base):
            return [
                weights[base, t, at, :] * xc[t]
                + weights[base + 1, t, at, :] * xn[t]
                + weights[base + 2, t, at, :] * xs[t]
                for t in span
            ]

        west, east = from_west(side(2), lanes), from_east(side(5), lanes)
        near = [weights[0, t, at, :] * xn[t] + weights[1, t, at, :] * xs[t] for t in span]
        return xc, [(near[t] - xc[t]) + (west[t] + east[t]) for t in span]

    fields = (xa, xb)
    factors = chebyshev_factors()
    arrived(t_copies, trans_e, 3, t_halo, t_corner, col_back)

    def forcing_body(i):
        start = i * CHUNK + CHUNK
        at = rows_at(start)
        above, below = pl.ds(start - 1, CHUNK), pl.ds(start + 1, CHUNK)
        second = [trans_e[1, t, at, :] for t in range(ext)]
        east, west = from_east(second, lanes), from_west(second, lanes)
        for t in range(ext):
            spread = trans_e[0, t, below, :] - trans_e[0, t, above, :] + east[t] - west[t]
            value = jnp.where(depth_e[0, t, at, :] > 0.0, -0.5 * spread, 0.0) * inv_c[t, at, :]
            forcing_e[t, at, :] = value

    with_rim(chunks, 16, forcing_body)
    for sweep in range(ITERS):
        omega, beta = factors[sweep]
        old, new = fields[sweep % 2], fields[(sweep + 1) % 2]
        if sweep == 1:
            for copy in t_copies:
                copy.wait_send()

        def sweep_body(i, old=old, new=new, sweep=sweep, omega=omega, beta=beta):
            start = i * CHUNK + CHUNK
            at = rows_at(start)
            xc, applied = stencil(old, start)
            for t in range(ext):
                step = omega * (forcing_e[t, at, :] + applied[t])
                if sweep > 0:
                    step = step + beta * step_e[(sweep + 1) % 2, t, at, :]
                if sweep < ITERS - 1:
                    step_e[sweep % 2, t, at, :] = step
                new[t, at, :] = xc[t] + step

        with_rim(chunks, 16, sweep_body)
    result = fields[ITERS % 2]

    for b in range(blocks):
        height_b[b] = result[b % tiles, pl.ds(first + (b // tiles) * block_x, block_x), :]
    for s in range(n_bcol):
        into = height_recv if s == 0 else height_send
        into[s] = height_b[block_for[s]]
    height_copies = all_pairs(height_send, height_recv, height_sem)

    def final_body(i):
        here = rows_at(i * CHUNK)
        start = i * CHUNK + PAD
        at = rows_at(start)
        span = range(ext)
        xc = [result[t, at, :] for t in span]
        east, west = from_east(xc, lanes), from_west(xc, lanes)
        for t in range(tiles):
            n = wet_levels[t, here, :]
            north, south = result[t, pl.ds(start - 1, CHUNK), :], result[t, pl.ds(start + 1, CHUNK), :]
            slopes = (0.5 * (south - north), 0.5 * (east[t] - west[t]))
            for k in range(level_count):
                wet = n > k
                for f in range(2):
                    star[f][k, here, columns(t)] = star[f][k, here, columns(t)] - jnp.where(wet, slopes[f], 0.0)

    grouped(0, chunks, 2, final_body)
    for copy in height_copies:
        copy.wait_recv()
    for slot in range(slots):
        source = source_of[slot]
        held = jnp.broadcast_to(source, (block_x, LANES)) >= 0
        height_out[slot] = jnp.where(held, height_recv[jnp.maximum(source, 0)], 0.0)
    for copies in (d_copies, r1_copies, eta_copies, height_copies):
        for copy in copies:
            copy.wait_send()


def drain(u_in, v_in, height_in, u_out, v_out, height_out, sems):
    copies = [pltpu.make_async_copy(height_in, height_out, sems.at[0])]
    for source, target in ((u_in, u_out), (v_in, v_out)):
        for k in range(source.shape[0]):
            copies.append(pltpu.make_async_copy(source.at[k], target.at[k], sems.at[len(copies)]))
    for copy in copies:
        copy.start()
    for copy in copies:
        copy.wait()


def solution(mesh):
    n_brow, n_bcol = mesh.shape["brow"], mesh.shape["bcol"]

    def local(uvel, vvel, wind_stress, ocean_mask, depth_level, baro_owner, eta_guess):
        level_count, rows, width = uvel.shape
        slots, block_x, block_y = eta_guess.shape
        tiles = width // LANES
        ext = tiles + 1
        span = rows + 2 * PAD
        sizes = (n_brow, n_bcol, level_count, rows, tiles, block_x, slots)
        f32 = jnp.float32
        vmem = pltpu.VMEM
        any_spec = pl.BlockSpec(memory_space=pltpu.HBM)
        vmem_spec = pl.BlockSpec(memory_space=vmem)

        def halo_buffers(count):
            return [
                vmem((LANES, rows), f32),
                vmem((LANES, rows), f32),
                vmem((4, count, CHUNK, LANES), f32),
            ]

        scratch = [
            vmem((level_count, 2, tiles, rows + 2 * CHUNK, LANES), f32),
            vmem((2, rows, width), f32),
            vmem((rows, width), jnp.int32),
            vmem((rows, width), jnp.int32),
            vmem((slots, block_x, LANES), f32),
            vmem((tiles, rows, LANES), jnp.int32),
            vmem((1, ext, span, LANES), f32),
            vmem((3, ext, span, LANES), f32),
            vmem((ext, span, LANES), f32),
            vmem((ext, span, LANES), f32),
            vmem((2, ext, span, LANES), f32),
            vmem((ext, span, LANES), f32),
            vmem((8, ext, span, LANES), f32),
            vmem((n_bcol, block_x, LANES), f32),
            vmem((n_bcol, block_x, LANES), f32),
            vmem((n_bcol, block_x, LANES), f32),
            vmem((n_bcol, block_x, LANES), f32),
            vmem((2, tiles, 2 * level_count, LANES), f32),
            vmem((2, tiles, 2 * level_count, LANES), f32),
            vmem((LANES, rows), f32),
            vmem((LANES, rows), f32),
            vmem((rows, LANES), f32),
            *halo_buffers(1),
            *halo_buffers(3),
            vmem(((rows // block_x) * tiles, block_x, LANES), f32),
            pltpu.SemaphoreType.DMA((4,)),
            pltpu.SemaphoreType.DMA((2, tiles, 2)),
            pltpu.SemaphoreType.DMA((2, 4)),
            pltpu.SemaphoreType.DMA((2, 8)),
            pltpu.SemaphoreType.DMA((2, 8)),
            pltpu.SemaphoreType.DMA((2, n_bcol)),
            pltpu.SemaphoreType.DMA((2, n_bcol)),
        ]
        fields = (uvel, vvel, wind_stress, ocean_mask, depth_level, eta_guess)
        results = pl.pallas_call(
            functools.partial(kernel, sizes),
            out_shape=(
                vmem(uvel.shape, f32),
                vmem(vvel.shape, f32),
                vmem(eta_guess.shape, f32),
            ),
            in_specs=[pl.BlockSpec(memory_space=pltpu.SMEM)] + [any_spec] * 6,
            out_specs=(vmem_spec,) * 3,
            scratch_shapes=scratch,
            compiler_params=pltpu.CompilerParams(
                collective_id=0, has_side_effects=True, vmem_limit_bytes=50 * 1024 * 1024
            ),
            cost_estimate=pl.CostEstimate(flops=60_000_000, bytes_accessed=20_000_000, transcendentals=0),
        )(baro_owner, *[pltpu.with_memory_space_constraint(x, pltpu.HBM) for x in fields])
        return pl.pallas_call(
            drain,
            out_shape=[jax.ShapeDtypeStruct(x.shape, f32) for x in results],
            in_specs=[vmem_spec] * 3,
            out_specs=[any_spec] * 3,
            scratch_shapes=[pltpu.SemaphoreType.DMA((2 * level_count + 1,))],
            compiler_params=pltpu.CompilerParams(vmem_limit_bytes=1024 * 1024),
            cost_estimate=pl.CostEstimate(flops=0, bytes_accessed=8_800_000, transcendentals=0),
        )(*[pltpu.with_memory_space_constraint(x, vmem) for x in results])

    in_specs = (
        P(None, "brow", "bcol"),
        P(None, "brow", "bcol"),
        P(None, "brow", "bcol"),
        P("brow", "bcol"),
        P("brow", "bcol"),
        P(),
        P(("brow", "bcol"), None, None),
    )
    out_specs = (P(None, "brow", "bcol"), P(None, "brow", "bcol"), P(("brow", "bcol"), None, None))
    return jax.shard_map(local, mesh=mesh, in_specs=in_specs, out_specs=out_specs, check_vma=False)
```

```python
import functools

import jax
import jax.numpy as jnp
from jax import lax
from jax.experimental import pallas as pl
from jax.experimental.pallas import tpu as pltpu
from jax.sharding import PartitionSpec as P

ITERS = 4
VISCOSITY = 0.2
CORIOLIS = 0.5
SURFACE_TERM = 0.25
LOWER_BOUND = 0.05
UPPER_BOUND = 2.0

LANES = 128
CHUNK = 8
PAD = 16
EAST_ROW = 64
MESH = pl.DeviceIdType.MESH
DIRECTIONS = ((-1, 0), (1, 0), (0, -1), (0, 1), (-1, -1), (-1, 1), (1, -1), (1, 1))


def chebyshev_factors():
    alpha = 2.0 / (UPPER_BOUND - LOWER_BOUND)
    gamma = (UPPER_BOUND + LOWER_BOUND) / 2.0
    omega = 2.0 / gamma
    factors = [(1.0 / gamma, 0.0)]
    for _ in range(ITERS - 1):
        omega = 1.0 / (gamma - omega / (4.0 * alpha * alpha))
        factors.append((omega, gamma * omega - 1.0))
    return factors


def lane_ids():
    return lax.broadcasted_iota(jnp.int32, (CHUNK, LANES), 1)


def from_west(tiles, lanes):
    rolled = [pltpu.roll(tile, 1, 1) for tile in tiles]
    return [jnp.where(lanes == 0, rolled[t - 1], rolled[t]) for t in range(len(tiles))]


def from_east(tiles, lanes):
    rolled = [pltpu.roll(tile, LANES - 1, 1) for tile in tiles]
    count = len(tiles)
    return [jnp.where(lanes == LANES - 1, rolled[(t + 1) % count], rolled[t]) for t in range(count)]


def grouped(first, count, group, body):
    def step(i, carry):
        for m in range(group):
            body(first + i * group + m)
        return carry

    lax.fori_loop(0, count // group, step, 0)


def rows_at(start):
    return pl.ds(pl.multiple_of(start, CHUNK), CHUNK)


def kernel(
    sizes,
    owner_ref, u_hbm, v_hbm, wind_hbm, mask_hbm, level_hbm, eta_hbm,
    u_out, v_out, height_out,
    vel, wind, mask_v, level_v, eta_v, wet_levels,
    depth_e, trans_e, xb, forcing_e, step_e, inv_c, weights,
    eta_send, eta_recv, height_send, height_recv,
    row_send, row_recv, col_send, col_recv, col_back,
    d_pack, d_halo, d_corner, t_pack, t_halo, t_corner,
    height_b,
    load_sem, vel_sem,
    r1_sem, d_sem, t_sem, eta_sem, height_sem,
):
    n_brow, n_bcol, level_count, rows, tiles, block_x, slots = sizes
    blocks_x = rows // block_x
    blocks = blocks_x * tiles
    chunks = rows // CHUNK
    ext = tiles + 1
    first, last = PAD, PAD + rows
    star = (u_out, v_out)
    xa = trans_e.at[2]
    r = lax.axis_index("brow")
    c = lax.axis_index("bcol")
    lanes = lane_ids()

    def device(dr, dc):
        return (lax.rem(r + dr + n_brow, n_brow), lax.rem(c + dc + n_bcol, n_bcol))

    barrier = pltpu.get_barrier_semaphore()
    partners = [(0, s) for s in range(1, n_bcol)]
    partners += [(dr, dc) for dr, dc in DIRECTIONS if dr != 0]
    for dr, dc in partners:
        pl.semaphore_signal(barrier, inc=1, device_id=device(dr, dc), device_id_type=MESH)

    loads = []

    def load(src, dst):
        copy = pltpu.make_async_copy(src, dst, load_sem.at[len(loads)])
        copy.start()
        loads.append(copy)
        return copy

    def columns(t):
        return slice(t * LANES, (t + 1) * LANES)

    load_eta = load(eta_hbm, eta_v)
    load_masks = [load(mask_hbm, mask_v), load(level_hbm, level_v)]
    groups = 2
    per_group = level_count // groups
    vel_loads = []
    for g in range(groups):
        these = []
        for t in range(tiles):
            for f, source in enumerate((u_hbm, v_hbm)):
                copy = pltpu.make_async_copy(
                    source.at[g * per_group : (g + 1) * per_group, :, columns(t)],
                    vel.at[g * per_group : (g + 1) * per_group, f, t, CHUNK : CHUNK + rows, :],
                    vel_sem.at[g, t, f],
                )
                copy.start()
                these.append(copy)
        vel_loads.append(these)
    load_wind = load(wind_hbm, wind)

    device_first = (r * n_bcol + c) * slots
    none = jnp.int32(-1)
    slot_of = []
    for s in range(n_bcol):
        q = lax.rem(c + s, n_bcol)
        found = none
        for b in range(blocks):
            local = owner_ref[r * blocks_x + b // tiles, q * tiles + b % tiles] - device_first
            found = jnp.where((local >= 0) & (local < slots), local, found)
        slot_of.append(found)
    def all_pairs(send, recv, sems):
        copies = []
        for s in range(1, n_bcol):
            copy = pltpu.make_async_remote_copy(
                src_ref=send.at[s], dst_ref=recv.at[s], send_sem=sems.at[0, s], recv_sem=sems.at[1, s],
                device_id=device(0, s), device_id_type=MESH,
            )
            copy.start()
            copies.append(copy)
        return copies

    load_eta.wait()
    for s in range(n_bcol):
        slot = jnp.maximum(slot_of[s], 0)
        into = eta_recv if s == 0 else eta_send
        into[s] = eta_v[slot]

    pl.semaphore_wait(barrier, len(partners))
    eta_copies = all_pairs(eta_send, eta_recv, eta_sem)

    zero = jnp.zeros((CHUNK, LANES), jnp.float32)
    for t in range(ext):
        for ref in (depth_e.at[0], trans_e.at[0], trans_e.at[1], xa, xb):
            ref[t, 0:CHUNK, :] = zero
            ref[t, last + CHUNK : last + 2 * CHUNK, :] = zero

    for t in range(tiles):
        for k in range(level_count):
            for f in range(2):
                vel[k, f, t, 0:CHUNK, :] = zero
                vel[k, f, t, CHUNK + rows : 2 * CHUNK + rows, :] = zero

    owners = [owner_ref[r * blocks_x + b // tiles, c * tiles + b % tiles] for b in range(blocks)]
    block_for, shift_of = [], [jnp.int32(0)] * blocks
    for s in range(n_bcol):
        holder_first = (r * n_bcol + lax.rem(c + s, n_bcol)) * slots
        found = jnp.int32(0)
        for b in range(blocks):
            here = (owners[b] >= holder_first) & (owners[b] < holder_first + slots)
            found = jnp.where(here, b, found)
            shift_of[b] = jnp.where(here, (n_bcol - s) % n_bcol, shift_of[b])
        block_for.append(found)
    source_of = []
    for slot in range(slots):
        found = none
        for s in range(n_bcol):
            found = jnp.where(slot_of[s] == slot, (n_bcol - s) % n_bcol, found)
        source_of.append(found)

    for copy in load_masks:
        copy.wait()

    def depth_body(i):
        at = rows_at(i * CHUNK)
        to = rows_at(i * CHUNK + PAD)
        for t in range(tiles):
            n = mask_v[at, columns(t)] * level_v[at, columns(t)]
            wet_levels[t, at, :] = n
            nf = n.astype(jnp.float32)
            depth_e[0, t, to, :] = nf * (nf + 1.0) * (1.0 / (2 * level_count))

    grouped(0, chunks, 4, depth_body)

    def pack(field_ref, count, packed_ref, back_ref):
        def pack_body(i):
            at = rows_at(i * CHUNK + PAD)
            value = jnp.zeros((CHUNK, LANES), jnp.float32)
            for f in range(count):
                low = EAST_ROW + CHUNK * f
                west = field_ref[f, 0, at, :]
                east = pltpu.roll(field_ref[f, tiles - 1, at, :], (low + CHUNK) % LANES, 1)
                if f > 0:
                    west = pltpu.roll(west, CHUNK * f, 1)
                value = jnp.where((lanes >= CHUNK * f) & (lanes < CHUNK * (f + 1)), west, value)
                value = jnp.where((lanes >= low) & (lanes < low + CHUNK), east, value)
            back_ref[rows_at(i * CHUNK), :] = value

        grouped(0, chunks, 16, pack_body)
        packed_ref[...] = jnp.transpose(back_ref[...])

    def exchange(field_ref, count, packed_ref, halo_ref, corner_ref, sems):
        height = CHUNK * count
        top, bottom = pl.ds(first, CHUNK), pl.ds(last - CHUNK, CHUNK)
        pairs = (
            (field_ref.at[:, 0:tiles, top, :], field_ref.at[:, 0:tiles, pl.ds(last, CHUNK), :]),
            (field_ref.at[:, 0:tiles, bottom, :], field_ref.at[:, 0:tiles, pl.ds(first - CHUNK, CHUNK), :]),
            (packed_ref.at[0:height, :], halo_ref.at[0:height, :]),
            (packed_ref.at[EAST_ROW : EAST_ROW + height, :], halo_ref.at[EAST_ROW : EAST_ROW + height, :]),
            (field_ref.at[:, 0, top, :], corner_ref.at[0]),
            (field_ref.at[:, tiles - 1, top, :], corner_ref.at[1]),
            (field_ref.at[:, 0, bottom, :], corner_ref.at[2]),
            (field_ref.at[:, tiles - 1, bottom, :], corner_ref.at[3]),
        )
        copies = []
        for d in (2, 3, 0, 1, 4, 5, 6, 7):
            src, dst = pairs[d]
            copy = pltpu.make_async_remote_copy(
                src_ref=src, dst_ref=dst, send_sem=sems.at[0, d], recv_sem=sems.at[1, d],
                device_id=device(*DIRECTIONS[d]), device_id_type=MESH,
            )
            copy.start()
            copies.append(copy)
        return copies

    def arrived(copies, field_ref, count, halo_ref, corner_ref, back_ref):
        for copy in copies:
            copy.wait_recv()
        has_n, has_s, has_w, has_e = r > 0, r < n_brow - 1, c > 0, c < n_bcol - 1
        height = CHUNK * count
        spare = jnp.zeros((EAST_ROW - height, rows), jnp.float32)
        halo = jnp.concatenate(
            [halo_ref[0:height, :], spare, halo_ref[EAST_ROW : EAST_ROW + height, :], spare], axis=0
        )
        back_ref[...] = jnp.transpose(halo)
        right = (lanes < CHUNK) & has_e
        left = (lanes >= LANES - CHUNK) & has_w

        def sides(east, west):
            return jnp.where(right, east, jnp.where(left, west, 0.0))

        def side_body(i):
            value = back_ref[rows_at(i * CHUNK), :]
            for f in range(count):
                east = value if f == 0 else pltpu.roll(value, LANES - CHUNK * f, 1)
                west = pltpu.roll(value, (2 * LANES - CHUNK - EAST_ROW - CHUNK * f) % LANES, 1)
                field_ref[f, tiles, rows_at(i * CHUNK + PAD), :] = sides(east, west)

        grouped(0, chunks, 16, side_body)
        north, south = pl.ds(first - CHUNK, CHUNK), pl.ds(last, CHUNK)
        for f in range(count):
            for t in range(tiles):
                field_ref[f, t, north, :] = jnp.where(has_n, field_ref[f, t, north, :], 0.0)
                field_ref[f, t, south, :] = jnp.where(has_s, field_ref[f, t, south, :], 0.0)
            field_ref[f, tiles, south, :] = jnp.where(has_s, sides(corner_ref[0, f], corner_ref[1, f]), 0.0)
            field_ref[f, tiles, north, :] = jnp.where(has_n, sides(corner_ref[2, f], corner_ref[3, f]), 0.0)

    pack(depth_e, 1, d_pack, col_back)
    d_copies = exchange(depth_e, 1, d_pack, d_halo, d_corner, d_sem)

    for g in range(groups):
        for copy in vel_loads[g]:
            copy.wait()

        def wet_body(i, g=g):
            at = rows_at(i * CHUNK + CHUNK)
            for t in range(tiles):
                n = wet_levels[t, rows_at(i * CHUNK), :]
                for k in range(g * per_group, (g + 1) * per_group):
                    wet = n > k
                    for f in range(2):
                        vel[k, f, t, at, :] = jnp.where(wet, VISCOSITY * vel[k, f, t, at, :], 0.0)

        grouped(0, chunks, 2, wet_body)

    def edge_body(i):
        at = rows_at(i * CHUNK + CHUNK)
        low = jnp.zeros((CHUNK, LANES), jnp.float32)
        high = low
        for k in range(level_count):
            for f in range(2):
                j = 2 * k + f
                west = vel[k, f, 0, at, :]
                if j > 0:
                    west = pltpu.roll(west, j, 1)
                east = pltpu.roll(vel[k, f, tiles - 1, at, :], EAST_ROW + j + 1, 1)
                low = jnp.where(lanes == j, west, low)
                high = jnp.where(lanes == EAST_ROW + j, east, high)
        col_back[rows_at(i * CHUNK), :] = jnp.where(lanes < EAST_ROW, low, high)

    grouped(0, chunks, 8, edge_body)
    col_send[...] = jnp.transpose(col_back[...])
    for k in range(level_count):
        for f in range(2):
            j = 2 * k + f
            for t in range(tiles):
                row_send[0, t, j : j + 1, :] = vel[k, f, t, CHUNK : CHUNK + 1, :]
                row_send[1, t, j : j + 1, :] = vel[k, f, t, CHUNK + rows - 1 : CHUNK + rows, :]
    count = 2 * level_count
    east_rows = slice(EAST_ROW, EAST_ROW + count)
    r1_pairs = (
        (row_send.at[0], row_recv.at[1]),
        (row_send.at[1], row_recv.at[0]),
        (col_send.at[0:count, :], col_recv.at[0:count, :]),
        (col_send.at[east_rows, :], col_recv.at[east_rows, :]),
    )
    r1_copies = []
    for d in (2, 3, 0, 1):
        src, dst = r1_pairs[d]
        copy = pltpu.make_async_remote_copy(
            src_ref=src, dst_ref=dst, send_sem=r1_sem.at[0, d], recv_sem=r1_sem.at[1, d],
            device_id=device(*DIRECTIONS[d]), device_id_type=MESH,
        )
        copy.start()
        r1_copies.append(copy)

    load_wind.wait()
    total_rows = rows * n_brow

    def momentum_body(i):
        here = rows_at(i * CHUNK)
        start = i * CHUNK + CHUNK
        at = rows_at(start)
        above, below = pl.ds(start - 1, CHUNK), pl.ds(start + 1, CHUNK)
        row_ids = (r * rows + i * CHUNK + lax.broadcasted_iota(jnp.int32, (CHUNK, LANES), 0)).astype(jnp.float32)
        coriolis = (CORIOLIS / VISCOSITY) * ((2.0 * row_ids + 1.0) * (1.0 / total_rows) - 1.0)
        n = [wet_levels[t, here, :] for t in range(tiles)]
        sums = [[None] * tiles, [None] * tiles]
        for k in range(level_count):
            centre = [[vel[k, f, t, at, :] for t in range(tiles)] for f in range(2)]
            for f in range(2):
                west_rolled = [pltpu.roll(tile, 1, 1) for tile in centre[f]]
                east_rolled = [pltpu.roll(tile, LANES - 1, 1) for tile in centre[f]]
                for t in range(tiles):
                    west = jnp.where(lanes == 0, west_rolled[t - 1] if t > 0 else 0.0, west_rolled[t])
                    east = jnp.where(
                        lanes == LANES - 1, east_rolled[t + 1] if t < tiles - 1 else 0.0, east_rolled[t]
                    )
                    spread = (west + east) + (vel[k, f, t, above, :] + vel[k, f, t, below, :]) + centre[f][t]
                    turn = coriolis * centre[1 - f][t]
                    value = spread + turn if f == 0 else spread - turn
                    if k == 0:
                        value = value + wind[f, here, columns(t)]
                    value = jnp.where(n[t] > k, value, 0.0)
                    star[f][k, here, columns(t)] = value
                    part = value * ((1.0 + k) / level_count)
                    sums[f][t] = part if k == 0 else sums[f][t] + part
        to = rows_at(i * CHUNK + PAD)
        for f in range(2):
            for t in range(tiles):
                trans_e[f, t, to, :] = sums[f][t]

    grouped(0, chunks, 4, momentum_body)

    for copy in r1_copies:
        copy.wait_recv()
    spare = jnp.zeros((EAST_ROW - count, rows), jnp.float32)
    col_back[...] = jnp.transpose(
        jnp.concatenate([col_recv[0:count, :], spare, col_recv[east_rows, :], spare], axis=0)
    )
    has_n, has_s, has_w, has_e = r > 0, r < n_brow - 1, c > 0, c < n_bcol - 1
    first_lane, last_lane = (lanes == 0) & has_w, (lanes == LANES - 1) & has_e

    def column_body(i):
        here = rows_at(i * CHUNK)
        to = rows_at(i * CHUNK + PAD)
        value = col_back[here, :]
        for t, edge in ((0, first_lane), (tiles - 1, last_lane)):
            n = jnp.where(edge, wet_levels[t, here, :], 0)
            sums = [trans_e[f, t, to, :] for f in range(2)]
            for k in range(level_count):
                for f in range(2):
                    j = 2 * k + f
                    turn = (EAST_ROW - j) % LANES if t == 0 else LANES - 1 - j
                    term = jnp.where(n > k, pltpu.roll(value, turn, 1), 0.0)
                    star[f][k, here, columns(t)] = star[f][k, here, columns(t)] + term
                    sums[f] = sums[f] + term * ((1.0 + k) / level_count)
            for f in range(2):
                trans_e[f, t, to, :] = sums[f]

    grouped(0, chunks, 4, column_body)
    sublanes = lax.broadcasted_iota(jnp.int32, (CHUNK, LANES), 0)
    for side, low, edge in ((0, 0, (sublanes == 0) & has_n), (1, rows - CHUNK, (sublanes == CHUNK - 1) & has_s)):
        here, to = slice(low, low + CHUNK), slice(low + PAD, low + PAD + CHUNK)
        for t in range(tiles):
            n = jnp.where(edge, wet_levels[t, here, :], 0)
            sums = [trans_e[f, t, to, :] for f in range(2)]
            for k in range(level_count):
                for f in range(2):
                    j = 2 * k + f
                    row = jnp.broadcast_to(row_recv[side, t, j : j + 1, :], (CHUNK, LANES))
                    term = jnp.where(n > k, row, 0.0)
                    star[f][k, here, columns(t)] = star[f][k, here, columns(t)] + term
                    sums[f] = sums[f] + term * ((1.0 + k) / level_count)
            for f in range(2):
                trans_e[f, t, to, :] = sums[f]

    for copy in eta_copies:
        copy.wait_recv()
    for b in range(blocks):
        a, t = b // tiles, b % tiles
        guess = eta_recv[shift_of[b]]
        at = pl.ds(first + a * block_x, block_x)
        xa[t, at, :] = jnp.where(depth_e[0, t, at, :] > 0.0, guess, 0.0)
    pack(trans_e, 3, t_pack, col_back)
    t_copies = exchange(trans_e, 3, t_pack, t_halo, t_corner, t_sem)

    arrived(d_copies, depth_e, 1, d_halo, d_corner, col_back)

    def weight_body(i):
        start = i * CHUNK + CHUNK
        at = rows_at(start)
        dc = [depth_e[0, t, at, :] for t in range(ext)]
        dn = [depth_e[0, t, pl.ds(start - 1, CHUNK), :] for t in range(ext)]
        ds = [depth_e[0, t, pl.ds(start + 1, CHUNK), :] for t in range(ext)]
        de, dw = from_east(dc, lanes), from_west(dc, lanes)
        span = range(ext)
        north = [jnp.minimum(dc[t], dn[t]) for t in span]
        south = [jnp.minimum(dc[t], ds[t]) for t in span]
        east = [
            [jnp.minimum(dc[t], de[t]) for t in span],
            [0.5 * jnp.minimum(dn[t], de[t]) for t in span],
            [0.5 * jnp.minimum(ds[t], de[t]) for t in span],
        ]
        west = [
            [jnp.minimum(dc[t], dw[t]) for t in span],
            [0.5 * jnp.minimum(dn[t], dw[t]) for t in span],
            [0.5 * jnp.minimum(ds[t], dw[t]) for t in span],
        ]
        sum_w = from_west([east[0][t] + east[1][t] + east[2][t] for t in span], lanes)
        sum_e = from_east([west[0][t] + west[1][t] + west[2][t] for t in span], lanes)
        inv = [1.0 / (SURFACE_TERM + north[t] + south[t] + sum_w[t] + sum_e[t]) for t in span]
        inv_e, inv_w = from_east(inv, lanes), from_west(inv, lanes)
        for t in span:
            inv_c[t, at, :] = inv[t]
            weights[0, t, at, :] = north[t] * inv[t]
            weights[1, t, at, :] = south[t] * inv[t]
            for m in range(3):
                weights[2 + m, t, at, :] = east[m][t] * inv_e[t]
                weights[5 + m, t, at, :] = west[m][t] * inv_w[t]

    grouped(0, chunks + 2, chunks // 2 + 1, weight_body)

    def stencil(old, start):
        at = rows_at(start)
        span = range(ext)
        xc = [old[t, at, :] for t in span]
        xn = [old[t, pl.ds(start - 1, CHUNK), :] for t in span]
        xs = [old[t, pl.ds(start + 1, CHUNK), :] for t in span]

        def side(base):
            return [
                weights[base, t, at, :] * xc[t]
                + weights[base + 1, t, at, :] * xn[t]
                + weights[base + 2, t, at, :] * xs[t]
                for t in span
            ]

        west, east = from_west(side(2), lanes), from_east(side(5), lanes)
        near = [weights[0, t, at, :] * xn[t] + weights[1, t, at, :] * xs[t] for t in span]
        return xc, [(near[t] - xc[t]) + (west[t] + east[t]) for t in span]

    fields = (xa, xb)
    factors = chebyshev_factors()
    arrived(t_copies, trans_e, 3, t_halo, t_corner, col_back)

    def forcing(start):
        at = rows_at(start)
        above, below = pl.ds(start - 1, CHUNK), pl.ds(start + 1, CHUNK)
        second = [trans_e[1, t, at, :] for t in range(ext)]
        east, west = from_east(second, lanes), from_west(second, lanes)
        values = []
        for t in range(ext):
            spread = trans_e[0, t, below, :] - trans_e[0, t, above, :] + east[t] - west[t]
            values.append(jnp.where(depth_e[0, t, at, :] > 0.0, -0.5 * spread, 0.0) * inv_c[t, at, :])
        return values

    for sweep in range(ITERS):
        omega, beta = factors[sweep]
        old, new = fields[sweep % 2], fields[(sweep + 1) % 2]
        if sweep == 1:
            for copy in t_copies:
                copy.wait_send()

        def sweep_body(i, old=old, new=new, sweep=sweep, omega=omega, beta=beta):
            start = i * CHUNK + CHUNK
            at = rows_at(start)
            xc, applied = stencil(old, start)
            force = forcing(start) if sweep == 0 else [forcing_e[t, at, :] for t in range(ext)]
            for t in range(ext):
                if sweep == 0:
                    forcing_e[t, at, :] = force[t]
                step = omega * (force[t] + applied[t])
                if sweep > 0:
                    step = step + beta * step_e[(sweep + 1) % 2, t, at, :]
                if sweep < ITERS - 1:
                    step_e[sweep % 2, t, at, :] = step
                new[t, at, :] = xc[t] + step

        grouped(0, chunks + 2, chunks // 2 + 1, sweep_body)
    result = fields[ITERS % 2]

    for b in range(blocks):
        height_b[b] = result[b % tiles, pl.ds(first + (b // tiles) * block_x, block_x), :]
    for s in range(n_bcol):
        into = height_recv if s == 0 else height_send
        into[s] = height_b[block_for[s]]
    height_copies = all_pairs(height_send, height_recv, height_sem)

    def final_body(i):
        here = rows_at(i * CHUNK)
        start = i * CHUNK + PAD
        at = rows_at(start)
        span = range(ext)
        xc = [result[t, at, :] for t in span]
        east, west = from_east(xc, lanes), from_west(xc, lanes)
        for t in range(tiles):
            n = wet_levels[t, here, :]
            north, south = result[t, pl.ds(start - 1, CHUNK), :], result[t, pl.ds(start + 1, CHUNK), :]
            slopes = (0.5 * (south - north), 0.5 * (east[t] - west[t]))
            for k in range(level_count):
                wet = n > k
                for f in range(2):
                    star[f][k, here, columns(t)] = star[f][k, here, columns(t)] - jnp.where(wet, slopes[f], 0.0)

    grouped(0, chunks, 4, final_body)
    for copy in height_copies:
        copy.wait_recv()
    for slot in range(slots):
        source = source_of[slot]
        held = jnp.broadcast_to(source, (block_x, LANES)) >= 0
        height_out[slot] = jnp.where(held, height_recv[jnp.maximum(source, 0)], 0.0)
    for copies in (d_copies, r1_copies, eta_copies, height_copies):
        for copy in copies:
            copy.wait_send()


def drain(u_in, v_in, height_in, u_out, v_out, height_out, sems):
    copies = [pltpu.make_async_copy(height_in, height_out, sems.at[0])]
    for source, target in ((u_in, u_out), (v_in, v_out)):
        for k in range(source.shape[0]):
            copies.append(pltpu.make_async_copy(source.at[k], target.at[k], sems.at[len(copies)]))
    for copy in copies:
        copy.start()
    for copy in copies:
        copy.wait()


def solution(mesh):
    n_brow, n_bcol = mesh.shape["brow"], mesh.shape["bcol"]

    def local(uvel, vvel, wind_stress, ocean_mask, depth_level, baro_owner, eta_guess):
        level_count, rows, width = uvel.shape
        slots, block_x, block_y = eta_guess.shape
        tiles = width // LANES
        ext = tiles + 1
        span = rows + 2 * PAD
        sizes = (n_brow, n_bcol, level_count, rows, tiles, block_x, slots)
        f32 = jnp.float32
        vmem = pltpu.VMEM
        any_spec = pl.BlockSpec(memory_space=pltpu.HBM)
        vmem_spec = pl.BlockSpec(memory_space=vmem)

        def halo_buffers(count):
            return [
                vmem((LANES, rows), f32),
                vmem((LANES, rows), f32),
                vmem((4, count, CHUNK, LANES), f32),
            ]

        scratch = [
            vmem((level_count, 2, tiles, rows + 2 * CHUNK, LANES), f32),
            vmem((2, rows, width), f32),
            vmem((rows, width), jnp.int32),
            vmem((rows, width), jnp.int32),
            vmem((slots, block_x, LANES), f32),
            vmem((tiles, rows, LANES), jnp.int32),
            vmem((1, ext, span, LANES), f32),
            vmem((3, ext, span, LANES), f32),
            vmem((ext, span, LANES), f32),
            vmem((ext, span, LANES), f32),
            vmem((2, ext, span, LANES), f32),
            vmem((ext, span, LANES), f32),
            vmem((8, ext, span, LANES), f32),
            vmem((n_bcol, block_x, LANES), f32),
            vmem((n_bcol, block_x, LANES), f32),
            vmem((n_bcol, block_x, LANES), f32),
            vmem((n_bcol, block_x, LANES), f32),
            vmem((2, tiles, 2 * level_count, LANES), f32),
            vmem((2, tiles, 2 * level_count, LANES), f32),
            vmem((LANES, rows), f32),
            vmem((LANES, rows), f32),
            vmem((rows, LANES), f32),
            *halo_buffers(1),
            *halo_buffers(3),
            vmem(((rows // block_x) * tiles, block_x, LANES), f32),
            pltpu.SemaphoreType.DMA((4,)),
            pltpu.SemaphoreType.DMA((2, tiles, 2)),
            pltpu.SemaphoreType.DMA((2, 4)),
            pltpu.SemaphoreType.DMA((2, 8)),
            pltpu.SemaphoreType.DMA((2, 8)),
            pltpu.SemaphoreType.DMA((2, n_bcol)),
            pltpu.SemaphoreType.DMA((2, n_bcol)),
        ]
        fields = (uvel, vvel, wind_stress, ocean_mask, depth_level, eta_guess)
        results = pl.pallas_call(
            functools.partial(kernel, sizes),
            out_shape=(
                vmem(uvel.shape, f32),
                vmem(vvel.shape, f32),
                vmem(eta_guess.shape, f32),
            ),
            in_specs=[pl.BlockSpec(memory_space=pltpu.SMEM)] + [any_spec] * 6,
            out_specs=(vmem_spec,) * 3,
            scratch_shapes=scratch,
            compiler_params=pltpu.CompilerParams(
                collective_id=0, has_side_effects=True, vmem_limit_bytes=50 * 1024 * 1024
            ),
            cost_estimate=pl.CostEstimate(flops=60_000_000, bytes_accessed=20_000_000, transcendentals=0),
        )(baro_owner, *[pltpu.with_memory_space_constraint(x, pltpu.HBM) for x in fields])
        return pl.pallas_call(
            drain,
            out_shape=[jax.ShapeDtypeStruct(x.shape, f32) for x in results],
            in_specs=[vmem_spec] * 3,
            out_specs=[any_spec] * 3,
            scratch_shapes=[pltpu.SemaphoreType.DMA((2 * level_count + 1,))],
            compiler_params=pltpu.CompilerParams(vmem_limit_bytes=1024 * 1024),
            cost_estimate=pl.CostEstimate(flops=0, bytes_accessed=8_800_000, transcendentals=0),
        )(*[pltpu.with_memory_space_constraint(x, vmem) for x in results])

    in_specs = (
        P(None, "brow", "bcol"),
        P(None, "brow", "bcol"),
        P(None, "brow", "bcol"),
        P("brow", "bcol"),
        P("brow", "bcol"),
        P(),
        P(("brow", "bcol"), None, None),
    )
    out_specs = (P(None, "brow", "bcol"), P(None, "brow", "bcol"), P(("brow", "bcol"), None, None))
    return jax.shard_map(local, mesh=mesh, in_specs=in_specs, out_specs=out_specs, check_vma=False)
```

```python
import functools

import jax
import jax.numpy as jnp
from jax import lax
from jax.experimental import pallas as pl
from jax.experimental.pallas import tpu as pltpu
from jax.sharding import PartitionSpec as P

ITERS = 4
VISCOSITY = 0.2
CORIOLIS = 0.5
SURFACE_TERM = 0.25
LOWER_BOUND = 0.05
UPPER_BOUND = 2.0

LANES = 128
CHUNK = 8
PAD = 16
EAST_ROW = 64
MESH = pl.DeviceIdType.MESH
DIRECTIONS = ((-1, 0), (1, 0), (0, -1), (0, 1), (-1, -1), (-1, 1), (1, -1), (1, 1))


def chebyshev_factors():
    alpha = 2.0 / (UPPER_BOUND - LOWER_BOUND)
    gamma = (UPPER_BOUND + LOWER_BOUND) / 2.0
    omega = 2.0 / gamma
    factors = [(1.0 / gamma, 0.0)]
    for _ in range(ITERS - 1):
        omega = 1.0 / (gamma - omega / (4.0 * alpha * alpha))
        factors.append((omega, gamma * omega - 1.0))
    return factors


def lane_ids():
    return lax.broadcasted_iota(jnp.int32, (CHUNK, LANES), 1)


def from_west(tiles, lanes):
    rolled = [pltpu.roll(tile, 1, 1) for tile in tiles]
    return [jnp.where(lanes == 0, rolled[t - 1], rolled[t]) for t in range(len(tiles))]


def from_east(tiles, lanes):
    rolled = [pltpu.roll(tile, LANES - 1, 1) for tile in tiles]
    count = len(tiles)
    return [jnp.where(lanes == LANES - 1, rolled[(t + 1) % count], rolled[t]) for t in range(count)]


def grouped(first, count, group, body):
    def step(i, carry):
        for m in range(group):
            body(first + i * group + m)
        return carry

    lax.fori_loop(0, count // group, step, 0)


def rows_at(start):
    return pl.ds(pl.multiple_of(start, CHUNK), CHUNK)


def kernel(
    sizes,
    owner_ref, u_hbm, v_hbm, wind_hbm, mask_hbm, level_hbm, eta_hbm,
    u_out, v_out, height_out,
    vel, wind, mask_v, level_v, eta_v, wet_levels,
    depth_e, trans_e, xb, forcing_e, step_e, inv_c, weights,
    eta_send, eta_recv, height_send, height_recv,
    row_send, row_recv, col_send, col_recv, col_back,
    d_pack, d_halo, d_corner, t_pack, t_halo, t_corner,
    height_b,
    load_sem, vel_sem,
    r1_sem, d_sem, t_sem, eta_sem, height_sem,
):
    n_brow, n_bcol, level_count, rows, tiles, block_x, slots = sizes
    blocks_x = rows // block_x
    blocks = blocks_x * tiles
    chunks = rows // CHUNK
    ext = tiles + 1
    first, last = PAD, PAD + rows
    star = (u_out, v_out)
    xa = trans_e.at[2]
    r = lax.axis_index("brow")
    c = lax.axis_index("bcol")
    lanes = lane_ids()

    def device(dr, dc):
        return (lax.rem(r + dr + n_brow, n_brow), lax.rem(c + dc + n_bcol, n_bcol))

    barrier = pltpu.get_barrier_semaphore()
    partners = [(0, s) for s in range(1, n_bcol)]
    partners += [(dr, dc) for dr, dc in DIRECTIONS if dr != 0]
    for dr, dc in partners:
        pl.semaphore_signal(barrier, inc=1, device_id=device(dr, dc), device_id_type=MESH)

    loads = []

    def load(src, dst):
        copy = pltpu.make_async_copy(src, dst, load_sem.at[len(loads)])
        copy.start()
        loads.append(copy)
        return copy

    def columns(t):
        return slice(t * LANES, (t + 1) * LANES)

    load_eta = load(eta_hbm, eta_v)
    load_masks = [load(mask_hbm, mask_v), load(level_hbm, level_v)]
    groups = 2
    per_group = level_count // groups
    vel_loads = []
    for g in range(groups):
        these = []
        for t in range(tiles):
            for f, source in enumerate((u_hbm, v_hbm)):
                copy = pltpu.make_async_copy(
                    source.at[g * per_group : (g + 1) * per_group, :, columns(t)],
                    vel.at[g * per_group : (g + 1) * per_group, f, t, CHUNK : CHUNK + rows, :],
                    vel_sem.at[g, t, f],
                )
                copy.start()
                these.append(copy)
        vel_loads.append(these)
    load_wind = load(wind_hbm, wind)

    device_first = (r * n_bcol + c) * slots
    none = jnp.int32(-1)
    slot_of = []
    for s in range(n_bcol):
        q = lax.rem(c + s, n_bcol)
        found = none
        for b in range(blocks):
            local = owner_ref[r * blocks_x + b // tiles, q * tiles + b % tiles] - device_first
            found = jnp.where((local >= 0) & (local < slots), local, found)
        slot_of.append(found)
    def copy_of(send, recv, sems, s):
        return pltpu.make_async_remote_copy(
            src_ref=send.at[s], dst_ref=recv.at[s], send_sem=sems.at[0, s], recv_sem=sems.at[1, s],
            device_id=device(0, s), device_id_type=MESH,
        )

    def all_pairs(send, recv, sems):
        core = lax.rem(c, 2)
        for i in range(1, n_bcol):
            copy_of(send, recv, sems, i + core * (n_bcol - 2 * i)).start()
        return [copy_of(send, recv, sems, s) for s in range(1, n_bcol)]

    load_eta.wait()
    for s in range(n_bcol):
        slot = jnp.maximum(slot_of[s], 0)
        into = eta_recv if s == 0 else eta_send
        into[s] = eta_v[slot]

    pl.semaphore_wait(barrier, len(partners))
    eta_copies = all_pairs(eta_send, eta_recv, eta_sem)

    zero = jnp.zeros((CHUNK, LANES), jnp.float32)
    for t in range(ext):
        for ref in (depth_e.at[0], trans_e.at[0], trans_e.at[1], xa, xb):
            ref[t, 0:CHUNK, :] = zero
            ref[t, last + CHUNK : last + 2 * CHUNK, :] = zero

    for t in range(tiles):
        for k in range(level_count):
            for f in range(2):
                vel[k, f, t, 0:CHUNK, :] = zero
                vel[k, f, t, CHUNK + rows : 2 * CHUNK + rows, :] = zero

    owners = [owner_ref[r * blocks_x + b // tiles, c * tiles + b % tiles] for b in range(blocks)]
    block_for, shift_of = [], [jnp.int32(0)] * blocks
    for s in range(n_bcol):
        holder_first = (r * n_bcol + lax.rem(c + s, n_bcol)) * slots
        found = jnp.int32(0)
        for b in range(blocks):
            here = (owners[b] >= holder_first) & (owners[b] < holder_first + slots)
            found = jnp.where(here, b, found)
            shift_of[b] = jnp.where(here, (n_bcol - s) % n_bcol, shift_of[b])
        block_for.append(found)
    source_of = []
    for slot in range(slots):
        found = none
        for s in range(n_bcol):
            found = jnp.where(slot_of[s] == slot, (n_bcol - s) % n_bcol, found)
        source_of.append(found)

    for copy in load_masks:
        copy.wait()

    def depth_body(i):
        at = rows_at(i * CHUNK)
        to = rows_at(i * CHUNK + PAD)
        for t in range(tiles):
            n = mask_v[at, columns(t)] * level_v[at, columns(t)]
            wet_levels[t, at, :] = n
            nf = n.astype(jnp.float32)
            depth_e[0, t, to, :] = nf * (nf + 1.0) * (1.0 / (2 * level_count))

    grouped(0, chunks, 4, depth_body)

    def pack(field_ref, count, packed_ref, back_ref):
        def pack_body(i):
            at = rows_at(i * CHUNK + PAD)
            value = jnp.zeros((CHUNK, LANES), jnp.float32)
            for f in range(count):
                low = EAST_ROW + CHUNK * f
                west = field_ref[f, 0, at, :]
                east = pltpu.roll(field_ref[f, tiles - 1, at, :], (low + CHUNK) % LANES, 1)
                if f > 0:
                    west = pltpu.roll(west, CHUNK * f, 1)
                value = jnp.where((lanes >= CHUNK * f) & (lanes < CHUNK * (f + 1)), west, value)
                value = jnp.where((lanes >= low) & (lanes < low + CHUNK), east, value)
            back_ref[rows_at(i * CHUNK), :] = value

        grouped(0, chunks, 16, pack_body)
        packed_ref[...] = jnp.transpose(back_ref[...])

    def exchange(field_ref, count, packed_ref, halo_ref, corner_ref, sems):
        height = CHUNK * count
        top, bottom = pl.ds(first, CHUNK), pl.ds(last - CHUNK, CHUNK)
        pairs = (
            (field_ref.at[:, 0:tiles, top, :], field_ref.at[:, 0:tiles, pl.ds(last, CHUNK), :]),
            (field_ref.at[:, 0:tiles, bottom, :], field_ref.at[:, 0:tiles, pl.ds(first - CHUNK, CHUNK), :]),
            (packed_ref.at[0:height, :], halo_ref.at[0:height, :]),
            (packed_ref.at[EAST_ROW : EAST_ROW + height, :], halo_ref.at[EAST_ROW : EAST_ROW + height, :]),
            (field_ref.at[:, 0, top, :], corner_ref.at[0]),
            (field_ref.at[:, tiles - 1, top, :], corner_ref.at[1]),
            (field_ref.at[:, 0, bottom, :], corner_ref.at[2]),
            (field_ref.at[:, tiles - 1, bottom, :], corner_ref.at[3]),
        )
        copies = []
        for d in (2, 3, 0, 1, 4, 5, 6, 7):
            src, dst = pairs[d]
            copy = pltpu.make_async_remote_copy(
                src_ref=src, dst_ref=dst, send_sem=sems.at[0, d], recv_sem=sems.at[1, d],
                device_id=device(*DIRECTIONS[d]), device_id_type=MESH,
            )
            copy.start()
            copies.append(copy)
        return copies

    def arrived(copies, field_ref, count, halo_ref, corner_ref, back_ref):
        for copy in copies:
            copy.wait_recv()
        has_n, has_s, has_w, has_e = r > 0, r < n_brow - 1, c > 0, c < n_bcol - 1
        height = CHUNK * count
        spare = jnp.zeros((EAST_ROW - height, rows), jnp.float32)
        halo = jnp.concatenate(
            [halo_ref[0:height, :], spare, halo_ref[EAST_ROW : EAST_ROW + height, :], spare], axis=0
        )
        back_ref[...] = jnp.transpose(halo)
        right = (lanes < CHUNK) & has_e
        left = (lanes >= LANES - CHUNK) & has_w

        def sides(east, west):
            return jnp.where(right, east, jnp.where(left, west, 0.0))

        def side_body(i):
            value = back_ref[rows_at(i * CHUNK), :]
            for f in range(count):
                east = value if f == 0 else pltpu.roll(value, LANES - CHUNK * f, 1)
                west = pltpu.roll(value, (2 * LANES - CHUNK - EAST_ROW - CHUNK * f) % LANES, 1)
                field_ref[f, tiles, rows_at(i * CHUNK + PAD), :] = sides(east, west)

        grouped(0, chunks, 16, side_body)
        north, south = pl.ds(first - CHUNK, CHUNK), pl.ds(last, CHUNK)
        for f in range(count):
            for t in range(tiles):
                field_ref[f, t, north, :] = jnp.where(has_n, field_ref[f, t, north, :], 0.0)
                field_ref[f, t, south, :] = jnp.where(has_s, field_ref[f, t, south, :], 0.0)
            field_ref[f, tiles, south, :] = jnp.where(has_s, sides(corner_ref[0, f], corner_ref[1, f]), 0.0)
            field_ref[f, tiles, north, :] = jnp.where(has_n, sides(corner_ref[2, f], corner_ref[3, f]), 0.0)

    pack(depth_e, 1, d_pack, col_back)
    d_copies = exchange(depth_e, 1, d_pack, d_halo, d_corner, d_sem)

    for g in range(groups):
        for copy in vel_loads[g]:
            copy.wait()

        def wet_body(i, g=g):
            at = rows_at(i * CHUNK + CHUNK)
            for t in range(tiles):
                n = wet_levels[t, rows_at(i * CHUNK), :]
                for k in range(g * per_group, (g + 1) * per_group):
                    wet = n > k
                    for f in range(2):
                        vel[k, f, t, at, :] = jnp.where(wet, VISCOSITY * vel[k, f, t, at, :], 0.0)

        grouped(0, chunks, 2, wet_body)

    def edge_body(i):
        at = rows_at(i * CHUNK + CHUNK)
        low = jnp.zeros((CHUNK, LANES), jnp.float32)
        high = low
        for k in range(level_count):
            for f in range(2):
                j = 2 * k + f
                west = vel[k, f, 0, at, :]
                if j > 0:
                    west = pltpu.roll(west, j, 1)
                east = pltpu.roll(vel[k, f, tiles - 1, at, :], EAST_ROW + j + 1, 1)
                low = jnp.where(lanes == j, west, low)
                high = jnp.where(lanes == EAST_ROW + j, east, high)
        col_back[rows_at(i * CHUNK), :] = jnp.where(lanes < EAST_ROW, low, high)

    grouped(0, chunks, 8, edge_body)
    col_send[...] = jnp.transpose(col_back[...])
    for k in range(level_count):
        for f in range(2):
            j = 2 * k + f
            for t in range(tiles):
                row_send[0, t, j : j + 1, :] = vel[k, f, t, CHUNK : CHUNK + 1, :]
                row_send[1, t, j : j + 1, :] = vel[k, f, t, CHUNK + rows - 1 : CHUNK + rows, :]
    count = 2 * level_count
    east_rows = slice(EAST_ROW, EAST_ROW + count)
    r1_pairs = (
        (row_send.at[0], row_recv.at[1]),
        (row_send.at[1], row_recv.at[0]),
        (col_send.at[0:count, :], col_recv.at[0:count, :]),
        (col_send.at[east_rows, :], col_recv.at[east_rows, :]),
    )
    r1_copies = []
    for d in (2, 3, 0, 1):
        src, dst = r1_pairs[d]
        copy = pltpu.make_async_remote_copy(
            src_ref=src, dst_ref=dst, send_sem=r1_sem.at[0, d], recv_sem=r1_sem.at[1, d],
            device_id=device(*DIRECTIONS[d]), device_id_type=MESH,
        )
        copy.start()
        r1_copies.append(copy)

    load_wind.wait()
    total_rows = rows * n_brow

    def momentum_body(i):
        here = rows_at(i * CHUNK)
        start = i * CHUNK + CHUNK
        at = rows_at(start)
        above, below = pl.ds(start - 1, CHUNK), pl.ds(start + 1, CHUNK)
        row_ids = (r * rows + i * CHUNK + lax.broadcasted_iota(jnp.int32, (CHUNK, LANES), 0)).astype(jnp.float32)
        coriolis = (CORIOLIS / VISCOSITY) * ((2.0 * row_ids + 1.0) * (1.0 / total_rows) - 1.0)
        n = [wet_levels[t, here, :] for t in range(tiles)]
        sums = [[None] * tiles, [None] * tiles]
        for k in range(level_count):
            centre = [[vel[k, f, t, at, :] for t in range(tiles)] for f in range(2)]
            for f in range(2):
                west_rolled = [pltpu.roll(tile, 1, 1) for tile in centre[f]]
                east_rolled = [pltpu.roll(tile, LANES - 1, 1) for tile in centre[f]]
                for t in range(tiles):
                    west = jnp.where(lanes == 0, west_rolled[t - 1] if t > 0 else 0.0, west_rolled[t])
                    east = jnp.where(
                        lanes == LANES - 1, east_rolled[t + 1] if t < tiles - 1 else 0.0, east_rolled[t]
                    )
                    spread = (west + east) + (vel[k, f, t, above, :] + vel[k, f, t, below, :]) + centre[f][t]
                    turn = coriolis * centre[1 - f][t]
                    value = spread + turn if f == 0 else spread - turn
                    if k == 0:
                        value = value + wind[f, here, columns(t)]
                    value = jnp.where(n[t] > k, value, 0.0)
                    star[f][k, here, columns(t)] = value
                    part = value * ((1.0 + k) / level_count)
                    sums[f][t] = part if k == 0 else sums[f][t] + part
        to = rows_at(i * CHUNK + PAD)
        for f in range(2):
            for t in range(tiles):
                trans_e[f, t, to, :] = sums[f][t]

    grouped(0, chunks, 4, momentum_body)

    for copy in r1_copies:
        copy.wait_recv()
    spare = jnp.zeros((EAST_ROW - count, rows), jnp.float32)
    col_back[...] = jnp.transpose(
        jnp.concatenate([col_recv[0:count, :], spare, col_recv[east_rows, :], spare], axis=0)
    )
    has_n, has_s, has_w, has_e = r > 0, r < n_brow - 1, c > 0, c < n_bcol - 1
    first_lane, last_lane = (lanes == 0) & has_w, (lanes == LANES - 1) & has_e

    def column_body(i):
        here = rows_at(i * CHUNK)
        to = rows_at(i * CHUNK + PAD)
        value = col_back[here, :]
        for t, edge in ((0, first_lane), (tiles - 1, last_lane)):
            n = jnp.where(edge, wet_levels[t, here, :], 0)
            sums = [trans_e[f, t, to, :] for f in range(2)]
            for k in range(level_count):
                for f in range(2):
                    j = 2 * k + f
                    turn = (EAST_ROW - j) % LANES if t == 0 else LANES - 1 - j
                    term = jnp.where(n > k, pltpu.roll(value, turn, 1), 0.0)
                    star[f][k, here, columns(t)] = star[f][k, here, columns(t)] + term
                    sums[f] = sums[f] + term * ((1.0 + k) / level_count)
            for f in range(2):
                trans_e[f, t, to, :] = sums[f]

    grouped(0, chunks, 4, column_body)
    sublanes = lax.broadcasted_iota(jnp.int32, (CHUNK, LANES), 0)
    for side, low, edge in ((0, 0, (sublanes == 0) & has_n), (1, rows - CHUNK, (sublanes == CHUNK - 1) & has_s)):
        here, to = slice(low, low + CHUNK), slice(low + PAD, low + PAD + CHUNK)
        for t in range(tiles):
            n = jnp.where(edge, wet_levels[t, here, :], 0)
            sums = [trans_e[f, t, to, :] for f in range(2)]
            for k in range(level_count):
                for f in range(2):
                    j = 2 * k + f
                    row = jnp.broadcast_to(row_recv[side, t, j : j + 1, :], (CHUNK, LANES))
                    term = jnp.where(n > k, row, 0.0)
                    star[f][k, here, columns(t)] = star[f][k, here, columns(t)] + term
                    sums[f] = sums[f] + term * ((1.0 + k) / level_count)
            for f in range(2):
                trans_e[f, t, to, :] = sums[f]

    for copy in eta_copies:
        copy.wait_recv()
    for b in range(blocks):
        a, t = b // tiles, b % tiles
        guess = eta_recv[shift_of[b]]
        at = pl.ds(first + a * block_x, block_x)
        xa[t, at, :] = jnp.where(depth_e[0, t, at, :] > 0.0, guess, 0.0)
    pack(trans_e, 3, t_pack, col_back)
    t_copies = exchange(trans_e, 3, t_pack, t_halo, t_corner, t_sem)

    arrived(d_copies, depth_e, 1, d_halo, d_corner, col_back)

    def weight_body(i):
        start = i * CHUNK + CHUNK
        at = rows_at(start)
        dc = [depth_e[0, t, at, :] for t in range(ext)]
        dn = [depth_e[0, t, pl.ds(start - 1, CHUNK), :] for t in range(ext)]
        ds = [depth_e[0, t, pl.ds(start + 1, CHUNK), :] for t in range(ext)]
        de, dw = from_east(dc, lanes), from_west(dc, lanes)
        span = range(ext)
        north = [jnp.minimum(dc[t], dn[t]) for t in span]
        south = [jnp.minimum(dc[t], ds[t]) for t in span]
        east = [
            [jnp.minimum(dc[t], de[t]) for t in span],
            [0.5 * jnp.minimum(dn[t], de[t]) for t in span],
            [0.5 * jnp.minimum(ds[t], de[t]) for t in span],
        ]
        west = [
            [jnp.minimum(dc[t], dw[t]) for t in span],
            [0.5 * jnp.minimum(dn[t], dw[t]) for t in span],
            [0.5 * jnp.minimum(ds[t], dw[t]) for t in span],
        ]
        sum_w = from_west([east[0][t] + east[1][t] + east[2][t] for t in span], lanes)
        sum_e = from_east([west[0][t] + west[1][t] + west[2][t] for t in span], lanes)
        inv = [1.0 / (SURFACE_TERM + north[t] + south[t] + sum_w[t] + sum_e[t]) for t in span]
        inv_e, inv_w = from_east(inv, lanes), from_west(inv, lanes)
        for t in span:
            inv_c[t, at, :] = inv[t]
            weights[0, t, at, :] = north[t] * inv[t]
            weights[1, t, at, :] = south[t] * inv[t]
            for m in range(3):
                weights[2 + m, t, at, :] = east[m][t] * inv_e[t]
                weights[5 + m, t, at, :] = west[m][t] * inv_w[t]

    grouped(0, chunks + 2, chunks // 2 + 1, weight_body)

    def stencil(old, start):
        at = rows_at(start)
        span = range(ext)
        xc = [old[t, at, :] for t in span]
        xn = [old[t, pl.ds(start - 1, CHUNK), :] for t in span]
        xs = [old[t, pl.ds(start + 1, CHUNK), :] for t in span]

        def side(base):
            return [
                weights[base, t, at, :] * xc[t]
                + weights[base + 1, t, at, :] * xn[t]
                + weights[base + 2, t, at, :] * xs[t]
                for t in span
            ]

        west, east = from_west(side(2), lanes), from_east(side(5), lanes)
        near = [weights[0, t, at, :] * xn[t] + weights[1, t, at, :] * xs[t] for t in span]
        return xc, [(near[t] - xc[t]) + (west[t] + east[t]) for t in span]

    fields = (xa, xb)
    factors = chebyshev_factors()
    arrived(t_copies, trans_e, 3, t_halo, t_corner, col_back)

    def forcing(start):
        at = rows_at(start)
        above, below = pl.ds(start - 1, CHUNK), pl.ds(start + 1, CHUNK)
        second = [trans_e[1, t, at, :] for t in range(ext)]
        east, west = from_east(second, lanes), from_west(second, lanes)
        values = []
        for t in range(ext):
            spread = trans_e[0, t, below, :] - trans_e[0, t, above, :] + east[t] - west[t]
            values.append(jnp.where(depth_e[0, t, at, :] > 0.0, -0.5 * spread, 0.0) * inv_c[t, at, :])
        return values

    for sweep in range(ITERS):
        omega, beta = factors[sweep]
        old, new = fields[sweep % 2], fields[(sweep + 1) % 2]
        if sweep == 1:
            for copy in t_copies:
                copy.wait_send()

        def sweep_body(i, old=old, new=new, sweep=sweep, omega=omega, beta=beta):
            start = i * CHUNK + CHUNK
            at = rows_at(start)
            xc, applied = stencil(old, start)
            force = forcing(start) if sweep == 0 else [forcing_e[t, at, :] for t in range(ext)]
            for t in range(ext):
                if sweep == 0:
                    forcing_e[t, at, :] = force[t]
                step = omega * (force[t] + applied[t])
                if sweep > 0:
                    step = step + beta * step_e[(sweep + 1) % 2, t, at, :]
                if sweep < ITERS - 1:
                    step_e[sweep % 2, t, at, :] = step
                new[t, at, :] = xc[t] + step
                if sweep == ITERS - 1 and t < tiles:
                    place = i + block_x // CHUNK - 1
                    block = lax.div(place, block_x // CHUNK) * tiles + t
                    row = lax.rem(place, block_x // CHUNK) * CHUNK
                    height_b[block, rows_at(row), :] = xc[t] + step

        grouped(0, chunks + 2, chunks // 2 + 1, sweep_body)
    result = fields[ITERS % 2]

    for s in range(n_bcol):
        into = height_recv if s == 0 else height_send
        into[s] = height_b[block_for[s] + tiles]
    height_copies = all_pairs(height_send, height_recv, height_sem)

    def final_body(i):
        here = rows_at(i * CHUNK)
        start = i * CHUNK + PAD
        at = rows_at(start)
        span = range(ext)
        xc = [result[t, at, :] for t in span]
        east, west = from_east(xc, lanes), from_west(xc, lanes)
        for t in range(tiles):
            n = wet_levels[t, here, :]
            north, south = result[t, pl.ds(start - 1, CHUNK), :], result[t, pl.ds(start + 1, CHUNK), :]
            slopes = (0.5 * (south - north), 0.5 * (east[t] - west[t]))
            for k in range(level_count):
                wet = n > k
                for f in range(2):
                    star[f][k, here, columns(t)] = star[f][k, here, columns(t)] - jnp.where(wet, slopes[f], 0.0)

    grouped(0, chunks, 4, final_body)
    for copy in height_copies:
        copy.wait_recv()
    for slot in range(slots):
        source = source_of[slot]
        held = jnp.broadcast_to(source, (block_x, LANES)) >= 0
        height_out[slot] = jnp.where(held, height_recv[jnp.maximum(source, 0)], 0.0)
    for copies in (d_copies, r1_copies, eta_copies, height_copies):
        for copy in copies:
            copy.wait_send()


def drain(u_in, v_in, height_in, u_out, v_out, height_out, sems):
    copies = [pltpu.make_async_copy(height_in, height_out, sems.at[0])]
    for source, target in ((u_in, u_out), (v_in, v_out)):
        for k in range(source.shape[0]):
            copies.append(pltpu.make_async_copy(source.at[k], target.at[k], sems.at[len(copies)]))
    for copy in copies:
        copy.start()
    for copy in copies:
        copy.wait()


def solution(mesh):
    n_brow, n_bcol = mesh.shape["brow"], mesh.shape["bcol"]

    def local(uvel, vvel, wind_stress, ocean_mask, depth_level, baro_owner, eta_guess):
        level_count, rows, width = uvel.shape
        slots, block_x, block_y = eta_guess.shape
        tiles = width // LANES
        ext = tiles + 1
        span = rows + 2 * PAD
        sizes = (n_brow, n_bcol, level_count, rows, tiles, block_x, slots)
        f32 = jnp.float32
        vmem = pltpu.VMEM
        any_spec = pl.BlockSpec(memory_space=pltpu.HBM)
        vmem_spec = pl.BlockSpec(memory_space=vmem)

        def halo_buffers(count):
            return [
                vmem((LANES, rows), f32),
                vmem((LANES, rows), f32),
                vmem((4, count, CHUNK, LANES), f32),
            ]

        scratch = [
            vmem((level_count, 2, tiles, rows + 2 * CHUNK, LANES), f32),
            vmem((2, rows, width), f32),
            vmem((rows, width), jnp.int32),
            vmem((rows, width), jnp.int32),
            vmem((slots, block_x, LANES), f32),
            vmem((tiles, rows, LANES), jnp.int32),
            vmem((1, ext, span, LANES), f32),
            vmem((3, ext, span, LANES), f32),
            vmem((ext, span, LANES), f32),
            vmem((ext, span, LANES), f32),
            vmem((2, ext, span, LANES), f32),
            vmem((ext, span, LANES), f32),
            vmem((8, ext, span, LANES), f32),
            vmem((n_bcol, block_x, LANES), f32),
            vmem((n_bcol, block_x, LANES), f32),
            vmem((n_bcol, block_x, LANES), f32),
            vmem((n_bcol, block_x, LANES), f32),
            vmem((2, tiles, 2 * level_count, LANES), f32),
            vmem((2, tiles, 2 * level_count, LANES), f32),
            vmem((LANES, rows), f32),
            vmem((LANES, rows), f32),
            vmem((rows, LANES), f32),
            *halo_buffers(1),
            *halo_buffers(3),
            vmem(((rows // block_x + 2) * tiles, block_x, LANES), f32),
            pltpu.SemaphoreType.DMA((4,)),
            pltpu.SemaphoreType.DMA((2, tiles, 2)),
            pltpu.SemaphoreType.DMA((2, 4)),
            pltpu.SemaphoreType.DMA((2, 8)),
            pltpu.SemaphoreType.DMA((2, 8)),
            pltpu.SemaphoreType.DMA((2, n_bcol)),
            pltpu.SemaphoreType.DMA((2, n_bcol)),
        ]
        fields = (uvel, vvel, wind_stress, ocean_mask, depth_level, eta_guess)
        results = pl.pallas_call(
            functools.partial(kernel, sizes),
            out_shape=(
                vmem(uvel.shape, f32),
                vmem(vvel.shape, f32),
                vmem(eta_guess.shape, f32),
            ),
            in_specs=[pl.BlockSpec(memory_space=pltpu.SMEM)] + [any_spec] * 6,
            out_specs=(vmem_spec,) * 3,
            scratch_shapes=scratch,
            compiler_params=pltpu.CompilerParams(
                collective_id=0, has_side_effects=True, vmem_limit_bytes=50 * 1024 * 1024
            ),
            cost_estimate=pl.CostEstimate(flops=60_000_000, bytes_accessed=20_000_000, transcendentals=0),
        )(baro_owner, *[pltpu.with_memory_space_constraint(x, pltpu.HBM) for x in fields])
        return pl.pallas_call(
            drain,
            out_shape=[jax.ShapeDtypeStruct(x.shape, f32) for x in results],
            in_specs=[vmem_spec] * 3,
            out_specs=[any_spec] * 3,
            scratch_shapes=[pltpu.SemaphoreType.DMA((2 * level_count + 1,))],
            compiler_params=pltpu.CompilerParams(vmem_limit_bytes=1024 * 1024),
            cost_estimate=pl.CostEstimate(flops=0, bytes_accessed=8_800_000, transcendentals=0),
        )(*[pltpu.with_memory_space_constraint(x, vmem) for x in results])

    in_specs = (
        P(None, "brow", "bcol"),
        P(None, "brow", "bcol"),
        P(None, "brow", "bcol"),
        P("brow", "bcol"),
        P("brow", "bcol"),
        P(),
        P(("brow", "bcol"), None, None),
    )
    out_specs = (P(None, "brow", "bcol"), P(None, "brow", "bcol"), P(("brow", "bcol"), None, None))
    return jax.shard_map(local, mesh=mesh, in_specs=in_specs, out_specs=out_specs, check_vma=False)
```

```python
import functools

import jax
import jax.numpy as jnp
from jax import lax
from jax.experimental import pallas as pl
from jax.experimental.pallas import tpu as pltpu
from jax.sharding import PartitionSpec as P

ITERS = 4
VISCOSITY = 0.2
CORIOLIS = 0.5
SURFACE_TERM = 0.25
LOWER_BOUND = 0.05
UPPER_BOUND = 2.0

LANES = 128
CHUNK = 8
PAD = 16
EAST_ROW = 64
MESH = pl.DeviceIdType.MESH
DIRECTIONS = ((-1, 0), (1, 0), (0, -1), (0, 1), (-1, -1), (-1, 1), (1, -1), (1, 1))


def chebyshev_factors():
    alpha = 2.0 / (UPPER_BOUND - LOWER_BOUND)
    gamma = (UPPER_BOUND + LOWER_BOUND) / 2.0
    omega = 2.0 / gamma
    factors = [(1.0 / gamma, 0.0)]
    for _ in range(ITERS - 1):
        omega = 1.0 / (gamma - omega / (4.0 * alpha * alpha))
        factors.append((omega, gamma * omega - 1.0))
    return factors


def lane_ids():
    return lax.broadcasted_iota(jnp.int32, (CHUNK, LANES), 1)


def from_west(tiles, lanes):
    rolled = [pltpu.roll(tile, 1, 1) for tile in tiles]
    return [jnp.where(lanes == 0, rolled[t - 1], rolled[t]) for t in range(len(tiles))]


def from_east(tiles, lanes):
    rolled = [pltpu.roll(tile, LANES - 1, 1) for tile in tiles]
    count = len(tiles)
    return [jnp.where(lanes == LANES - 1, rolled[(t + 1) % count], rolled[t]) for t in range(count)]


def grouped(first, count, group, body):
    def step(i, carry):
        for m in range(group):
            body(first + i * group + m)
        return carry

    lax.fori_loop(0, count // group, step, 0)


def rows_at(start):
    return pl.ds(pl.multiple_of(start, CHUNK), CHUNK)


def kernel(
    sizes,
    owner_ref, u_hbm, v_hbm, wind_hbm, mask_hbm, level_hbm, eta_hbm,
    u_out, v_out, height_out,
    vel, wind, mask_v, level_v, eta_v, wet_levels,
    depth_e, trans_e, xb, forcing_e, step_e, inv_c, weights,
    eta_send, eta_recv, height_send, height_recv,
    row_send, row_recv, col_send, col_recv, col_back,
    d_pack, d_halo, d_corner, t_pack, t_halo, t_corner,
    height_b,
    load_sem, vel_sem,
    r1_sem, d_sem, t_sem, eta_sem, height_sem,
):
    n_brow, n_bcol, level_count, rows, tiles, block_x, slots = sizes
    blocks_x = rows // block_x
    blocks = blocks_x * tiles
    chunks = rows // CHUNK
    ext = tiles + 1
    first, last = PAD, PAD + rows
    star = (u_out, v_out)
    xa = trans_e.at[2]
    r = lax.axis_index("brow")
    c = lax.axis_index("bcol")
    lanes = lane_ids()

    def device(dr, dc):
        return (lax.rem(r + dr + n_brow, n_brow), lax.rem(c + dc + n_bcol, n_bcol))

    barrier = pltpu.get_barrier_semaphore()
    partners = [(0, s) for s in range(1, n_bcol)]
    partners += [(dr, dc) for dr, dc in DIRECTIONS if dr != 0]
    for dr, dc in partners:
        pl.semaphore_signal(barrier, inc=1, device_id=device(dr, dc), device_id_type=MESH)

    loads = []

    def load(src, dst):
        copy = pltpu.make_async_copy(src, dst, load_sem.at[len(loads)])
        copy.start()
        loads.append(copy)
        return copy

    def columns(t):
        return slice(t * LANES, (t + 1) * LANES)

    load_eta = load(eta_hbm, eta_v)
    load_masks = [load(mask_hbm, mask_v), load(level_hbm, level_v)]
    groups = 2
    per_group = level_count // groups
    vel_loads = []
    for g in range(groups):
        these = []
        for t in range(tiles):
            for f, source in enumerate((u_hbm, v_hbm)):
                copy = pltpu.make_async_copy(
                    source.at[g * per_group : (g + 1) * per_group, :, columns(t)],
                    vel.at[g * per_group : (g + 1) * per_group, f, t, CHUNK : CHUNK + rows, :],
                    vel_sem.at[g, t, f],
                )
                copy.start()
                these.append(copy)
        vel_loads.append(these)
    load_wind = load(wind_hbm, wind)

    device_first = (r * n_bcol + c) * slots
    none = jnp.int32(-1)
    slot_of = []
    for s in range(n_bcol):
        q = lax.rem(c + s, n_bcol)
        found = none
        for b in range(blocks):
            local = owner_ref[r * blocks_x + b // tiles, q * tiles + b % tiles] - device_first
            found = jnp.where((local >= 0) & (local < slots), local, found)
        slot_of.append(found)
    def all_pairs(send, recv, sems):
        copies = []
        for s in range(1, n_bcol):
            copy = pltpu.make_async_remote_copy(
                src_ref=send.at[s], dst_ref=recv.at[s], send_sem=sems.at[0, s], recv_sem=sems.at[1, s],
                device_id=device(0, s), device_id_type=MESH,
            )
            copy.start()
            copies.append(copy)
        return copies

    load_eta.wait()
    for s in range(n_bcol):
        slot = jnp.maximum(slot_of[s], 0)
        into = eta_recv if s == 0 else eta_send
        into[s] = eta_v[slot]

    pl.semaphore_wait(barrier, len(partners))
    eta_copies = all_pairs(eta_send, eta_recv, eta_sem)

    zero = jnp.zeros((CHUNK, LANES), jnp.float32)
    for t in range(ext):
        for ref in (depth_e.at[0], trans_e.at[0], trans_e.at[1], xa, xb):
            ref[t, 0:CHUNK, :] = zero
            ref[t, last + CHUNK : last + 2 * CHUNK, :] = zero

    for t in range(tiles):
        for k in range(level_count):
            for f in range(2):
                vel[k, f, t, 0:CHUNK, :] = zero
                vel[k, f, t, CHUNK + rows : 2 * CHUNK + rows, :] = zero

    owners = [owner_ref[r * blocks_x + b // tiles, c * tiles + b % tiles] for b in range(blocks)]
    block_for, shift_of = [], [jnp.int32(0)] * blocks
    for s in range(n_bcol):
        holder_first = (r * n_bcol + lax.rem(c + s, n_bcol)) * slots
        found = jnp.int32(0)
        for b in range(blocks):
            here = (owners[b] >= holder_first) & (owners[b] < holder_first + slots)
            found = jnp.where(here, b, found)
            shift_of[b] = jnp.where(here, (n_bcol - s) % n_bcol, shift_of[b])
        block_for.append(found)
    source_of = []
    for slot in range(slots):
        found = none
        for s in range(n_bcol):
            found = jnp.where(slot_of[s] == slot, (n_bcol - s) % n_bcol, found)
        source_of.append(found)

    for copy in load_masks:
        copy.wait()

    def depth_body(i):
        at = rows_at(i * CHUNK)
        to = rows_at(i * CHUNK + PAD)
        for t in range(tiles):
            n = mask_v[at, columns(t)] * level_v[at, columns(t)]
            wet_levels[t, at, :] = n
            nf = n.astype(jnp.float32)
            depth_e[0, t, to, :] = nf * (nf + 1.0) * (1.0 / (2 * level_count))

    grouped(0, chunks, 4, depth_body)

    def pack(field_ref, count, packed_ref, back_ref):
        def pack_body(i):
            at = rows_at(i * CHUNK + PAD)
            value = jnp.zeros((CHUNK, LANES), jnp.float32)
            for f in range(count):
                low = EAST_ROW + CHUNK * f
                west = field_ref[f, 0, at, :]
                east = pltpu.roll(field_ref[f, tiles - 1, at, :], (low + CHUNK) % LANES, 1)
                if f > 0:
                    west = pltpu.roll(west, CHUNK * f, 1)
                value = jnp.where((lanes >= CHUNK * f) & (lanes < CHUNK * (f + 1)), west, value)
                value = jnp.where((lanes >= low) & (lanes < low + CHUNK), east, value)
            back_ref[rows_at(i * CHUNK), :] = value

        grouped(0, chunks, 16, pack_body)
        packed_ref[...] = jnp.transpose(back_ref[...])

    def exchange(field_ref, count, packed_ref, halo_ref, corner_ref, sems):
        height = CHUNK * count
        top, bottom = pl.ds(first, CHUNK), pl.ds(last - CHUNK, CHUNK)
        pairs = (
            (field_ref.at[:, 0:tiles, top, :], field_ref.at[:, 0:tiles, pl.ds(last, CHUNK), :]),
            (field_ref.at[:, 0:tiles, bottom, :], field_ref.at[:, 0:tiles, pl.ds(first - CHUNK, CHUNK), :]),
            (packed_ref.at[0:height, :], halo_ref.at[0:height, :]),
            (packed_ref.at[EAST_ROW : EAST_ROW + height, :], halo_ref.at[EAST_ROW : EAST_ROW + height, :]),
            (field_ref.at[:, 0, top, :], corner_ref.at[0]),
            (field_ref.at[:, tiles - 1, top, :], corner_ref.at[1]),
            (field_ref.at[:, 0, bottom, :], corner_ref.at[2]),
            (field_ref.at[:, tiles - 1, bottom, :], corner_ref.at[3]),
        )
        copies = []
        for d in (2, 3, 0, 1, 4, 5, 6, 7):
            src, dst = pairs[d]
            copy = pltpu.make_async_remote_copy(
                src_ref=src, dst_ref=dst, send_sem=sems.at[0, d], recv_sem=sems.at[1, d],
                device_id=device(*DIRECTIONS[d]), device_id_type=MESH,
            )
            copy.start()
            copies.append(copy)
        return copies

    def arrived(copies, field_ref, count, halo_ref, corner_ref, back_ref):
        for copy in copies:
            copy.wait_recv()
        has_n, has_s, has_w, has_e = r > 0, r < n_brow - 1, c > 0, c < n_bcol - 1
        height = CHUNK * count
        spare = jnp.zeros((EAST_ROW - height, rows), jnp.float32)
        halo = jnp.concatenate(
            [halo_ref[0:height, :], spare, halo_ref[EAST_ROW : EAST_ROW + height, :], spare], axis=0
        )
        back_ref[...] = jnp.transpose(halo)
        right = (lanes < CHUNK) & has_e
        left = (lanes >= LANES - CHUNK) & has_w

        def sides(east, west):
            return jnp.where(right, east, jnp.where(left, west, 0.0))

        def side_body(i):
            value = back_ref[rows_at(i * CHUNK), :]
            for f in range(count):
                east = value if f == 0 else pltpu.roll(value, LANES - CHUNK * f, 1)
                west = pltpu.roll(value, (2 * LANES - CHUNK - EAST_ROW - CHUNK * f) % LANES, 1)
                field_ref[f, tiles, rows_at(i * CHUNK + PAD), :] = sides(east, west)

        grouped(0, chunks, 16, side_body)
        north, south = pl.ds(first - CHUNK, CHUNK), pl.ds(last, CHUNK)
        for f in range(count):
            for t in range(tiles):
                field_ref[f, t, north, :] = jnp.where(has_n, field_ref[f, t, north, :], 0.0)
                field_ref[f, t, south, :] = jnp.where(has_s, field_ref[f, t, south, :], 0.0)
            field_ref[f, tiles, south, :] = jnp.where(has_s, sides(corner_ref[0, f], corner_ref[1, f]), 0.0)
            field_ref[f, tiles, north, :] = jnp.where(has_n, sides(corner_ref[2, f], corner_ref[3, f]), 0.0)

    pack(depth_e, 1, d_pack, col_back)
    d_copies = exchange(depth_e, 1, d_pack, d_halo, d_corner, d_sem)

    for g in range(groups):
        for copy in vel_loads[g]:
            copy.wait()

        def wet_body(i, g=g):
            at = rows_at(i * CHUNK + CHUNK)
            for t in range(tiles):
                n = wet_levels[t, rows_at(i * CHUNK), :]
                for k in range(g * per_group, (g + 1) * per_group):
                    wet = n > k
                    for f in range(2):
                        vel[k, f, t, at, :] = jnp.where(wet, VISCOSITY * vel[k, f, t, at, :], 0.0)

        grouped(0, chunks, 2, wet_body)

    def edge_body(i):
        at = rows_at(i * CHUNK + CHUNK)
        low = jnp.zeros((CHUNK, LANES), jnp.float32)
        high = low
        for k in range(level_count):
            for f in range(2):
                j = 2 * k + f
                west = vel[k, f, 0, at, :]
                if j > 0:
                    west = pltpu.roll(west, j, 1)
                east = pltpu.roll(vel[k, f, tiles - 1, at, :], EAST_ROW + j + 1, 1)
                low = jnp.where(lanes == j, west, low)
                high = jnp.where(lanes == EAST_ROW + j, east, high)
        col_back[rows_at(i * CHUNK), :] = jnp.where(lanes < EAST_ROW, low, high)

    grouped(0, chunks, 8, edge_body)
    col_send[...] = jnp.transpose(col_back[...])
    for k in range(level_count):
        for f in range(2):
            j = 2 * k + f
            for t in range(tiles):
                row_send[0, t, j : j + 1, :] = vel[k, f, t, CHUNK : CHUNK + 1, :]
                row_send[1, t, j : j + 1, :] = vel[k, f, t, CHUNK + rows - 1 : CHUNK + rows, :]
    count = 2 * level_count
    east_rows = slice(EAST_ROW, EAST_ROW + count)
    r1_pairs = (
        (row_send.at[0], row_recv.at[1]),
        (row_send.at[1], row_recv.at[0]),
        (col_send.at[0:count, :], col_recv.at[0:count, :]),
        (col_send.at[east_rows, :], col_recv.at[east_rows, :]),
    )
    r1_copies = []
    for d in (2, 3, 0, 1):
        src, dst = r1_pairs[d]
        copy = pltpu.make_async_remote_copy(
            src_ref=src, dst_ref=dst, send_sem=r1_sem.at[0, d], recv_sem=r1_sem.at[1, d],
            device_id=device(*DIRECTIONS[d]), device_id_type=MESH,
        )
        copy.start()
        r1_copies.append(copy)

    load_wind.wait()
    total_rows = rows * n_brow

    def momentum_body(i):
        here = rows_at(i * CHUNK)
        start = i * CHUNK + CHUNK
        at = rows_at(start)
        above, below = pl.ds(start - 1, CHUNK), pl.ds(start + 1, CHUNK)
        row_ids = (r * rows + i * CHUNK + lax.broadcasted_iota(jnp.int32, (CHUNK, LANES), 0)).astype(jnp.float32)
        coriolis = (CORIOLIS / VISCOSITY) * ((2.0 * row_ids + 1.0) * (1.0 / total_rows) - 1.0)
        n = [wet_levels[t, here, :] for t in range(tiles)]
        sums = [[None] * tiles, [None] * tiles]
        for k in range(level_count):
            centre = [[vel[k, f, t, at, :] for t in range(tiles)] for f in range(2)]
            for f in range(2):
                west_rolled = [pltpu.roll(tile, 1, 1) for tile in centre[f]]
                east_rolled = [pltpu.roll(tile, LANES - 1, 1) for tile in centre[f]]
                for t in range(tiles):
                    west = jnp.where(lanes == 0, west_rolled[t - 1] if t > 0 else 0.0, west_rolled[t])
                    east = jnp.where(
                        lanes == LANES - 1, east_rolled[t + 1] if t < tiles - 1 else 0.0, east_rolled[t]
                    )
                    spread = (west + east) + (vel[k, f, t, above, :] + vel[k, f, t, below, :]) + centre[f][t]
                    turn = coriolis * centre[1 - f][t]
                    value = spread + turn if f == 0 else spread - turn
                    if k == 0:
                        value = value + wind[f, here, columns(t)]
                    value = jnp.where(n[t] > k, value, 0.0)
                    star[f][k, here, columns(t)] = value
                    part = value * ((1.0 + k) / level_count)
                    sums[f][t] = part if k == 0 else sums[f][t] + part
        to = rows_at(i * CHUNK + PAD)
        for f in range(2):
            for t in range(tiles):
                trans_e[f, t, to, :] = sums[f][t]

    grouped(0, chunks, 2, momentum_body)

    for copy in r1_copies:
        copy.wait_recv()
    spare = jnp.zeros((EAST_ROW - count, rows), jnp.float32)
    col_back[...] = jnp.transpose(
        jnp.concatenate([col_recv[0:count, :], spare, col_recv[east_rows, :], spare], axis=0)
    )
    has_n, has_s, has_w, has_e = r > 0, r < n_brow - 1, c > 0, c < n_bcol - 1
    first_lane, last_lane = (lanes == 0) & has_w, (lanes == LANES - 1) & has_e

    def column_body(i):
        here = rows_at(i * CHUNK)
        to = rows_at(i * CHUNK + PAD)
        value = col_back[here, :]
        for t, edge in ((0, first_lane), (tiles - 1, last_lane)):
            n = jnp.where(edge, wet_levels[t, here, :], 0)
            sums = [trans_e[f, t, to, :] for f in range(2)]
            for k in range(level_count):
                for f in range(2):
                    j = 2 * k + f
                    turn = (EAST_ROW - j) % LANES if t == 0 else LANES - 1 - j
                    term = jnp.where(n > k, pltpu.roll(value, turn, 1), 0.0)
                    star[f][k, here, columns(t)] = star[f][k, here, columns(t)] + term
                    sums[f] = sums[f] + term * ((1.0 + k) / level_count)
            for f in range(2):
                trans_e[f, t, to, :] = sums[f]

    grouped(0, chunks, 4, column_body)
    sublanes = lax.broadcasted_iota(jnp.int32, (CHUNK, LANES), 0)
    for side, low, edge in ((0, 0, (sublanes == 0) & has_n), (1, rows - CHUNK, (sublanes == CHUNK - 1) & has_s)):
        here, to = slice(low, low + CHUNK), slice(low + PAD, low + PAD + CHUNK)
        for t in range(tiles):
            n = jnp.where(edge, wet_levels[t, here, :], 0)
            sums = [trans_e[f, t, to, :] for f in range(2)]
            for k in range(level_count):
                for f in range(2):
                    j = 2 * k + f
                    row = jnp.broadcast_to(row_recv[side, t, j : j + 1, :], (CHUNK, LANES))
                    term = jnp.where(n > k, row, 0.0)
                    star[f][k, here, columns(t)] = star[f][k, here, columns(t)] + term
                    sums[f] = sums[f] + term * ((1.0 + k) / level_count)
            for f in range(2):
                trans_e[f, t, to, :] = sums[f]

    for copy in eta_copies:
        copy.wait_recv()
    for b in range(blocks):
        a, t = b // tiles, b % tiles
        guess = eta_recv[shift_of[b]]
        at = pl.ds(first + a * block_x, block_x)
        xa[t, at, :] = jnp.where(depth_e[0, t, at, :] > 0.0, guess, 0.0)
    pack(trans_e, 3, t_pack, col_back)
    t_copies = exchange(trans_e, 3, t_pack, t_halo, t_corner, t_sem)

    arrived(d_copies, depth_e, 1, d_halo, d_corner, col_back)

    def weight_body(i):
        start = i * CHUNK + CHUNK
        at = rows_at(start)
        dc = [depth_e[0, t, at, :] for t in range(ext)]
        dn = [depth_e[0, t, pl.ds(start - 1, CHUNK), :] for t in range(ext)]
        ds = [depth_e[0, t, pl.ds(start + 1, CHUNK), :] for t in range(ext)]
        de, dw = from_east(dc, lanes), from_west(dc, lanes)
        span = range(ext)
        north = [jnp.minimum(dc[t], dn[t]) for t in span]
        south = [jnp.minimum(dc[t], ds[t]) for t in span]
        east = [
            [jnp.minimum(dc[t], de[t]) for t in span],
            [0.5 * jnp.minimum(dn[t], de[t]) for t in span],
            [0.5 * jnp.minimum(ds[t], de[t]) for t in span],
        ]
        west = [
            [jnp.minimum(dc[t], dw[t]) for t in span],
            [0.5 * jnp.minimum(dn[t], dw[t]) for t in span],
            [0.5 * jnp.minimum(ds[t], dw[t]) for t in span],
        ]
        sum_w = from_west([east[0][t] + east[1][t] + east[2][t] for t in span], lanes)
        sum_e = from_east([west[0][t] + west[1][t] + west[2][t] for t in span], lanes)
        inv = [1.0 / (SURFACE_TERM + north[t] + south[t] + sum_w[t] + sum_e[t]) for t in span]
        inv_e, inv_w = from_east(inv, lanes), from_west(inv, lanes)
        for t in span:
            inv_c[t, at, :] = inv[t]
            weights[0, t, at, :] = north[t] * inv[t]
            weights[1, t, at, :] = south[t] * inv[t]
            for m in range(3):
                weights[2 + m, t, at, :] = east[m][t] * inv_e[t]
                weights[5 + m, t, at, :] = west[m][t] * inv_w[t]

    grouped(0, chunks + 2, chunks // 2 + 1, weight_body)

    def stencil(old, start):
        at = rows_at(start)
        span = range(ext)
        xc = [old[t, at, :] for t in span]
        xn = [old[t, pl.ds(start - 1, CHUNK), :] for t in span]
        xs = [old[t, pl.ds(start + 1, CHUNK), :] for t in span]

        def side(base):
            return [
                weights[base, t, at, :] * xc[t]
                + weights[base + 1, t, at, :] * xn[t]
                + weights[base + 2, t, at, :] * xs[t]
                for t in span
            ]

        west, east = from_west(side(2), lanes), from_east(side(5), lanes)
        near = [weights[0, t, at, :] * xn[t] + weights[1, t, at, :] * xs[t] for t in span]
        return xc, [(near[t] - xc[t]) + (west[t] + east[t]) for t in span]

    fields = (xa, xb)
    factors = chebyshev_factors()
    arrived(t_copies, trans_e, 3, t_halo, t_corner, col_back)

    def forcing(start):
        at = rows_at(start)
        above, below = pl.ds(start - 1, CHUNK), pl.ds(start + 1, CHUNK)
        second = [trans_e[1, t, at, :] for t in range(ext)]
        east, west = from_east(second, lanes), from_west(second, lanes)
        values = []
        for t in range(ext):
            spread = trans_e[0, t, below, :] - trans_e[0, t, above, :] + east[t] - west[t]
            values.append(jnp.where(depth_e[0, t, at, :] > 0.0, -0.5 * spread, 0.0) * inv_c[t, at, :])
        return values

    for sweep in range(ITERS):
        omega, beta = factors[sweep]
        old, new = fields[sweep % 2], fields[(sweep + 1) % 2]
        if sweep == 1:
            for copy in t_copies:
                copy.wait_send()

        def sweep_body(i, old=old, new=new, sweep=sweep, omega=omega, beta=beta):
            start = i * CHUNK + CHUNK
            at = rows_at(start)
            xc, applied = stencil(old, start)
            force = forcing(start) if sweep == 0 else [forcing_e[t, at, :] for t in range(ext)]
            for t in range(ext):
                if sweep == 0:
                    forcing_e[t, at, :] = force[t]
                step = omega * (force[t] + applied[t])
                if sweep > 0:
                    step = step + beta * step_e[(sweep + 1) % 2, t, at, :]
                if sweep < ITERS - 1:
                    step_e[sweep % 2, t, at, :] = step
                new[t, at, :] = xc[t] + step

        grouped(0, chunks + 2, chunks // 2 + 1, sweep_body)
    result = fields[ITERS % 2]

    for b in range(blocks):
        height_b[b] = result[b % tiles, pl.ds(first + (b // tiles) * block_x, block_x), :]
    for s in range(n_bcol):
        into = height_recv if s == 0 else height_send
        into[s] = height_b[block_for[s]]
    height_copies = all_pairs(height_send, height_recv, height_sem)

    def final_body(i):
        here = rows_at(i * CHUNK)
        start = i * CHUNK + PAD
        at = rows_at(start)
        span = range(ext)
        xc = [result[t, at, :] for t in span]
        east, west = from_east(xc, lanes), from_west(xc, lanes)
        for t in range(tiles):
            n = wet_levels[t, here, :]
            north, south = result[t, pl.ds(start - 1, CHUNK), :], result[t, pl.ds(start + 1, CHUNK), :]
            slopes = (0.5 * (south - north), 0.5 * (east[t] - west[t]))
            for k in range(level_count):
                wet = n > k
                for f in range(2):
                    star[f][k, here, columns(t)] = star[f][k, here, columns(t)] - jnp.where(wet, slopes[f], 0.0)

    grouped(0, chunks, 4, final_body)
    for copy in height_copies:
        copy.wait_recv()
    for slot in range(slots):
        source = source_of[slot]
        held = jnp.broadcast_to(source, (block_x, LANES)) >= 0
        height_out[slot] = jnp.where(held, height_recv[jnp.maximum(source, 0)], 0.0)
    for copies in (d_copies, r1_copies, eta_copies, height_copies):
        for copy in copies:
            copy.wait_send()


def drain(u_in, v_in, height_in, u_out, v_out, height_out, sems):
    copies = [pltpu.make_async_copy(height_in, height_out, sems.at[0])]
    for source, target in ((u_in, u_out), (v_in, v_out)):
        copies.append(pltpu.make_async_copy(source, target, sems.at[len(copies)]))
    for copy in copies:
        copy.start()
    for copy in copies:
        copy.wait()


def solution(mesh):
    n_brow, n_bcol = mesh.shape["brow"], mesh.shape["bcol"]

    def local(uvel, vvel, wind_stress, ocean_mask, depth_level, baro_owner, eta_guess):
        level_count, rows, width = uvel.shape
        slots, block_x, block_y = eta_guess.shape
        tiles = width // LANES
        ext = tiles + 1
        span = rows + 2 * PAD
        sizes = (n_brow, n_bcol, level_count, rows, tiles, block_x, slots)
        f32 = jnp.float32
        vmem = pltpu.VMEM
        any_spec = pl.BlockSpec(memory_space=pltpu.HBM)
        vmem_spec = pl.BlockSpec(memory_space=vmem)

        def halo_buffers(count):
            return [
                vmem((LANES, rows), f32),
                vmem((LANES, rows), f32),
                vmem((4, count, CHUNK, LANES), f32),
            ]

        scratch = [
            vmem((level_count, 2, tiles, rows + 2 * CHUNK, LANES), f32),
            vmem((2, rows, width), f32),
            vmem((rows, width), jnp.int32),
            vmem((rows, width), jnp.int32),
            vmem((slots, block_x, LANES), f32),
            vmem((tiles, rows, LANES), jnp.int32),
            vmem((1, ext, span, LANES), f32),
            vmem((3, ext, span, LANES), f32),
            vmem((ext, span, LANES), f32),
            vmem((ext, span, LANES), f32),
            vmem((2, ext, span, LANES), f32),
            vmem((ext, span, LANES), f32),
            vmem((8, ext, span, LANES), f32),
            vmem((n_bcol, block_x, LANES), f32),
            vmem((n_bcol, block_x, LANES), f32),
            vmem((n_bcol, block_x, LANES), f32),
            vmem((n_bcol, block_x, LANES), f32),
            vmem((2, tiles, 2 * level_count, LANES), f32),
            vmem((2, tiles, 2 * level_count, LANES), f32),
            vmem((LANES, rows), f32),
            vmem((LANES, rows), f32),
            vmem((rows, LANES), f32),
            *halo_buffers(1),
            *halo_buffers(3),
            vmem(((rows // block_x) * tiles, block_x, LANES), f32),
            pltpu.SemaphoreType.DMA((4,)),
            pltpu.SemaphoreType.DMA((2, tiles, 2)),
            pltpu.SemaphoreType.DMA((2, 4)),
            pltpu.SemaphoreType.DMA((2, 8)),
            pltpu.SemaphoreType.DMA((2, 8)),
            pltpu.SemaphoreType.DMA((2, n_bcol)),
            pltpu.SemaphoreType.DMA((2, n_bcol)),
        ]
        fields = (uvel, vvel, wind_stress, ocean_mask, depth_level, eta_guess)
        results = pl.pallas_call(
            functools.partial(kernel, sizes),
            out_shape=(
                vmem(uvel.shape, f32),
                vmem(vvel.shape, f32),
                vmem(eta_guess.shape, f32),
            ),
            in_specs=[pl.BlockSpec(memory_space=pltpu.SMEM)] + [any_spec] * 6,
            out_specs=(vmem_spec,) * 3,
            scratch_shapes=scratch,
            compiler_params=pltpu.CompilerParams(
                collective_id=0, has_side_effects=True, vmem_limit_bytes=50 * 1024 * 1024
            ),
            cost_estimate=pl.CostEstimate(flops=60_000_000, bytes_accessed=20_000_000, transcendentals=0),
        )(baro_owner, *[pltpu.with_memory_space_constraint(x, pltpu.HBM) for x in fields])
        return pl.pallas_call(
            drain,
            out_shape=[jax.ShapeDtypeStruct(x.shape, f32) for x in results],
            in_specs=[vmem_spec] * 3,
            out_specs=[any_spec] * 3,
            scratch_shapes=[pltpu.SemaphoreType.DMA((3,))],
            compiler_params=pltpu.CompilerParams(vmem_limit_bytes=1024 * 1024),
            cost_estimate=pl.CostEstimate(flops=0, bytes_accessed=8_800_000, transcendentals=0),
        )(*[pltpu.with_memory_space_constraint(x, vmem) for x in results])

    in_specs = (
        P(None, "brow", "bcol"),
        P(None, "brow", "bcol"),
        P(None, "brow", "bcol"),
        P("brow", "bcol"),
        P("brow", "bcol"),
        P(),
        P(("brow", "bcol"), None, None),
    )
    out_specs = (P(None, "brow", "bcol"), P(None, "brow", "bcol"), P(("brow", "bcol"), None, None))
    return jax.shard_map(local, mesh=mesh, in_specs=in_specs, out_specs=out_specs, check_vma=False)
```
